32 devices in a mesh: mod: 2 (over core), seq: 4 (over z), mp: 4 (over y, x).
Axes of the slice: x: 2, y: 2, z: 4, core: 2. Of those that a mesh axis runs over, the one named last changes fastest.
Arguments:
- inputs: bfloat16 [2, 1024, 1024], P('mod', 'seq'), may hold values from -6 to 6
- text_patches: int32 [1024, 4], P('seq'), may hold values from 0 to 255, as said below
- patch_valid: int32 [1024, 4], P('seq'), may hold values 0 or 1
- text_lengths: int32 [4, 2], P('seq'), may hold values from 64 to 192, as said below
- bucket_table: int32 [639], replicated, may hold values from 0 to 31
- attn_gain: bfloat16 [1024], replicated, may hold values from 0.099609375 to 1.8984375
- query_weight: bfloat16 [1024, 1024], P(None, 'mp'), may hold values from -0.1875 to 0.1875
- key_weight: bfloat16 [1024, 1024], P(None, 'mp'), may hold values from -0.1875 to 0.1875
- value_weight: bfloat16 [1024, 1024], P(None, 'mp'), may hold values from -0.1875 to 0.1875
- output_weight: bfloat16 [1024, 1024], P('mp'), may hold values from -1.5 to 1.5
- position_bias: float32 [32, 16], P(None, 'mp'), may hold values from -4 to 4
- ffn_gain: bfloat16 [1024], replicated, may hold values from 0.099609375 to 1.8984375
- gate_weight: bfloat16 [1024, 2816], P(None, 'mp'), may hold values from -0.1875 to 0.1875
- up_weight: bfloat16 [1024, 2816], P(None, 'mp'), may hold values from -0.1875 to 0.1875
- down_weight: bfloat16 [2816, 1024], P('mp'), may hold values from -0.109375 to 0.109375
- cotangent: bfloat16 [2, 1024, 1024], P('mod', 'seq'), may hold values from -6 to 6
Outputs:
- outputs: bfloat16 [2, 1024, 1024], P('mod', 'seq')
- input_grad: float32 [2, 1024, 1024], P('mod', 'seq')
- attn_gain_grad: float32 [1024], P(('mod', 'seq'))
- query_weight_grad: float32 [1024, 1024], P(('mod', 'seq'), 'mp')
- key_weight_grad: float32 [1024, 1024], P(('mod', 'seq'), 'mp')
- value_weight_grad: float32 [1024, 1024], P(('mod', 'seq'), 'mp')
- output_weight_grad: float32 [1024, 1024], P('mp', ('mod', 'seq'))
- position_bias_grad: float32 [32, 16], P(('mod', 'seq'), 'mp')
- ffn_gain_grad: float32 [1024], P(('mod', 'seq'))
- gate_weight_grad: float32 [1024, 2816], P(('mod', 'seq'), 'mp')
- up_weight_grad: float32 [1024, 2816], P(('mod', 'seq'), 'mp')
- down_weight_grad: float32 [2816, 1024], P('mp', ('mod', 'seq'))
The draws below stay inside these ranges and needn't reach their ends.
Inputs may be any that keep to these rules, and one draw needn't show every extreme that they name: text_patches[t, j] names a patch row of the same seq index inside the text row's own document: from 128 * d to 128 * d + 127 for document d. `text_lengths`: each row holds two lengths, 192 and 64, in either order.
All inputs are finite; a program needn't handle non-finite values. No bound on the sum of `patch_valid` on one device may be relied on, other than what follows from the above.
Results may differ from the reference program's by a relative error of at most 0.015.
Values may be sent and summed in bfloat16 or wider, within the bound.
A program may use at most 128 MiB of HBM per device.

```python
import jax
import jax.numpy as jnp
from jax import lax

D = 1024
H = 16
HD = 64
FF = 2816
NB = 32
ROWS = 256
PDOC = 128
MOST_TEXT = 192
MAXPOS = 320
SPAN = 639
TOKENS = 1024


def shared_order(key):
    groups = TOKENS // ROWS
    order_bits = jax.random.randint(jax.random.fold_in(key, 7), (groups,), 0, 2)
    return jnp.where(order_bits == 1, MOST_TEXT, ROWS - MOST_TEXT).astype(jnp.int32)


def draw_text_lengths(key, part):
    first_len = shared_order(key)
    return jnp.stack([first_len, ROWS - first_len], axis=1).astype(jnp.int32)


def draw_text_patches(key, part):
    groups = TOKENS // ROWS
    first_len = shared_order(key)
    local_rows = jnp.arange(ROWS, dtype=jnp.int32)
    doc_ids = (local_rows[None, :] >= first_len[:, None]).astype(jnp.int32)
    offsets = jax.random.randint(jax.random.fold_in(key, 11), (groups, ROWS, 4), 0, PDOC)
    return (doc_ids[:, :, None] * PDOC + offsets).reshape(TOKENS, 4).astype(jnp.int32)


def with_ends(entries, own_key, smallest, top_value):
    longest = entries.shape.index(max(entries.shape))
    spots = []
    for shift in (0, 1):
        where = [jax.random.randint(jax.random.fold_in(own_key, axis), (), 0, length) for axis, length in enumerate(entries.shape)]
        where[longest] = (where[longest] + shift) % entries.shape[longest]
        spots.append(tuple(where))
    return entries.at[spots[0]].set(smallest).at[spots[1]].set(top_value)


def steps_of(rng, shape, split, least, high):
    level, own = 1.0, jax.random.fold_in(rng, 6)
    for axis_at, shards_of in split:
        steps = jnp.exp(jax.random.uniform(jax.random.fold_in(own, axis_at), (shards_of,), jnp.float32, least / len(split), high / len(split)))
        level = level * jnp.repeat(steps, shape[axis_at] // shards_of).reshape([-1 if axis == axis_at else 1 for axis in range(len(shape))])
    return level


def noise(own_key, extent, spread, bound, shards=(), held_as=jnp.bfloat16):
    drawn = jax.random.normal(own_key, extent, jnp.float32) * spread
    if len(shards) > 0:
        drawn = steps_of(own_key, extent, shards, -0.22, 0.18) * drawn
    return jnp.clip(drawn, min=-bound, max=bound).astype(held_as)


def setup_inputs(seed: int = 0) -> dict:
    key_of = jax.random.split(jax.random.key(seed), 17)
    inputs = noise(key_of[0], (2, TOKENS, D), 1.0, 6.0, ((0, 2), (1, 4)))
    text_patches = draw_text_patches(jax.random.fold_in(key_of[16], 71), 0)
    patch_valid = with_ends((jax.random.randint(key_of[2], (TOKENS, 4), 0, 4) < 3).astype(jnp.int32), jax.random.fold_in(key_of[2], 1), 0, 1)
    text_lengths = draw_text_lengths(jax.random.fold_in(key_of[16], 71), 0)
    bucket_table = with_ends(jax.random.randint(key_of[4], (SPAN,), 0, NB), jax.random.fold_in(key_of[4], 1), 0, NB - 1).astype(jnp.int32)
    attn_gain = jnp.clip(1.0 + 0.18 * jax.random.normal(key_of[5], (D,), jnp.float32), 0.099609375, 1.8984375).astype(jnp.bfloat16)
    query_weight = noise(key_of[6], (D, H * HD), D ** -0.5, 0.1875, ((1, 4),))
    key_weight = noise(key_of[7], (D, H * HD), D ** -0.5, 0.1875, ((1, 4),))
    value_weight = noise(key_of[8], (D, H * HD), D ** -0.5, 0.1875, ((1, 4),))
    output_weight = noise(key_of[9], (H * HD, D), (H * HD // 64) ** -0.5, 1.5, ((0, 4),))
    position_bias = noise(key_of[10], (NB, H), 1.0, 4.0, ((1, 4),), jnp.float32)
    ffn_gain = jnp.clip(1.0 + 0.18 * jax.random.normal(key_of[11], (D,), jnp.float32), 0.099609375, 1.8984375).astype(jnp.bfloat16)
    gate_weight = noise(key_of[12], (D, FF), D ** -0.5, 0.1875, ((1, 4),))
    up_weight = noise(key_of[13], (D, FF), D ** -0.5, 0.1875, ((1, 4),))
    down_weight = noise(key_of[14], (FF, D), FF ** -0.5, 0.109375, ((0, 4),))
    cotangent = noise(key_of[15], (2, TOKENS, D), 1.0, 6.0, ((0, 2), (1, 4)))
    return dict(inputs=inputs, text_patches=text_patches, patch_valid=patch_valid, text_lengths=text_lengths, bucket_table=bucket_table, attn_gain=attn_gain, query_weight=query_weight, key_weight=key_weight, value_weight=value_weight, output_weight=output_weight, position_bias=position_bias, ffn_gain=ffn_gain, gate_weight=gate_weight, up_weight=up_weight, down_weight=down_weight, cotangent=cotangent)


epsilon = 1e-06
highest = lax.Precision.HIGHEST
root_two_pi = 0.7978845608028654

@jax.custom_vjp
def low(v):
    return lax.optimization_barrier(v.astype(jnp.bfloat16)).astype(jnp.float32)

@jax.custom_vjp
def low_back(v):
    return v

def low_keep(v):
    return (low(v), None)

def low_pass(kept, grad):
    return (grad,)

def back_keep(v):
    return (v, None)

def back_low(kept, grad):
    return (low(grad),)
low.defvjp(low_keep, low_pass)
low_back.defvjp(back_keep, back_low)

def matmul(left, right):
    return jnp.dot(left, right, precision=highest)

def both_ways(tensor):
    return low_back(low(tensor))

def rms_norm(hidden, gain_values):
    return hidden * lax.rsqrt(lax.optimization_barrier(jnp.mean(hidden * hidden, axis=-1, keepdims=True)) + epsilon) * gain_values

def gelu_gated(gate_values, up_values):
    cubic = gate_values + 0.044715 * gate_values * gate_values * gate_values
    return 0.5 * gate_values * (1.0 + jnp.tanh(root_two_pi * cubic)) * up_values

def doc_positions(length_row):
    patch_rows = jnp.arange(ROWS, dtype=jnp.int32)
    patch_doc = patch_rows // PDOC
    patch_pos = patch_rows % PDOC
    first_len = length_row[0]
    text_doc = (patch_rows >= first_len).astype(jnp.int32)
    text_pos = PDOC + patch_rows - text_doc * first_len
    return (patch_doc, patch_pos, text_doc, text_pos)

def layer(block_in, patch_ids, valid_flags, length_row, bucket_table, attn_gain, query_weight, key_weight, value_weight, output_weight, position_bias, ffn_gain, gate_weight, up_weight, down_weight):
    patch_in = block_in[0]
    text_in = block_in[1]
    patch_sum = lax.optimization_barrier(jnp.sum(patch_in[patch_ids] * valid_flags.astype(jnp.float32)[:, :, None], axis=1))
    united_rows = jnp.concatenate([patch_in, text_in + patch_sum], axis=0)
    patch_doc, patch_pos, text_doc, text_pos = doc_positions(length_row)
    documents = jnp.concatenate([patch_doc, text_doc])
    positions = jnp.concatenate([patch_pos, text_pos])
    rel_index = jnp.clip(positions[None, :] - positions[:, None] + MAXPOS - 1, 0, SPAN - 1)
    same_doc = documents[:, None] == documents[None, :]
    normed_attn = low(rms_norm(united_rows, attn_gain))
    queries = both_ways(matmul(normed_attn, query_weight)).reshape(2 * ROWS, H, HD)
    keys_all = both_ways(matmul(normed_attn, key_weight)).reshape(2 * ROWS, H, HD)
    values_all = both_ways(matmul(normed_attn, value_weight)).reshape(2 * ROWS, H, HD)
    bias_rows = position_bias[bucket_table]

    def one_head(pieces):
        head_query, head_key, head_value, head_bias = pieces
        scores = matmul(head_query, head_key.T) * 0.125 + head_bias[rel_index]
        scores = jnp.where(same_doc, low_back(scores), -1000000000.0)
        row_max = lax.optimization_barrier(jnp.max(scores, axis=-1, keepdims=True))
        unnormed = jnp.exp(scores - row_max)
        attn_probs = unnormed / lax.optimization_barrier(jnp.sum(unnormed, axis=-1, keepdims=True))
        return matmul(low(attn_probs), head_value)
    head_out = lax.map(jax.checkpoint(one_head), (jnp.moveaxis(queries, 1, 0), jnp.moveaxis(keys_all, 1, 0), jnp.moveaxis(values_all, 1, 0), bias_rows.T))
    attended = both_ways(jnp.moveaxis(head_out, 0, 1).reshape(2 * ROWS, H * HD))
    middle = united_rows + low_back(matmul(attended, output_weight))
    normed_ffn = low(rms_norm(middle, ffn_gain))
    gate_values = low_back(matmul(normed_ffn, gate_weight))
    up_values = low_back(matmul(normed_ffn, up_weight))
    hidden = low(gelu_gated(gate_values, up_values))
    result = middle + low_back(matmul(hidden, down_weight))
    return result.reshape(2, ROWS, D)

def reference(inputs, text_patches, patch_valid, text_lengths, bucket_table, attn_gain, query_weight, key_weight, value_weight, output_weight, position_bias, ffn_gain, gate_weight, up_weight, down_weight, cotangent):
    groups = TOKENS // ROWS
    blocks = inputs.astype(jnp.float32).reshape(2, groups, ROWS, D).transpose(1, 0, 2, 3)
    tangents = cotangent.astype(jnp.float32).reshape(2, groups, ROWS, D).transpose(1, 0, 2, 3)
    patch_ids = text_patches.reshape(groups, ROWS, 4)
    valid_rows = patch_valid.reshape(groups, ROWS, 4)
    params = tuple((weight.astype(jnp.float32) for weight in (attn_gain, query_weight, key_weight, value_weight, output_weight, position_bias, ffn_gain, gate_weight, up_weight, down_weight)))

    def scan_step(totals, item_list):
        block_in, tangent, ids_row, flags_row, length_row = item_list

        def forward(block_value, *weights):
            return layer(block_value, ids_row, flags_row, length_row, bucket_table, *weights)
        result, pullback = jax.vjp(forward, block_in, *params)
        gradients = pullback(tangent)
        totals = tuple((running + fresh for running, fresh in zip(totals, gradients[1:])))
        return (totals, (result.astype(jnp.bfloat16), gradients[0]))
    zeros_init = tuple((jnp.zeros_like(weight) for weight in params))
    totals, (results, input_grads) = lax.scan(scan_step, zeros_init, (blocks, tangents, patch_ids, valid_rows, text_lengths))
    outputs = results.transpose(1, 0, 2, 3).reshape(2, TOKENS, D)
    input_grad = input_grads.transpose(1, 0, 2, 3).reshape(2, TOKENS, D)
    return (outputs, input_grad, totals[0], totals[1], totals[2], totals[3], totals[4], totals[5], totals[6], totals[7], totals[8], totals[9])
```

```python
import functools
import types

import jax
import jax.numpy as jnp
from jax import lax
from jax.experimental import pallas as pl
from jax.experimental.pallas import tpu as pltpu
from jax.sharding import PartitionSpec as P

MESH = pl.DeviceIdType.MESH
EPS = 1e-06
ROOT = 0.7978845608028654
HEAD = 64
NB = 32
PDOC = 128
LONG = 192
SPANS = 640
WIDE = 896
f32 = jnp.float32
bf16 = jnp.bfloat16


def nn(a, b):
    return jnp.dot(a, b, preferred_element_type=f32)


def nt(a, b):
    return lax.dot_general(a, b, (((1,), (1,)), ((), ())), preferred_element_type=f32)


def rms_scale(x):
    return lax.rsqrt(jnp.mean(x * x, axis=-1, keepdims=True) + EPS)


def row_chunks(total, step, body):
    def one(i, carry):
        body(pl.ds(pl.multiple_of(i * step, step), step))
        return carry

    lax.fori_loop(0, total // step, one, 0)


def bucket_hot(ids_row):
    return (lax.broadcasted_iota(jnp.int32, (NB, SPANS), 0) == ids_row).astype(f32)


def patch_counts(ids, valid, rows):
    places = lax.broadcasted_iota(jnp.int32, (rows, rows), 0)
    count = jnp.zeros((rows, rows), f32)
    for j in range(ids.shape[0]):
        count += jnp.where(ids[j : j + 1, :] == places, valid[j : j + 1, :].astype(f32), 0.0)
    return count


def flat(ref):
    value = ref[...].astype(f32)
    return jnp.concatenate([value[i : i + 1, :] for i in range(value.shape[0])], axis=1)


def sizes_of(heads, ff):
    width = heads * HEAD
    return (ff, ff, ff, width, 3 * width)


def mega(n_seq, n_mp, heads, order, *refs):
    ref, refs = types.SimpleNamespace(), list(refs)
    for name, many in order:
        setattr(ref, name, [refs.pop(0) for _ in range(many)] if many else refs.pop(0))
    mod, seq, mp = lax.axis_index("mod"), lax.axis_index("seq"), lax.axis_index("mp")
    rows, dim = ref.united.shape
    width = heads * HEAD
    ff = ref.wg.shape[0]
    half = dim // 2
    block = half // n_seq
    own_rows = rows // n_mp
    mine = pl.ds(pl.multiple_of(mp * own_rows, own_rows), own_rows)
    here = pl.ds(pl.multiple_of(mod * half, half), half)
    there = pl.ds(pl.multiple_of((1 - mod) * half, half), half)
    sibling = (1 - mod, seq, mp)
    used = [0]
    sends = []

    def peer_of(o):
        if n_mp == 4:
            return (mp + 1 - 2 * (mp % 2), (mp + 2) % 4, 3 - mp)[o - 1]
        return (mp + o) % n_mp

    def source_of(o):
        if n_mp == 4:
            return peer_of(o)
        return (mp + n_mp - o) % n_mp

    def message(src, dst, device, cond=None):
        index = used[0]
        used[0] += 1
        copy = pltpu.make_async_remote_copy(
            src_ref=src,
            dst_ref=dst,
            send_sem=ref.ssem.at[index],
            recv_sem=ref.rsem.at[index],
            device_id=device,
            device_id_type=MESH,
        )
        sends.append((cond, copy))
        return copy

    loads = types.SimpleNamespace()
    pairs = (
        (ref.inp_h.at[0], ref.inp), (ref.ids_h, ref.ids), (ref.pb_h, ref.pb), (ref.tp_h, ref.tp), (ref.pv_h, ref.pv),
        (ref.ag_h, ref.ag), (ref.wk_h, ref.wk), (ref.wv_h, ref.wv), (ref.wq_h, ref.wq), (ref.cot_h.at[0], ref.cot),
        (ref.wo_h, ref.wo), (ref.wd_h, ref.wd), (ref.fg_h, ref.fg), (ref.wg_h, ref.wg), (ref.wu_h, ref.wu),
    )
    copies = [pltpu.make_async_copy(src, dst, ref.lsem.at[i]) for i, (src, dst) in enumerate(pairs)]
    for copy in copies:
        copy.start()
    (loads.inp, loads.ids, loads.pb, loads.tp, loads.pv, loads.ag, loads.wk, loads.wv, loads.wq, loads.cot, loads.wo,
     loads.wd, loads.fg, loads.wg, loads.wu) = copies

    barrier = pltpu.get_barrier_semaphore()
    pl.semaphore_signal(barrier, 1, device_id=sibling, device_id_type=MESH)
    for o in range(1, n_mp):
        pl.semaphore_signal(barrier, 1, device_id=(mod, seq, peer_of(o)), device_id_type=MESH)

    @pl.when(seq > 0)
    def _():
        pl.semaphore_signal(barrier, 1, device_id=(mod, seq - 1, mp), device_id_type=MESH)

    @pl.when(seq < n_seq - 1)
    def _():
        pl.semaphore_signal(barrier, 1, device_id=(mod, seq + 1, mp), device_id_type=MESH)

    lower = (seq + n_seq - 1) // n_seq
    upper = (2 * n_seq - 2 - seq) // n_seq
    pl.semaphore_wait(barrier, n_mp + lower + upper)

    to_text = message(ref.inp_h.at[0], ref.inc, sibling, mod == 0)

    @pl.when(mod == 0)
    def _():
        to_text.start()

    first = ref.len_s[0, 0]
    long_first = first == LONG
    loads.ids.wait()
    loads.pb.wait()
    mirror = (
        lax.broadcasted_iota(jnp.int32, (128, 128), 0) + lax.broadcasted_iota(jnp.int32, (128, 128), 1) == 127
    ).astype(f32)
    turned_ids = nn(ref.ids[...].astype(f32).astype(bf16), mirror.astype(bf16))
    lines = turned_ids.shape[0]
    turned_ids = jnp.concatenate([turned_ids[i : i + 1, :] for i in reversed(range(lines))], axis=1)
    hot = bucket_hot(turned_ids.astype(jnp.int32))
    ref.hot[...] = hot
    rel = jnp.dot(ref.pb[...], hot, precision=lax.Precision.HIGHEST, preferred_element_type=f32)
    rel = jnp.concatenate([rel, jnp.zeros((heads, WIDE - SPANS), f32)], axis=1)
    blocks = rows // 64
    apart = ((-128, -128), (-128, -192), (-128, -192), (-64, -192))
    along = ((128, 128), (128, 128), (64, 192), (64, 192))

    def window(c):
        return pltpu.roll(rel, (WIDE - (c + 256)) % WIDE, 1)[:, :384]

    lane_row = lax.broadcasted_iota(jnp.int32, (1, rows), 1)
    patch_doc = lane_row // PDOC
    text_doc = (lane_row >= first).astype(jnp.int32)
    query_doc = jnp.where(mod == 0, patch_doc, text_doc)
    for kb in range(blocks):
        ref.win[kb] = window(-64 * kb)
        a0, a1 = (window(c - 64 * kb) for c in apart[kb])
        b0, b1 = (window(c - 64 * kb) for c in along[kb])
        ref.win[blocks + kb] = jnp.where(
            mod == 0, jnp.where(long_first, a0, a1), jnp.where(long_first, b0, b1)
        )
    for kb in range(2 * blocks):
        at = kb % blocks
        in_patch = (mod == 0) if kb < blocks else (mod == 1)
        key_doc = jnp.where(in_patch, at * 64 // PDOC, jnp.where(at * 64 >= first, 1, 0))
        same = query_doc == key_doc

        def one_bias(h, carry, kb=kb, same=same):
            line = jnp.broadcast_to(ref.win[kb, pl.ds(h, 1), :], (64, 384))
            table = pltpu.roll(line, 320, 1, stride=1, stride_axis=0)[:, :rows]
            ref.bias[h, kb * 64 : kb * 64 + 64, :] = jnp.where(same, table, -1000000000.0)
            return carry

        lax.fori_loop(0, heads, one_bias, 0)

    loads.cot.wait()

    def transposed(source, sides):
        sides.s[...] = source[:, there].T
        copy = message(sides.s, sides.r, sibling)
        copy.start()
        sides.t[...] = source[:, here].T
        return copy

    x_tan, x_na, x_nf, x_branch = (
        types.SimpleNamespace(t=ref.xt.at[i], s=ref.xs.at[i], r=ref.xr.at[i]) for i in range(4)
    )
    tan_sent = transposed(ref.cot, x_tan)

    loads.tp.wait()
    loads.pv.wait()
    loads.inp.wait()

    @pl.when(mod == 1)
    def _():
        count = patch_counts(ref.tp[...], ref.pv[...], rows).T.astype(bf16)
        to_text.wait_recv()
        ref.united[...] = nn(count, ref.inc[...])

    @pl.when(mod == 0)
    def _():
        ref.united[...] = jnp.zeros((rows, dim), f32)

    loads.ag.wait()
    attn_gain = flat(ref.ag)

    def first_norm(at):
        u = ref.united[at, :] + ref.inp[at, :].astype(f32)
        ref.united[at, :] = u
        ref.na[at, :] = (u * rms_scale(u) * attn_gain).astype(bf16)

    row_chunks(rows, 32, first_norm)
    loads.wk.wait()
    ref.kv[:, :width] = nn(ref.na[...], ref.wk[...]).astype(bf16)
    loads.wv.wait()
    ref.kv[:, width:] = nn(ref.na[...], ref.wv[...]).astype(bf16)
    kv_sent = message(ref.kv, ref.kvr, sibling)
    kv_sent.start()
    loads.wq.wait()
    ref.q[...] = nn(ref.na[...], ref.wq[...]).astype(bf16)
    ref.kvt[:, :rows] = ref.kv[...].T
    na_sent = transposed(ref.na, x_na)
    kv_sent.wait_recv()
    ref.kvt[:, rows:] = ref.kvr[...].T
    head_of = lax.broadcasted_iota(jnp.int32, (1, width), 1) // HEAD

    def head_mask(h):
        return (head_of == h).astype(f32).astype(bf16)

    def head_rows(h, base=0):
        return pl.ds(pl.multiple_of(base + h * HEAD, HEAD), HEAD)

    def head_fwd(h, carry):
        qm = ref.q[...] * head_mask(h)
        ref.qm[h] = qm
        s0 = nt(ref.kv[:, :width], qm) * 0.125 + ref.bias[h, :rows, :]
        s1 = nt(ref.kvr[:, :width], qm) * 0.125 + ref.bias[h, rows:, :]
        top = jnp.maximum(jnp.max(s0, axis=0, keepdims=True), jnp.max(s1, axis=0, keepdims=True))
        e0 = jnp.exp(s0 - top)
        e1 = jnp.exp(s1 - top)
        total = jnp.sum(e0, axis=0, keepdims=True) + jnp.sum(e1, axis=0, keepdims=True)
        scale = 1.0 / total
        p0 = e0 * scale
        p1 = e1 * scale
        ref.prob[h, :rows, :] = p0
        ref.prob[h, rows:, :] = p1
        values_t = ref.kvt[head_rows(h, width), :]
        ref.att_t[head_rows(h), :] = nn(values_t[:, :rows], p0.astype(bf16)) + nn(
            values_t[:, rows:], p1.astype(bf16)
        )
        return carry

    lax.fori_loop(0, heads, head_fwd, 0)
    ref.att[...] = ref.att_t[...].T.astype(bf16)
    att_sent = message(ref.att, ref.att_r, sibling)
    att_sent.start()
    loads.wo.wait()

    def scatter(c, product):
        ref.part[...] = product
        stage, land = ref.stage.at[c], ref.land.at[c]

        def cast(at):
            stage[at, :] = ref.part[at, :].astype(bf16)

        row_chunks(rows, 32, cast)
        copies = []
        for o in range(1, n_mp):
            to = peer_of(o)
            src = stage.at[pl.ds(pl.multiple_of(to * own_rows, own_rows), own_rows)]
            copies.append(message(src, land.at[o - 1], (mod, seq, to)))
        for copy in reversed(copies):
            copy.start()
        ref.keep[c] = ref.part[mine, :]
        return copies

    def summed(c, copies):
        for copy in copies:
            copy.wait_recv()
        total = ref.keep[c]
        for o in range(1, n_mp):
            total += ref.land[c, o - 1].astype(f32)
        return total

    def gather(c):
        whole = ref.whole.at[c]
        copies = [
            message(whole.at[mine], whole.at[mine], (mod, seq, peer_of(o))) for o in range(1, n_mp)
        ]
        for copy in reversed(copies):
            copy.start()
        return copies

    attn_sum = scatter(0, nn(ref.att[...], ref.wo[...]))
    loads.wd.wait()
    ref.hg[...] = nt(ref.cot[...], ref.wd[...])
    loads.fg.wait()
    ffn_gain = flat(ref.fg)
    middle = ref.united[mine, :] + summed(0, attn_sum)
    ref.mid[...] = middle
    ref.whole[0, mine, :] = (middle * rms_scale(middle) * ffn_gain).astype(bf16)
    nf_parts = gather(0)
    loads.wg.wait()
    loads.wu.wait()
    for copy in nf_parts:
        copy.wait_recv()
    ref.gate[...] = nt(ref.whole[0], ref.wg[...])
    ref.up[...] = nt(ref.whole[0], ref.wu[...])

    def gelu_rows(at):
        g, u, back = ref.gate[at, :], ref.up[at, :], ref.hg[at, :]
        squared = g * g
        t = jnp.tanh(ROOT * (g + 0.044715 * squared * g))
        left = 0.5 * (1.0 + t)
        gelu = left * g
        slope = left + 0.5 * g * (1.0 - t * t) * (ROOT * (1.0 + 0.134145 * squared))
        ref.hid[at, :] = (gelu * u).astype(bf16)
        ref.gg[at, :] = (back * u * slope).astype(bf16)
        ref.ug[at, :] = (back * gelu).astype(bf16)

    row_chunks(rows, 32, gelu_rows)
    ffn_in = scatter(1, nn(ref.gg[...], ref.wg[...]) + nn(ref.ug[...], ref.wu[...]))
    hid_sent = message(ref.hid, ref.hid_r, sibling)
    hid_sent.start()
    nf_sent = transposed(ref.whole.at[0], x_nf)
    gg_sent = message(ref.gg, ref.gg_r, sibling)
    ug_sent = message(ref.ug, ref.ug_r, sibling)
    gg_sent.start()
    ug_sent.start()

    after = (mod, jnp.minimum(seq + 1, n_seq - 1), mp)
    before = (mod, jnp.maximum(seq - 1, 0), mp)
    weights = []
    for g, s, a, b, o in zip(ref.wgrad, ref.wsend, ref.wleft, ref.wright, ref.wout, strict=True):
        right, left = {}, {}
        for j in range(n_seq):
            rng = pl.ds(j * block, block)
            if j > 0:
                right[j] = message(s.at[rng], a.at[rng], after, seq < j)
            if j < n_seq - 1:
                left[j] = message(s.at[rng], b.at[rng], before, seq > j)
        weights.append(types.SimpleNamespace(g=g, s=s, a=a, b=b, o=o, right=right, left=left))
    w_down, w_gate, w_up, w_proj, w_qkv = weights

    def product(w, x, pieces):
        lo = 0
        for own, other in pieces:
            size = own.shape[1]
            w.g[:, lo : lo + size] = nn(x.t[...], own[...]) + nn(x.r[...], other[...])
            lo += size

    def hop(w, step):
        @pl.when(seq == step)
        def _():
            for j in range(n_seq - 1, step, -1):
                rng = slice(j * block, (j + 1) * block)
                value = w.g[rng, :]
                if step > 0:
                    w.right[j].wait_recv()
                    value += w.a[rng, :].astype(f32)
                w.s[rng, :] = value.astype(bf16)
                w.right[j].start()

        @pl.when(seq == n_seq - 1 - step)
        def _():
            for j in range(n_seq - 1 - step):
                rng = slice(j * block, (j + 1) * block)
                value = w.g[rng, :]
                if step > 0:
                    w.left[j].wait_recv()
                    value += w.b[rng, :].astype(f32)
                w.s[rng, :] = value.astype(bf16)
                w.left[j].start()

    def arrive(w):
        for j in range(n_seq):

            @pl.when(seq == j)
            def _(j=j):
                rng = slice(j * block, (j + 1) * block)
                value = w.g[rng, :]
                if j > 0:
                    w.right[j].wait_recv()
                    value += w.a[rng, :].astype(f32)
                if j < n_seq - 1:
                    w.left[j].wait_recv()
                    value += w.b[rng, :].astype(f32)
                w.o[...] = value

    normed_grad = summed(1, ffn_in)
    middle = ref.mid[...]
    scale = rms_scale(middle)
    spread = normed_grad * ffn_gain
    ffn_gain_grad = jnp.sum(normed_grad * middle * scale, axis=0, keepdims=True)
    middle_grad = (
        ref.cot[mine, :].astype(f32)
        + scale * spread
        - middle * (scale * scale * scale) * jnp.mean(spread * middle, axis=-1, keepdims=True)
    )
    ref.mgrad[...] = middle_grad
    ref.whole[1, mine, :] = middle_grad.astype(bf16)
    branch_parts = gather(1)

    ffn_out = scatter(2, nn(ref.hid[...], ref.wd[...]))
    hid_sent.wait_recv()
    tan_sent.wait_recv()
    product(w_down, x_tan, [(ref.hid, ref.hid_r)])
    hop(w_down, 0)
    nf_sent.wait_recv()
    gg_sent.wait_recv()
    product(w_gate, x_nf, [(ref.gg, ref.gg_r)])
    hop(w_gate, 0)
    ug_sent.wait_recv()
    product(w_up, x_nf, [(ref.ug, ref.ug_r)])
    hop(w_up, 0)
    for copy in branch_parts:
        copy.wait_recv()
    ref.ga[...] = nt(ref.whole[1], ref.wo[...]).astype(bf16)
    branch_sent = transposed(ref.whole.at[1], x_branch)
    hop(w_down, 1)

    flip = (
        lax.broadcasted_iota(jnp.int32, (rows, rows), 0) // 64 == lax.broadcasted_iota(jnp.int32, (rows, rows), 1) // 64
    ) & (
        lax.broadcasted_iota(jnp.int32, (rows, rows), 0) % 64
        + lax.broadcasted_iota(jnp.int32, (rows, rows), 1) % 64
        == 63
    )
    ref.turn[...] = flip.astype(f32).astype(bf16)
    ref.dk[...] = jnp.zeros((2 * rows, width), f32)
    ref.dv[...] = jnp.zeros((2 * rows, width), f32)

    def head_bwd(h, carry):
        gm = ref.ga[...] * head_mask(h)
        p0, p1 = ref.prob[h, :rows, :], ref.prob[h, rows:, :]
        d0 = nt(ref.kv[:, width:], gm)
        d1 = nt(ref.kvr[:, width:], gm)
        inner = jnp.sum(p0 * d0, axis=0, keepdims=True) + jnp.sum(p1 * d1, axis=0, keepdims=True)
        g0 = (p0 * (d0 - inner)).astype(bf16)
        g1 = (p1 * (d1 - inner)).astype(bf16)
        keys_t = ref.kvt[head_rows(h), :]
        ref.dq_t[head_rows(h), :] = nn(keys_t[:, :rows], g0) + nn(keys_t[:, rows:], g1)
        qm = ref.qm[h]
        ref.dk[:rows, :] += nn(g0, qm)
        ref.dk[rows:, :] += nn(g1, qm)
        ref.dv[:rows, :] += nn(p0.astype(bf16), gm)
        ref.dv[rows:, :] += nn(p1.astype(bf16), gm)
        turn = ref.turn[...]
        for side, g in ((0, g0), (1, g1)):
            turned = nn(turn, g)
            for at in range(blocks):
                piece = turned[at * 64 : at * 64 + 64, :]
                piece = jnp.concatenate([piece, jnp.zeros((64, 384 - rows), f32)], axis=1)
                piece = pltpu.roll(piece, 1, 1, stride=1, stride_axis=0)
                ref.diag[side * blocks + at, pl.ds(h, 1), :] = jnp.sum(piece, axis=0, keepdims=True)
        return carry

    lax.fori_loop(0, heads, head_bwd, 0)
    ref.kvg_s[:, :width] = (ref.dk[rows:, :] * 0.125).astype(bf16)
    ref.kvg_s[:, width:] = ref.dv[rows:, :].astype(bf16)
    kvg_sent = message(ref.kvg_s, ref.kvg_r, sibling)
    kvg_sent.start()
    hop(w_gate, 1)
    att_sent.wait_recv()
    branch_sent.wait_recv()
    product(w_proj, x_branch, [(ref.att, ref.att_r)])
    hop(w_proj, 0)
    ref.dqb[...] = (ref.dq_t[...].T * 0.125).astype(bf16)
    kvg_sent.wait_recv()
    ref.dkb[...] = (ref.dk[:rows, :] * 0.125 + ref.kvg_r[:, :width].astype(f32)).astype(bf16)
    ref.dvb[...] = (ref.dv[:rows, :] + ref.kvg_r[:, width:].astype(f32)).astype(bf16)
    ref.part2[...] = (
        nt(ref.dqb[...], ref.wq[...]) + nt(ref.dkb[...], ref.wk[...]) + nt(ref.dvb[...], ref.wv[...])
    )
    attn_in = scatter(3, ref.part2[...])
    dq_sent = message(ref.dqb, ref.dq_r, sibling)
    dk_sent = message(ref.dkb, ref.dk_r, sibling)
    dv_sent = message(ref.dvb, ref.dv_r, sibling)
    for copy in (dq_sent, dk_sent, dv_sent):
        copy.start()

    def gain_rows(i, total):
        at = pl.ds(pl.multiple_of(i * 32, 32), 32)
        u = ref.united[at, :]
        return total + jnp.sum(ref.part2[at, :] * u * rms_scale(u), axis=0, keepdims=True)

    attn_gain_grad = lax.fori_loop(0, rows // 32, gain_rows, jnp.zeros((1, dim), f32))

    def unwindow(piece, c):
        grown = jnp.concatenate([piece, jnp.zeros((heads, WIDE - 384), f32)], axis=1)
        return pltpu.roll(grown, (c + 256) % WIDE, 1)

    total = jnp.zeros((heads, WIDE), f32)
    for kb in range(blocks):
        total += unwindow(ref.diag[kb], -64 * kb)
        piece = ref.diag[blocks + kb]
        a0, a1 = (unwindow(piece, c - 64 * kb) for c in apart[kb])
        b0, b1 = (unwindow(piece, c - 64 * kb) for c in along[kb])
        total += jnp.where(mod == 0, jnp.where(long_first, a0, a1), jnp.where(long_first, b0, b1))
    bias_grad = lax.dot_general(
        total[:, :SPANS], ref.hot[...], (((1,), (1,)), ((), ())), precision=lax.Precision.HIGHEST, preferred_element_type=f32
    )
    quarter = dim // 4
    for i, line in enumerate((attn_gain_grad, ffn_gain_grad)):
        for k in range(4):
            ref.small[4 * i + k : 4 * i + k + 1, :quarter] = line[:, k * quarter : (k + 1) * quarter]
    ref.small[:, quarter:] = jnp.zeros((8, 128), f32)
    ref.small[:heads, quarter : quarter + NB] = bias_grad
    small_mp = [message(ref.small, ref.small_p.at[o - 1], (mod, seq, peer_of(o))) for o in range(1, n_mp)]
    for copy in small_mp:
        copy.start()

    for copy in (na_sent, dq_sent, dk_sent, dv_sent):
        copy.wait_recv()
    product(w_qkv, x_na, [(ref.dqb, ref.dq_r), (ref.dkb, ref.dk_r), (ref.dvb, ref.dv_r)])
    hop(w_qkv, 0)
    hop(w_up, 1)
    for copy in small_mp:
        copy.wait_recv()
    gains = ref.small[:, :quarter]
    for o in range(1, n_mp):
        gains += ref.small_p[o - 1, :, :quarter]
    ref.small2[:, :quarter] = gains
    ref.small2[:, quarter:] = ref.small[:, quarter:]
    small_mod = message(ref.small2, ref.small_m, sibling)
    small_mod.start()

    normed_grad = summed(3, attn_in)
    u = ref.united[mine, :]
    scale = rms_scale(u)
    spread = normed_grad * attn_gain
    united_grad = (
        ref.mgrad[...]
        + scale * spread
        - u * (scale * scale * scale) * jnp.mean(spread * u, axis=-1, keepdims=True)
    )
    ref.whole[3, mine, :] = united_grad.astype(bf16)
    united_parts = gather(3)
    ref.whole[2, mine, :] = (ref.mid[...] + summed(2, ffn_out)).astype(bf16)
    output_parts = gather(2)
    small_mod.wait_recv()
    ref.small3[...] = ref.small2[...] + ref.small_m[...]
    small_right = message(ref.small4, ref.small_a, (mod, jnp.minimum(seq + 1, n_seq - 1), mp), seq < n_seq - 1)
    small_left = message(ref.small5, ref.small_b, (mod, jnp.maximum(seq - 1, 0), mp), seq > 0)

    def small_hop(step):
        @pl.when(seq == step)
        def _():
            value = ref.small3[...]
            if step > 0:
                small_right.wait_recv()
                value += ref.small_a[...]
            ref.small4[...] = value
            small_right.start()

        @pl.when(seq == n_seq - 1 - step)
        def _():
            value = ref.small3[...]
            if step > 0:
                small_left.wait_recv()
                value += ref.small_b[...]
            ref.small5[...] = value
            small_left.start()

    for step in range(n_seq - 1):
        small_hop(step)
    hop(w_proj, 1)
    hop(w_qkv, 1)
    for step in range(2, n_seq - 1):
        for w in weights:
            hop(w, step)

    backs = []
    for o in range(n_mp):
        who = mp if o == 0 else source_of(o)
        at = pl.ds(pl.multiple_of(who * own_rows, own_rows), own_rows)
        if o:
            united_parts[o - 1].wait_recv()
        back = message(ref.whole.at[3, at], ref.text_o.at[at], sibling, mod == 1)

        @pl.when(mod == 1)
        def _(back=back):
            back.start()

        backs.append(back)
    for copy in output_parts:
        copy.wait_recv()
    ref.out_o[...] = ref.whole[2]
    ref.own_o[...] = ref.whole[3]
    for w in weights:
        arrive(w)

    @pl.when(seq == n_seq - 1)
    def _():
        small_right.wait_recv()

    @pl.when(seq == 0)
    def _():
        small_left.wait_recv()

    ref.small_o[...] = (
        ref.small3[...]
        + jnp.where(seq > 0, ref.small_a[...], 0.0)
        + jnp.where(seq < n_seq - 1, ref.small_b[...], 0.0)
    )

    @pl.when(mod == 0)
    def _():
        for back in backs:
            back.wait_recv()

    @pl.when(mod == 1)
    def _():
        ref.text_o[...] = jnp.zeros((rows, dim), bf16)

    for cond, copy in sends:
        if cond is None:
            copy.wait_send()
        else:

            @pl.when(cond)
            def _(copy=copy):
                copy.wait_send()

    assert used[0] <= ref.ssem.shape[0]


def finish(n_seq, heads, width, ids, valid, own, text, out, gd, gg, gu, go, gqkv, small,
           o_out, o_in, o_ag, o_q, o_k, o_v, o_o, o_pb, o_fg, o_gate, o_up, o_down, hold):
    mod, seq = lax.axis_index("mod"), lax.axis_index("seq")
    rows, dim = own.shape
    place = mod * n_seq + seq
    o_out[0] = out[...]

    @pl.when(mod == 0)
    def _():
        count = patch_counts(ids[...], valid[...], rows)
        o_in[0] = own[...].astype(f32) + nn(count.astype(bf16), text[...])

    @pl.when(mod == 1)
    def _():
        o_in[0] = own[...].astype(f32)

    o_q[...] = gqkv[:, :width]
    o_k[...] = gqkv[:, width : 2 * width]
    o_v[...] = gqkv[:, 2 * width :]
    o_o[...] = go[...].T
    o_gate[...] = gg[...].T
    o_up[...] = gu[...].T
    o_down[...] = gd[...].T
    quarter = dim // 4
    part = dim // (2 * n_seq)
    for i, o_gain in enumerate((o_ag, o_fg)):
        line = jnp.concatenate([small[4 * i + k : 4 * i + k + 1, :quarter] for k in range(4)], axis=1)
        line = pltpu.roll(jnp.broadcast_to(line, (8, dim)), dim - place * part, 1)
        o_gain[...] = line[:1, :part]
    few = NB // (2 * n_seq)
    hold[...] = small[:, quarter:].T
    o_pb[...] = hold[pl.ds(place * few, few), :heads]


def per_device(n_seq, n_mp, *args):
    (inputs, text_patches, patch_valid, text_lengths, bucket_table, attn_gain, query_weight, key_weight,
     value_weight, output_weight, position_bias, ffn_gain, gate_weight, up_weight, down_weight, cotangent) = args
    rows, dim = inputs.shape[1:]
    heads = position_bias.shape[1]
    width = heads * HEAD
    ff = down_weight.shape[0]
    own_rows = rows // n_mp
    half = dim // 2
    block = half // n_seq
    text_patches, patch_valid, position_bias = text_patches.T, patch_valid.T, position_bias.T
    gate_weight, up_weight = gate_weight.T, up_weight.T
    ids = jnp.pad(bucket_table, (0, SPANS - bucket_table.shape[0])).reshape(SPANS // 128, 128)
    given = dict(
        len_s=text_lengths, inp_h=inputs, tp_h=text_patches, pv_h=patch_valid, ids_h=ids, pb_h=position_bias,
        ag_h=attn_gain.reshape(dim // 128, 128), fg_h=ffn_gain.reshape(dim // 128, 128), wq_h=query_weight, wk_h=key_weight,
        wv_h=value_weight, wo_h=output_weight, wg_h=gate_weight, wu_h=up_weight, wd_h=down_weight, cot_h=cotangent,
    )
    sizes = sizes_of(heads, ff)
    results = dict(
        wout=[((block, size), f32) for size in sizes], out_o=((rows, dim), bf16), own_o=((rows, dim), bf16),
        text_o=((rows, dim), bf16), small_o=((8, dim // 4 + 128), f32),
    )
    small = ((8, dim // 4 + 128), f32)
    sent = [((half, size), bf16) for size in sizes]
    held = dict(
        inp=((rows, dim), bf16), ids=(ids.shape, jnp.int32), hot=((NB, SPANS), f32), pb=((heads, NB), f32), tp=(text_patches.shape, jnp.int32),
        pv=(patch_valid.shape, jnp.int32), ag=((dim // 128, 128), bf16), fg=((dim // 128, 128), bf16), wq=((dim, width), bf16),
        wk=((dim, width), bf16), wv=((dim, width), bf16), wo=((width, dim), bf16), wg=((ff, dim), bf16),
        wu=((ff, dim), bf16), wd=((ff, dim), bf16), cot=((rows, dim), bf16), inc=((rows, dim), bf16),
        win=((2 * rows // 64, heads, 384), f32), diag=((2 * rows // 64, heads, 384), f32),
        bias=((heads, 2 * rows, rows), f32), prob=((heads, 2 * rows, rows), f32), xt=((4, half, rows), bf16), xs=((4, half, rows), bf16), xr=((4, half, rows), bf16),
        united=((rows, dim), f32), na=((rows, dim), bf16),
        kv=((rows, 2 * width), bf16), kvr=((rows, 2 * width), bf16), kvt=((2 * width, 2 * rows), bf16),
        q=((rows, width), bf16), qm=((heads, rows, width), bf16), att_t=((width, rows), f32), att=((rows, width), bf16),
        att_r=((rows, width), bf16), part=((rows, dim), f32), part2=((rows, dim), f32), stage=((4, rows, dim), bf16),
        land=((4, n_mp - 1, own_rows, dim), bf16), keep=((4, own_rows, dim), f32), whole=((4, rows, dim), bf16),
        hg=((rows, ff), f32), mid=((own_rows, dim), f32), mgrad=((own_rows, dim), f32), gate=((rows, ff), f32),
        up=((rows, ff), f32), ga=((rows, width), bf16), turn=((rows, rows), bf16), dk=((2 * rows, width), f32),
        dv=((2 * rows, width), f32), dq_t=((width, rows), f32), kvg_s=((rows, 2 * width), bf16),
        kvg_r=((rows, 2 * width), bf16),
    )
    held.update(
        hid=((rows, ff), bf16), hid_r=((rows, ff), bf16), gg=((rows, ff), bf16), gg_r=((rows, ff), bf16),
        ug=((rows, ff), bf16), ug_r=((rows, ff), bf16), dqb=((rows, width), bf16), dq_r=((rows, width), bf16),
        dkb=((rows, width), bf16), dk_r=((rows, width), bf16), dvb=((rows, width), bf16), dv_r=((rows, width), bf16),
        wgrad=[((half, size), f32) for size in sizes], wsend=sent, wleft=sent, wright=sent, small=small, small2=small,
        small3=small, small4=small, small5=small, small_m=small, small_a=small, small_b=small,
        small_p=((n_mp - 1,) + small[0], f32),
    )
    count = 40 + 9 * n_mp + 10 * n_seq
    order = [(name, 0) for name in given]
    out_shape, scratch = [], []
    for specs, into, make in ((results, out_shape, jax.ShapeDtypeStruct), (held, scratch, pltpu.VMEM)):
        for name, spec in specs.items():
            many = spec if isinstance(spec, list) else [spec]
            order.append((name, len(many) if isinstance(spec, list) else 0))
            into.extend(make(*one) for one in many)
    for i, size in enumerate((count, count, len(given) - 1)):
        order.append((("ssem", "rsem", "lsem")[i], 0))
        scratch.append(pltpu.SemaphoreType.DMA((size,)))
    vmem = pl.BlockSpec(memory_space=pltpu.VMEM)
    done = pl.pallas_call(
        functools.partial(mega, n_seq, n_mp, heads, order),
        out_shape=out_shape,
        in_specs=[pl.BlockSpec(memory_space=pltpu.SMEM)] + [pl.BlockSpec(memory_space=pl.ANY)] * (len(given) - 1),
        out_specs=[vmem] * len(out_shape),
        scratch_shapes=scratch,
        compiler_params=pltpu.CompilerParams(
            collective_id=0, has_side_effects=True, vmem_limit_bytes=63 * 2**20
        ),
        name="layer",
    )(*given.values())
    *wout, out, own, text, small_sum = done
    down_sum, gate_sum, up_sum, proj_sum, qkv_sum = wout
    part = dim // (2 * n_seq)
    few = NB // (2 * n_seq)
    shapes = [
        ((1, rows, dim), bf16), ((1, rows, dim), f32), ((1, part), f32), ((block, width), f32), ((block, width), f32),
        ((block, width), f32), ((width, block), f32), ((few, heads), f32), ((1, part), f32), ((ff, block), f32),
        ((ff, block), f32), ((ff, block), f32),
    ]
    outs = pl.pallas_call(
        functools.partial(finish, n_seq, heads, width),
        out_shape=[jax.ShapeDtypeStruct(*spec) for spec in shapes],
        in_specs=[vmem] * 11,
        out_specs=[vmem] * 12,
        scratch_shapes=[pltpu.VMEM((128, 8), f32)],
        compiler_params=pltpu.CompilerParams(vmem_limit_bytes=63 * 2**20),
        name="finish",
    )(
        text_patches, patch_valid, own, text, out, down_sum, gate_sum, up_sum, proj_sum, qkv_sum, small_sum
    )
    outs = list(outs)
    for i in (9, 10):
        outs[i] = outs[i].T
    outs[2] = outs[2].reshape(part)
    outs[8] = outs[8].reshape(part)
    return tuple(outs)


def solution(mesh):
    group = ("mod", "seq")
    in_specs = (
        P("mod", "seq", None), P("seq", None), P("seq", None), P("seq", None), P(), P(), P(None, "mp"), P(None, "mp"),
        P(None, "mp"), P("mp", None), P(None, "mp"), P(), P(None, "mp"), P(None, "mp"), P("mp", None),
        P("mod", "seq", None),
    )
    out_specs = (
        P("mod", "seq", None), P("mod", "seq", None), P(group), P(group, "mp"), P(group, "mp"), P(group, "mp"),
        P("mp", group), P(group, "mp"), P(group), P(group, "mp"), P(group, "mp"), P("mp", group),
    )
    body = functools.partial(per_device, mesh.shape["seq"], mesh.shape["mp"])
    return jax.shard_map(body, mesh=mesh, in_specs=in_specs, out_specs=out_specs, check_vma=False)
```

```python
import functools
import types

import jax
import jax.numpy as jnp
from jax import lax
from jax.experimental import pallas as pl
from jax.experimental.pallas import tpu as pltpu
from jax.sharding import PartitionSpec as P

MESH = pl.DeviceIdType.MESH
EPS = 1e-06
ROOT = 0.7978845608028654
HEAD = 64
NB = 32
PDOC = 128
LONG = 192
SPANS = 640
WIDE = 896
f32 = jnp.float32
bf16 = jnp.bfloat16


def nn(a, b):
    return jnp.dot(a, b, preferred_element_type=f32)


def nt(a, b):
    return lax.dot_general(a, b, (((1,), (1,)), ((), ())), preferred_element_type=f32)


def rms_scale(x):
    return lax.rsqrt(jnp.mean(x * x, axis=-1, keepdims=True) + EPS)


def row_chunks(total, step, body):
    def one(i, carry):
        body(pl.ds(pl.multiple_of(i * step, step), step))
        return carry

    lax.fori_loop(0, total // step, one, 0)


def bucket_hot(ids_row):
    return (lax.broadcasted_iota(jnp.int32, (NB, SPANS), 0) == ids_row).astype(f32)


def patch_counts(ids, valid, rows):
    places = lax.broadcasted_iota(jnp.int32, (rows, rows), 0)
    count = jnp.zeros((rows, rows), f32)
    for j in range(ids.shape[0]):
        count += jnp.where(ids[j : j + 1, :] == places, valid[j : j + 1, :].astype(f32), 0.0)
    return count


def flat(ref):
    value = ref[...].astype(f32)
    return jnp.concatenate([value[i : i + 1, :] for i in range(value.shape[0])], axis=1)


def sizes_of(heads, ff):
    width = heads * HEAD
    return (ff, ff, ff, width, 3 * width)


def mega(n_seq, n_mp, heads, order, *refs):
    ref, refs = types.SimpleNamespace(), list(refs)
    for name, many in order:
        setattr(ref, name, [refs.pop(0) for _ in range(many)] if many else refs.pop(0))
    mod, seq, mp = lax.axis_index("mod"), lax.axis_index("seq"), lax.axis_index("mp")
    rows, dim = ref.united.shape
    width = heads * HEAD
    ff = ref.wg.shape[0]
    half = dim // 2
    block = half // n_seq
    own_rows = rows // n_mp
    mine = pl.ds(pl.multiple_of(mp * own_rows, own_rows), own_rows)
    here = pl.ds(pl.multiple_of(mod * half, half), half)
    there = pl.ds(pl.multiple_of((1 - mod) * half, half), half)
    sibling = (1 - mod, seq, mp)
    used = [0]
    sends = []
    is_end = (seq == 0) | (seq == n_seq - 1)
    not_end = (seq > 0) & (seq < n_seq - 1)
    is_inner = (seq == 1) | (seq == n_seq - 2)
    inner = (mod, seq + 1 - 2 * (seq // (n_seq - 1)), mp)

    def when(cond, body):
        if cond is None:
            body()
        else:
            pl.when(cond)(body)

    def peer_of(o):
        if n_mp == 4:
            return (mp + 1 - 2 * (mp % 2), (mp + 2) % 4, 3 - mp)[o - 1]
        return (mp + o) % n_mp

    def source_of(o):
        if n_mp == 4:
            return peer_of(o)
        return (mp + n_mp - o) % n_mp

    def message(src, dst, device, cond=None):
        index = used[0]
        used[0] += 1
        copy = pltpu.make_async_remote_copy(
            src_ref=src,
            dst_ref=dst,
            send_sem=ref.ssem.at[index],
            recv_sem=ref.rsem.at[index],
            device_id=device,
            device_id_type=MESH,
        )
        sends.append((cond, copy))
        return copy

    loads = types.SimpleNamespace()
    pairs = (
        (ref.inp_h.at[0], ref.inp), (ref.ids_h, ref.ids), (ref.pb_h, ref.pb), (ref.tp_h, ref.tp), (ref.pv_h, ref.pv),
        (ref.ag_h, ref.ag), (ref.wk_h, ref.wk), (ref.wv_h, ref.wv), (ref.wq_h, ref.wq), (ref.cot_h.at[0], ref.cot),
        (ref.wo_h, ref.wo), (ref.wd_h, ref.wd), (ref.fg_h, ref.fg), (ref.wg_h, ref.wg), (ref.wu_h, ref.wu),
    )
    copies = [pltpu.make_async_copy(src, dst, ref.lsem.at[i]) for i, (src, dst) in enumerate(pairs)]
    for copy in copies:
        copy.start()
    (loads.inp, loads.ids, loads.pb, loads.tp, loads.pv, loads.ag, loads.wk, loads.wv, loads.wq, loads.cot, loads.wo,
     loads.wd, loads.fg, loads.wg, loads.wu) = copies

    barrier = pltpu.get_barrier_semaphore()
    pl.semaphore_signal(barrier, 1, device_id=sibling, device_id_type=MESH)
    for o in range(1, n_mp):
        pl.semaphore_signal(barrier, 1, device_id=(mod, seq, peer_of(o)), device_id_type=MESH)

    for o in range(1, n_seq):
        pl.semaphore_signal(barrier, 1, device_id=(mod, (seq + o) % n_seq, mp), device_id_type=MESH)
    pl.semaphore_wait(barrier, n_mp + n_seq - 1)

    to_text = message(ref.inp_h.at[0], ref.inc, sibling, mod == 0)

    @pl.when(mod == 0)
    def _():
        to_text.start()

    cot_end = message(ref.cot_h.at[0], ref.cot_e, inner, is_end)
    when(is_end, cot_end.start)

    first = ref.len_s[0, 0]
    long_first = first == LONG
    loads.ids.wait()
    loads.pb.wait()
    mirror = (
        lax.broadcasted_iota(jnp.int32, (128, 128), 0) + lax.broadcasted_iota(jnp.int32, (128, 128), 1) == 127
    ).astype(f32)
    turned_ids = nn(ref.ids[...].astype(f32).astype(bf16), mirror.astype(bf16))
    lines = turned_ids.shape[0]
    turned_ids = jnp.concatenate([turned_ids[i : i + 1, :] for i in reversed(range(lines))], axis=1)
    hot = bucket_hot(turned_ids.astype(jnp.int32))
    ref.hot[...] = hot
    rel = jnp.dot(ref.pb[...], hot, precision=lax.Precision.HIGHEST, preferred_element_type=f32)
    rel = jnp.concatenate([rel, jnp.zeros((heads, WIDE - SPANS), f32)], axis=1)
    blocks = rows // 64
    apart = ((-128, -128), (-128, -192), (-128, -192), (-64, -192))
    along = ((128, 128), (128, 128), (64, 192), (64, 192))

    def window(c):
        return pltpu.roll(rel, (WIDE - (c + 256)) % WIDE, 1)[:, :384]

    lane_row = lax.broadcasted_iota(jnp.int32, (1, rows), 1)
    patch_doc = lane_row // PDOC
    text_doc = (lane_row >= first).astype(jnp.int32)
    query_doc = jnp.where(mod == 0, patch_doc, text_doc)
    for kb in range(blocks):
        ref.win[kb] = window(-64 * kb)
        a0, a1 = (window(c - 64 * kb) for c in apart[kb])
        b0, b1 = (window(c - 64 * kb) for c in along[kb])
        ref.win[blocks + kb] = jnp.where(
            mod == 0, jnp.where(long_first, a0, a1), jnp.where(long_first, b0, b1)
        )
    for kb in range(2 * blocks):
        at = kb % blocks
        in_patch = (mod == 0) if kb < blocks else (mod == 1)
        key_doc = jnp.where(in_patch, at * 64 // PDOC, jnp.where(at * 64 >= first, 1, 0))
        same = query_doc == key_doc

        def one_bias(h, carry, kb=kb, same=same):
            line = jnp.broadcast_to(ref.win[kb, pl.ds(h, 1), :], (64, 384))
            table = pltpu.roll(line, 320, 1, stride=1, stride_axis=0)[:, :rows]
            ref.bias[h, kb * 64 : kb * 64 + 64, :] = jnp.where(same, table, -1000000000.0)
            return carry

        lax.fori_loop(0, heads, one_bias, 0)

    loads.cot.wait()

    def transposed(source, sides, cond=None):
        copy = message(sides.s, sides.r, sibling, cond)

        def body():
            sides.s[...] = source[:, there].T
            copy.start()
            sides.t[...] = source[:, here].T

        when(cond, body)
        return copy

    x_tan, x_na, x_nf, x_branch, x_tan_e, x_nf_e = (
        types.SimpleNamespace(t=ref.xt.at[i], s=ref.xs.at[i], r=ref.xr.at[i]) for i in range(6)
    )
    tan_sent = transposed(ref.cot, x_tan, not_end)

    loads.tp.wait()
    loads.pv.wait()
    loads.inp.wait()

    @pl.when(mod == 1)
    def _():
        count = patch_counts(ref.tp[...], ref.pv[...], rows).T.astype(bf16)
        to_text.wait_recv()
        ref.united[...] = nn(count, ref.inc[...])

    @pl.when(mod == 0)
    def _():
        ref.united[...] = jnp.zeros((rows, dim), f32)

    loads.ag.wait()
    attn_gain = flat(ref.ag)

    def first_norm(at):
        u = ref.united[at, :] + ref.inp[at, :].astype(f32)
        ref.united[at, :] = u
        ref.na[at, :] = (u * rms_scale(u) * attn_gain).astype(bf16)

    row_chunks(rows, 32, first_norm)
    loads.wk.wait()
    ref.kv[:, :width] = nn(ref.na[...], ref.wk[...]).astype(bf16)
    loads.wv.wait()
    ref.kv[:, width:] = nn(ref.na[...], ref.wv[...]).astype(bf16)
    kv_sent = message(ref.kv, ref.kvr, sibling)
    kv_sent.start()
    loads.wq.wait()
    ref.q[...] = nn(ref.na[...], ref.wq[...]).astype(bf16)
    ref.kvt[:, :rows] = ref.kv[...].T
    na_sent = transposed(ref.na, x_na)
    kv_sent.wait_recv()
    ref.kvt[:, rows:] = ref.kvr[...].T
    head_of = lax.broadcasted_iota(jnp.int32, (1, width), 1) // HEAD

    def head_mask(h):
        return (head_of == h).astype(f32).astype(bf16)

    def head_rows(h, base=0):
        return pl.ds(pl.multiple_of(base + h * HEAD, HEAD), HEAD)

    def head_fwd(h, carry):
        qm = ref.q[...] * head_mask(h)
        ref.qm[h] = qm
        s0 = nt(ref.kv[:, :width], qm) * 0.125 + ref.bias[h, :rows, :]
        s1 = nt(ref.kvr[:, :width], qm) * 0.125 + ref.bias[h, rows:, :]
        top = jnp.maximum(jnp.max(s0, axis=0, keepdims=True), jnp.max(s1, axis=0, keepdims=True))
        e0 = jnp.exp(s0 - top)
        e1 = jnp.exp(s1 - top)
        total = jnp.sum(e0, axis=0, keepdims=True) + jnp.sum(e1, axis=0, keepdims=True)
        scale = 1.0 / total
        p0 = e0 * scale
        p1 = e1 * scale
        ref.prob[h, :rows, :] = p0
        ref.prob[h, rows:, :] = p1
        values_t = ref.kvt[head_rows(h, width), :]
        ref.att_t[head_rows(h), :] = nn(values_t[:, :rows], p0.astype(bf16)) + nn(
            values_t[:, rows:], p1.astype(bf16)
        )
        return carry

    lax.fori_loop(0, heads, head_fwd, 0)
    ref.att[...] = ref.att_t[...].T.astype(bf16)
    att_sent = message(ref.att, ref.att_r, sibling)
    att_sent.start()
    loads.wo.wait()

    def scatter(c, rows_of, hold=False):
        stage, land = ref.stage.at[c], ref.land.at[c]
        copies = []
        for o in range(n_mp - 1, 0, -1):
            to = peer_of(o)
            at = pl.ds(pl.multiple_of(to * own_rows, own_rows), own_rows)
            stage[at, :] = rows_of(at).astype(bf16)
            copies.append(message(stage.at[at], land.at[o - 1], (mod, seq, to)))
            if not hold:
                copies[-1].start()
        ref.keep[c] = rows_of(mine)
        return copies

    def summed(c, copies):
        for copy in copies:
            copy.wait_recv()
        total = ref.keep[c]
        for o in range(1, n_mp):
            total += ref.land[c, o - 1].astype(f32)
        return total

    def gather(c):
        whole = ref.whole.at[c]
        copies = [
            message(whole.at[mine], whole.at[mine], (mod, seq, peer_of(o))) for o in range(1, n_mp)
        ]
        for copy in reversed(copies):
            copy.start()
        return copies

    attn_sum = scatter(0, lambda at: nn(ref.att[at, :], ref.wo[...]))
    loads.wd.wait()
    ref.hg[...] = nt(ref.cot[...], ref.wd[...])
    loads.fg.wait()
    ffn_gain = flat(ref.fg)
    middle = ref.united[mine, :] + summed(0, attn_sum)
    ref.mid[...] = middle
    ref.whole[0, mine, :] = (middle * rms_scale(middle) * ffn_gain).astype(bf16)
    nf_parts = gather(0)

    def to_inner(who):
        at = pl.ds(pl.multiple_of(who * own_rows, own_rows), own_rows)
        copy = message(ref.whole.at[0, at], ref.nf_e.at[at], inner, is_end)
        when(is_end, copy.start)
        return copy

    nf_end = [to_inner(mp)]
    tan_e_sent = message(x_tan_e.s, x_tan_e.r, sibling, is_inner)

    @pl.when(is_inner)
    def _():
        cot_end.wait_recv()
        x_tan_e.s[...] = ref.cot_e[:, there].T
        tan_e_sent.start()
        x_tan_e.t[...] = ref.cot_e[:, here].T
        ref.hg_e[...] = nt(ref.cot_e[...], ref.wd[...])

    loads.wg.wait()
    loads.wu.wait()
    for o, copy in enumerate(nf_parts, 1):
        copy.wait_recv()
        nf_end.append(to_inner(source_of(o)))
    ref.gate[...] = nt(ref.whole[0], ref.wg[...])
    ref.up[...] = nt(ref.whole[0], ref.wu[...])

    def gelu_rows(at, back_ref=ref.hg, hid=ref.hid, gg=ref.gg, ug=ref.ug):
        g, u, back = ref.gate[at, :], ref.up[at, :], back_ref[at, :]
        squared = g * g
        t = jnp.tanh(ROOT * (g + 0.044715 * squared * g))
        left = 0.5 * (1.0 + t)
        gelu = left * g
        slope = left + 0.5 * g * (1.0 - t * t) * (ROOT * (1.0 + 0.134145 * squared))
        hid[at, :] = (gelu * u).astype(bf16)
        gg[at, :] = (back * u * slope).astype(bf16)
        ug[at, :] = (back * gelu).astype(bf16)

    row_chunks(rows, 32, gelu_rows)
    ffn_in = scatter(1, lambda at: nn(ref.gg[at, :], ref.wg[...]) + nn(ref.ug[at, :], ref.wu[...]))
    hid_sent = message(ref.hid, ref.hid_r, sibling, not_end)
    gg_sent = message(ref.gg, ref.gg_r, sibling, not_end)
    ug_sent = message(ref.ug, ref.ug_r, sibling, not_end)
    when(not_end, hid_sent.start)
    nf_sent = transposed(ref.whole.at[0], x_nf, not_end)
    when(not_end, gg_sent.start)
    when(not_end, ug_sent.start)

    after = (mod, jnp.minimum(seq + 1, n_seq - 1), mp)
    before = (mod, jnp.maximum(seq - 1, 0), mp)
    weights = []
    ends = (1, 1, 1, 0, 0)
    for e, g, s, a, b, o in zip(ends, ref.wgrad, ref.wsend, ref.wleft, ref.wright, ref.wout, strict=True):
        right, left = {}, {}
        for j in range(n_seq):
            rng = pl.ds(j * block, block)
            if j > e:
                right[j] = message(s.at[rng], a.at[rng], after, (seq >= e) & (seq < j))
            if j < n_seq - 1 - e:
                left[j] = message(s.at[rng], b.at[rng], before, (seq < n_seq - e) & (seq > j))
        weights.append(types.SimpleNamespace(e=e, g=g, s=s, a=a, b=b, o=o, right=right, left=left))
    w_down, w_gate, w_up, w_proj, w_qkv = weights

    def product(w, x, pieces, more=False):
        lo = 0
        for own, other in pieces:
            size = own.shape[1]
            both = nn(x.t[...], own[...]) + nn(x.r[...], other[...])
            if more:
                both += w.g[:, lo : lo + size]
            w.g[:, lo : lo + size] = both
            lo += size

    def hop(w, step):
        if step >= n_seq - 1 - w.e:
            return

        @pl.when(seq == w.e + step)
        def _():
            for j in range(n_seq - 1, w.e + step, -1):
                rng = slice(j * block, (j + 1) * block)
                value = w.g[rng, :]
                if step > 0:
                    w.right[j].wait_recv()
                    value += w.a[rng, :].astype(f32)
                w.s[rng, :] = value.astype(bf16)
                w.right[j].start()

        @pl.when(seq == n_seq - 1 - w.e - step)
        def _():
            for j in range(n_seq - 1 - w.e - step):
                rng = slice(j * block, (j + 1) * block)
                value = w.g[rng, :]
                if step > 0:
                    w.left[j].wait_recv()
                    value += w.b[rng, :].astype(f32)
                w.s[rng, :] = value.astype(bf16)
                w.left[j].start()

    def arrive(w):
        for j in range(n_seq):

            @pl.when(seq == j)
            def _(j=j):
                rng = slice(j * block, (j + 1) * block)
                value = w.g[rng, :] if w.e <= j < n_seq - w.e else jnp.zeros(w.o.shape, f32)
                if j > w.e:
                    w.right[j].wait_recv()
                    value += w.a[rng, :].astype(f32)
                if j < n_seq - 1 - w.e:
                    w.left[j].wait_recv()
                    value += w.b[rng, :].astype(f32)
                w.o[...] = value

    hid_e_sent = message(ref.hid_e, ref.hid_er, sibling, is_inner)
    gg_e_sent = message(ref.gg_e, ref.gg_er, sibling, is_inner)
    ug_e_sent = message(ref.ug_e, ref.ug_er, sibling, is_inner)
    nf_e_sent = message(x_nf_e.s, x_nf_e.r, sibling, is_inner)

    @pl.when(is_inner)
    def _():
        for copy in nf_end:
            copy.wait_recv()
        ref.gate[...] = nt(ref.nf_e[...], ref.wg[...])
        ref.up[...] = nt(ref.nf_e[...], ref.wu[...])
        row_chunks(rows, 32, lambda at: gelu_rows(at, ref.hg_e, ref.hid_e, ref.gg_e, ref.ug_e))
        hid_e_sent.start()
        x_nf_e.s[...] = ref.nf_e[:, there].T
        nf_e_sent.start()
        gg_e_sent.start()
        ug_e_sent.start()
        x_nf_e.t[...] = ref.nf_e[:, here].T

    @pl.when(not_end)
    def _():
        hid_sent.wait_recv()
        tan_sent.wait_recv()
        product(w_down, x_tan, [(ref.hid, ref.hid_r)])
        nf_sent.wait_recv()
        gg_sent.wait_recv()
        product(w_gate, x_nf, [(ref.gg, ref.gg_r)])
        ug_sent.wait_recv()
        product(w_up, x_nf, [(ref.ug, ref.ug_r)])

    def end_products(w, x, pieces, needs):
        @pl.when(is_inner)
        def _():
            for copy in needs:
                copy.wait_recv()
            product(w, x, pieces, more=True)

        hop(w, 0)

    normed_grad = summed(1, ffn_in)
    middle = ref.mid[...]
    scale = rms_scale(middle)
    spread = normed_grad * ffn_gain
    ffn_gain_grad = jnp.sum(normed_grad * middle * scale, axis=0, keepdims=True)
    middle_grad = (
        ref.cot[mine, :].astype(f32)
        + scale * spread
        - middle * (scale * scale * scale) * jnp.mean(spread * middle, axis=-1, keepdims=True)
    )
    ref.mgrad[...] = middle_grad
    ref.whole[1, mine, :] = middle_grad.astype(bf16)
    branch_parts = gather(1)

    end_products(w_down, x_tan_e, [(ref.hid_e, ref.hid_er)], (hid_e_sent, tan_e_sent))
    end_products(w_gate, x_nf_e, [(ref.gg_e, ref.gg_er)], (gg_e_sent, nf_e_sent))
    end_products(w_up, x_nf_e, [(ref.ug_e, ref.ug_er)], (ug_e_sent,))
    ffn_out = scatter(2, lambda at: nn(ref.hid[at, :], ref.wd[...]), hold=True)
    for copy in branch_parts:
        copy.wait_recv()
    for copy in ffn_out:
        copy.start()
    ref.ga[...] = nt(ref.whole[1], ref.wo[...]).astype(bf16)
    branch_sent = transposed(ref.whole.at[1], x_branch)

    flip = (
        lax.broadcasted_iota(jnp.int32, (rows, rows), 0) // 64 == lax.broadcasted_iota(jnp.int32, (rows, rows), 1) // 64
    ) & (
        lax.broadcasted_iota(jnp.int32, (rows, rows), 0) % 64
        + lax.broadcasted_iota(jnp.int32, (rows, rows), 1) % 64
        == 63
    )
    ref.turn[...] = flip.astype(f32).astype(bf16)
    ref.dk[...] = jnp.zeros((2 * rows, width), f32)
    ref.dv[...] = jnp.zeros((2 * rows, width), f32)

    def head_bwd(h, carry):
        gm = ref.ga[...] * head_mask(h)
        p0, p1 = ref.prob[h, :rows, :], ref.prob[h, rows:, :]
        d0 = nt(ref.kv[:, width:], gm)
        d1 = nt(ref.kvr[:, width:], gm)
        inner = jnp.sum(p0 * d0, axis=0, keepdims=True) + jnp.sum(p1 * d1, axis=0, keepdims=True)
        g0 = (p0 * (d0 - inner)).astype(bf16)
        g1 = (p1 * (d1 - inner)).astype(bf16)
        keys_t = ref.kvt[head_rows(h), :]
        ref.dq_t[head_rows(h), :] = nn(keys_t[:, :rows], g0) + nn(keys_t[:, rows:], g1)
        qm = ref.qm[h]
        ref.dk[:rows, :] += nn(g0, qm)
        ref.dk[rows:, :] += nn(g1, qm)
        ref.dv[:rows, :] += nn(p0.astype(bf16), gm)
        ref.dv[rows:, :] += nn(p1.astype(bf16), gm)
        turn = ref.turn[...]
        for side, g in ((0, g0), (1, g1)):
            turned = nn(turn, g)
            for at in range(blocks):
                piece = turned[at * 64 : at * 64 + 64, :]
                piece = jnp.concatenate([piece, jnp.zeros((64, 384 - rows), f32)], axis=1)
                piece = pltpu.roll(piece, 1, 1, stride=1, stride_axis=0)
                ref.diag[side * blocks + at, pl.ds(h, 1), :] = jnp.sum(piece, axis=0, keepdims=True)
        return carry

    lax.fori_loop(0, heads, head_bwd, 0)
    ref.kvg_s[:, :width] = (ref.dk[rows:, :] * 0.125).astype(bf16)
    ref.kvg_s[:, width:] = ref.dv[rows:, :].astype(bf16)
    kvg_sent = message(ref.kvg_s, ref.kvg_r, sibling)
    kvg_sent.start()
    ref.whole[2, mine, :] = (ref.mid[...] + summed(2, ffn_out)).astype(bf16)
    output_parts = gather(2)
    att_sent.wait_recv()
    branch_sent.wait_recv()
    product(w_proj, x_branch, [(ref.att, ref.att_r)])
    hop(w_proj, 0)
    ref.dqb[...] = (ref.dq_t[...].T * 0.125).astype(bf16)
    kvg_sent.wait_recv()
    ref.dkb[...] = (ref.dk[:rows, :] * 0.125 + ref.kvg_r[:, :width].astype(f32)).astype(bf16)
    ref.dvb[...] = (ref.dv[:rows, :] + ref.kvg_r[:, width:].astype(f32)).astype(bf16)

    def attn_rows(at):
        rows_in = nt(ref.dqb[at, :], ref.wq[...]) + nt(ref.dkb[at, :], ref.wk[...]) + nt(ref.dvb[at, :], ref.wv[...])
        ref.part2[at, :] = rows_in
        return rows_in

    attn_in = scatter(3, attn_rows)
    dq_sent = message(ref.dqb, ref.dq_r, sibling)
    dk_sent = message(ref.dkb, ref.dk_r, sibling)
    dv_sent = message(ref.dvb, ref.dv_r, sibling)
    for copy in (dq_sent, dk_sent, dv_sent):
        copy.start()

    def gain_rows(i, total):
        at = pl.ds(pl.multiple_of(i * 32, 32), 32)
        u = ref.united[at, :]
        return total + jnp.sum(ref.part2[at, :] * u * rms_scale(u), axis=0, keepdims=True)

    attn_gain_grad = lax.fori_loop(0, rows // 32, gain_rows, jnp.zeros((1, dim), f32))

    def unwindow(piece, c):
        grown = jnp.concatenate([piece, jnp.zeros((heads, WIDE - 384), f32)], axis=1)
        return pltpu.roll(grown, (c + 256) % WIDE, 1)

    total = jnp.zeros((heads, WIDE), f32)
    for kb in range(blocks):
        total += unwindow(ref.diag[kb], -64 * kb)
        piece = ref.diag[blocks + kb]
        a0, a1 = (unwindow(piece, c - 64 * kb) for c in apart[kb])
        b0, b1 = (unwindow(piece, c - 64 * kb) for c in along[kb])
        total += jnp.where(mod == 0, jnp.where(long_first, a0, a1), jnp.where(long_first, b0, b1))
    bias_grad = lax.dot_general(
        total[:, :SPANS], ref.hot[...], (((1,), (1,)), ((), ())), precision=lax.Precision.HIGHEST, preferred_element_type=f32
    )
    quarter = dim // 4
    for i, line in enumerate((attn_gain_grad, ffn_gain_grad)):
        for k in range(4):
            ref.small[4 * i + k : 4 * i + k + 1, :quarter] = line[:, k * quarter : (k + 1) * quarter]
    ref.small[:, quarter:] = jnp.zeros((8, 128), f32)
    ref.small[:heads, quarter : quarter + NB] = bias_grad
    small_mp = [message(ref.small, ref.small_p.at[o - 1], (mod, seq, peer_of(o))) for o in range(1, n_mp)]
    for copy in small_mp:
        copy.start()

    for copy in (na_sent, dq_sent, dk_sent, dv_sent):
        copy.wait_recv()
    product(w_qkv, x_na, [(ref.dqb, ref.dq_r), (ref.dkb, ref.dk_r), (ref.dvb, ref.dv_r)])
    hop(w_qkv, 0)
    hop(w_down, 1)
    hop(w_proj, 1)
    hop(w_gate, 1)
    for copy in small_mp:
        copy.wait_recv()
    gains = ref.small[:, :quarter]
    for o in range(1, n_mp):
        gains += ref.small_p[o - 1, :, :quarter]
    ref.small2[:, :quarter] = gains
    ref.small2[:, quarter:] = ref.small[:, quarter:]
    small_mod = message(ref.small2, ref.small_m, sibling)
    small_mod.start()

    normed_grad = summed(3, attn_in)
    u = ref.united[mine, :]
    scale = rms_scale(u)
    spread = normed_grad * attn_gain
    united_grad = (
        ref.mgrad[...]
        + scale * spread
        - u * (scale * scale * scale) * jnp.mean(spread * u, axis=-1, keepdims=True)
    )
    ref.whole[3, mine, :] = united_grad.astype(bf16)
    united_parts = gather(3)
    small_mod.wait_recv()
    ref.small3[...] = ref.small2[...] + ref.small_m[...]
    small_seq = [
        message(ref.small3, ref.small_q.at[o - 1], (mod, (seq + o) % n_seq, mp)) for o in range(1, n_seq)
    ]
    for copy in small_seq:
        copy.start()
    hop(w_up, 1)
    hop(w_qkv, 1)
    for step in range(2, n_seq - 1):
        for w in weights:
            hop(w, step)

    backs = []
    for o in range(n_mp):
        who = mp if o == 0 else source_of(o)
        at = pl.ds(pl.multiple_of(who * own_rows, own_rows), own_rows)
        if o:
            united_parts[o - 1].wait_recv()
        back = message(ref.whole.at[3, at], ref.text_o.at[at], sibling, mod == 1)

        @pl.when(mod == 1)
        def _(back=back):
            back.start()

        backs.append(back)
    for copy in output_parts:
        copy.wait_recv()
    ref.out_o[...] = ref.whole[2]
    ref.own_o[...] = ref.whole[3]
    for w in weights:
        arrive(w)

    total = ref.small3[...]
    for i, copy in enumerate(small_seq):
        copy.wait_recv()
        total += ref.small_q[i]
    ref.small_o[...] = total

    @pl.when(mod == 0)
    def _():
        for back in backs:
            back.wait_recv()

    @pl.when(mod == 1)
    def _():
        ref.text_o[...] = jnp.zeros((rows, dim), bf16)

    for cond, copy in sends:
        if cond is None:
            copy.wait_send()
        else:

            @pl.when(cond)
            def _(copy=copy):
                copy.wait_send()

    assert used[0] <= ref.ssem.shape[0]


def finish(n_seq, heads, width, ids, valid, own, text, out, gd, gg, gu, go, gqkv, small,
           o_out, o_in, o_ag, o_q, o_k, o_v, o_o, o_pb, o_fg, o_gate, o_up, o_down, hold):
    mod, seq = lax.axis_index("mod"), lax.axis_index("seq")
    rows, dim = own.shape
    place = mod * n_seq + seq
    o_out[0] = out[...]

    @pl.when(mod == 0)
    def _():
        count = patch_counts(ids[...], valid[...], rows)
        o_in[0] = own[...].astype(f32) + nn(count.astype(bf16), text[...])

    @pl.when(mod == 1)
    def _():
        o_in[0] = own[...].astype(f32)

    o_q[...] = gqkv[:, :width]
    o_k[...] = gqkv[:, width : 2 * width]
    o_v[...] = gqkv[:, 2 * width :]
    o_o[...] = go[...].T
    o_gate[...] = gg[...].T
    o_up[...] = gu[...].T
    o_down[...] = gd[...].T
    quarter = dim // 4
    part = dim // (2 * n_seq)
    for i, o_gain in enumerate((o_ag, o_fg)):
        line = jnp.concatenate([small[4 * i + k : 4 * i + k + 1, :quarter] for k in range(4)], axis=1)
        line = pltpu.roll(jnp.broadcast_to(line, (8, dim)), dim - place * part, 1)
        o_gain[...] = line[:1, :part]
    few = NB // (2 * n_seq)
    hold[...] = small[:, quarter:].T
    o_pb[...] = hold[pl.ds(place * few, few), :heads]


def per_device(n_seq, n_mp, *args):
    (inputs, text_patches, patch_valid, text_lengths, bucket_table, attn_gain, query_weight, key_weight,
     value_weight, output_weight, position_bias, ffn_gain, gate_weight, up_weight, down_weight, cotangent) = args
    rows, dim = inputs.shape[1:]
    heads = position_bias.shape[1]
    width = heads * HEAD
    ff = down_weight.shape[0]
    own_rows = rows // n_mp
    half = dim // 2
    block = half // n_seq
    text_patches, patch_valid, position_bias = text_patches.T, patch_valid.T, position_bias.T
    gate_weight, up_weight = gate_weight.T, up_weight.T
    ids = jnp.pad(bucket_table, (0, SPANS - bucket_table.shape[0])).reshape(SPANS // 128, 128)
    given = dict(
        len_s=text_lengths, inp_h=inputs, tp_h=text_patches, pv_h=patch_valid, ids_h=ids, pb_h=position_bias,
        ag_h=attn_gain.reshape(dim // 128, 128), fg_h=ffn_gain.reshape(dim // 128, 128), wq_h=query_weight, wk_h=key_weight,
        wv_h=value_weight, wo_h=output_weight, wg_h=gate_weight, wu_h=up_weight, wd_h=down_weight, cot_h=cotangent,
    )
    sizes = sizes_of(heads, ff)
    results = dict(
        wout=[((block, size), f32) for size in sizes], out_o=((rows, dim), bf16), own_o=((rows, dim), bf16),
        text_o=((rows, dim), bf16), small_o=((8, dim // 4 + 128), f32),
    )
    small = ((8, dim // 4 + 128), f32)
    sent = [((half, size), bf16) for size in sizes]
    held = dict(
        inp=((rows, dim), bf16), ids=(ids.shape, jnp.int32), hot=((NB, SPANS), f32), pb=((heads, NB), f32), tp=(text_patches.shape, jnp.int32),
        pv=(patch_valid.shape, jnp.int32), ag=((dim // 128, 128), bf16), fg=((dim // 128, 128), bf16), wq=((dim, width), bf16),
        wk=((dim, width), bf16), wv=((dim, width), bf16), wo=((width, dim), bf16), wg=((ff, dim), bf16),
        wu=((ff, dim), bf16), wd=((ff, dim), bf16), cot=((rows, dim), bf16), inc=((rows, dim), bf16),
        win=((2 * rows // 64, heads, 384), f32), diag=((2 * rows // 64, heads, 384), f32),
        bias=((heads, 2 * rows, rows), f32), prob=((heads, 2 * rows, rows), f32), xt=((6, half, rows), bf16), xs=((6, half, rows), bf16), xr=((6, half, rows), bf16),
        united=((rows, dim), f32), na=((rows, dim), bf16),
        kv=((rows, 2 * width), bf16), kvr=((rows, 2 * width), bf16), kvt=((2 * width, 2 * rows), bf16),
        q=((rows, width), bf16), qm=((heads, rows, width), bf16), att_t=((width, rows), f32), att=((rows, width), bf16),
        att_r=((rows, width), bf16), part2=((rows, dim), f32), stage=((4, rows, dim), bf16),
        land=((4, n_mp - 1, own_rows, dim), bf16), keep=((4, own_rows, dim), f32), whole=((4, rows, dim), bf16),
        cot_e=((rows, dim), bf16), nf_e=((rows, dim), bf16), hg_e=((rows, ff), f32), hid_e=((rows, ff), bf16),
        hid_er=((rows, ff), bf16), gg_e=((rows, ff), bf16), gg_er=((rows, ff), bf16), ug_e=((rows, ff), bf16),
        ug_er=((rows, ff), bf16), hg=((rows, ff), f32), mid=((own_rows, dim), f32), mgrad=((own_rows, dim), f32), gate=((rows, ff), f32),
        up=((rows, ff), f32), ga=((rows, width), bf16), turn=((rows, rows), bf16), dk=((2 * rows, width), f32),
        dv=((2 * rows, width), f32), dq_t=((width, rows), f32), kvg_s=((rows, 2 * width), bf16),
        kvg_r=((rows, 2 * width), bf16),
    )
    held.update(
        hid=((rows, ff), bf16), hid_r=((rows, ff), bf16), gg=((rows, ff), bf16), gg_r=((rows, ff), bf16),
        ug=((rows, ff), bf16), ug_r=((rows, ff), bf16), dqb=((rows, width), bf16), dq_r=((rows, width), bf16),
        dkb=((rows, width), bf16), dk_r=((rows, width), bf16), dvb=((rows, width), bf16), dv_r=((rows, width), bf16),
        wgrad=[((half, size), f32) for size in sizes], wsend=sent, wleft=sent, wright=sent, small=small, small2=small,
        small3=small, small_m=small, small_q=((n_seq - 1,) + small[0], f32),
        small_p=((n_mp - 1,) + small[0], f32),
    )
    count = 40 + 9 * n_mp + 10 * n_seq
    order = [(name, 0) for name in given]
    out_shape, scratch = [], []
    for specs, into, make in ((results, out_shape, jax.ShapeDtypeStruct), (held, scratch, pltpu.VMEM)):
        for name, spec in specs.items():
            many = spec if isinstance(spec, list) else [spec]
            order.append((name, len(many) if isinstance(spec, list) else 0))
            into.extend(make(*one) for one in many)
    for i, size in enumerate((count, count, len(given) - 1)):
        order.append((("ssem", "rsem", "lsem")[i], 0))
        scratch.append(pltpu.SemaphoreType.DMA((size,)))
    vmem = pl.BlockSpec(memory_space=pltpu.VMEM)
    done = pl.pallas_call(
        functools.partial(mega, n_seq, n_mp, heads, order),
        out_shape=out_shape,
        in_specs=[pl.BlockSpec(memory_space=pltpu.SMEM)] + [pl.BlockSpec(memory_space=pl.ANY)] * (len(given) - 1),
        out_specs=[vmem] * len(out_shape),
        scratch_shapes=scratch,
        compiler_params=pltpu.CompilerParams(
            collective_id=0, has_side_effects=True, vmem_limit_bytes=63 * 2**20
        ),
        name="layer",
    )(*given.values())
    *wout, out, own, text, small_sum = done
    down_sum, gate_sum, up_sum, proj_sum, qkv_sum = wout
    part = dim // (2 * n_seq)
    few = NB // (2 * n_seq)
    shapes = [
        ((1, rows, dim), bf16), ((1, rows, dim), f32), ((1, part), f32), ((block, width), f32), ((block, width), f32),
        ((block, width), f32), ((width, block), f32), ((few, heads), f32), ((1, part), f32), ((ff, block), f32),
        ((ff, block), f32), ((ff, block), f32),
    ]
    outs = pl.pallas_call(
        functools.partial(finish, n_seq, heads, width),
        out_shape=[jax.ShapeDtypeStruct(*spec) for spec in shapes],
        in_specs=[vmem] * 11,
        out_specs=[vmem] * 12,
        scratch_shapes=[pltpu.VMEM((128, 8), f32)],
        compiler_params=pltpu.CompilerParams(vmem_limit_bytes=63 * 2**20),
        name="finish",
    )(
        text_patches, patch_valid, own, text, out, down_sum, gate_sum, up_sum, proj_sum, qkv_sum, small_sum
    )
    outs = list(outs)
    for i in (9, 10):
        outs[i] = outs[i].T
    outs[2] = outs[2].reshape(part)
    outs[8] = outs[8].reshape(part)
    return tuple(outs)


def solution(mesh):
    group = ("mod", "seq")
    in_specs = (
        P("mod", "seq", None), P("seq", None), P("seq", None), P("seq", None), P(), P(), P(None, "mp"), P(None, "mp"),
        P(None, "mp"), P("mp", None), P(None, "mp"), P(), P(None, "mp"), P(None, "mp"), P("mp", None),
        P("mod", "seq", None),
    )
    out_specs = (
        P("mod", "seq", None), P("mod", "seq", None), P(group), P(group, "mp"), P(group, "mp"), P(group, "mp"),
        P("mp", group), P(group, "mp"), P(group), P(group, "mp"), P(group, "mp"), P("mp", group),
    )
    body = functools.partial(per_device, mesh.shape["seq"], mesh.shape["mp"])
    return jax.shard_map(body, mesh=mesh, in_specs=in_specs, out_specs=out_specs, check_vma=False)
```

```python
import functools
import types

import jax
import jax.numpy as jnp
from jax import lax
from jax.experimental import pallas as pl
from jax.experimental.pallas import tpu as pltpu
from jax.sharding import PartitionSpec as P

MESH = pl.DeviceIdType.MESH
EPS = 1e-06
PARTS = 2
ROOT = 0.7978845608028654
HEAD = 64
NB = 32
PDOC = 128
LONG = 192
SPANS = 640
WIDE = 896
f32 = jnp.float32
bf16 = jnp.bfloat16


def nn(a, b):
    return jnp.dot(a, b, preferred_element_type=f32)


def nt(a, b):
    return lax.dot_general(a, b, (((1,), (1,)), ((), ())), preferred_element_type=f32)


def rms_scale(x):
    return lax.rsqrt(jnp.mean(x * x, axis=-1, keepdims=True) + EPS)


def row_chunks(first, total, step, body):
    def one(i, carry):
        body(pl.ds(pl.multiple_of(first + i * step, step), step))
        return carry

    lax.fori_loop(0, total // step, one, 0)


def bucket_hot(ids_row):
    return (lax.broadcasted_iota(jnp.int32, (NB, SPANS), 0) == ids_row).astype(f32)


def patch_counts(ids, valid, rows):
    places = lax.broadcasted_iota(jnp.int32, (rows, rows), 0)
    count = jnp.zeros((rows, rows), f32)
    for j in range(ids.shape[0]):
        count += jnp.where(ids[j : j + 1, :] == places, valid[j : j + 1, :].astype(f32), 0.0)
    return count


def flat(ref):
    value = ref[...].astype(f32)
    return jnp.concatenate([value[i : i + 1, :] for i in range(value.shape[0])], axis=1)


def sizes_of(heads, ff):
    width = heads * HEAD
    return (ff, ff, ff, width, width, width, width)


def mega(n_seq, n_mp, heads, order, *refs):
    ref, refs = types.SimpleNamespace(), list(refs)
    for name, many in order:
        setattr(ref, name, [refs.pop(0) for _ in range(many)] if many else refs.pop(0))
    mod, seq, mp = lax.axis_index("mod"), lax.axis_index("seq"), lax.axis_index("mp")
    rows, dim = ref.united.shape
    width = heads * HEAD
    ff = ref.wg.shape[0]
    half = dim // 2
    block = half // n_seq
    part_rows = rows // PARTS
    own_rows = part_rows // n_mp
    parts = range(PARTS)

    def part(k):
        return slice(k * part_rows, (k + 1) * part_rows)

    def share(k, who):
        return pl.ds(pl.multiple_of(k * part_rows + who * own_rows, own_rows), own_rows)

    def kept(k):
        return slice(k * own_rows, (k + 1) * own_rows)

    here = pl.ds(pl.multiple_of(mod * half, half), half)
    there = pl.ds(pl.multiple_of((1 - mod) * half, half), half)
    sibling = (1 - mod, seq, mp)
    used = [0]
    sends = []
    is_end = (seq == 0) | (seq == n_seq - 1)
    not_end = (seq > 0) & (seq < n_seq - 1)
    is_inner = (seq == 1) | (seq == n_seq - 2)
    inner = (mod, seq + 1 - 2 * (seq // (n_seq - 1)), mp)

    def when(cond, body):
        if cond is None:
            body()
        else:
            pl.when(cond)(body)

    def peer_of(o):
        if n_mp == 4:
            return (mp + 1 - 2 * (mp % 2), (mp + 2) % 4, 3 - mp)[o - 1]
        return (mp + o) % n_mp

    def source_of(o):
        if n_mp == 4:
            return peer_of(o)
        return (mp + n_mp - o) % n_mp

    def message(src, dst, device, cond=None):
        index = used[0]
        used[0] += 1
        copy = pltpu.make_async_remote_copy(
            src_ref=src,
            dst_ref=dst,
            send_sem=ref.ssem.at[index],
            recv_sem=ref.rsem.at[index],
            device_id=device,
            device_id_type=MESH,
        )
        sends.append((cond, copy))
        return copy

    loads = types.SimpleNamespace()
    pairs = (
        (ref.inp_h.at[0], ref.inp), (ref.ids_h, ref.ids), (ref.pb_h, ref.pb), (ref.tp_h, ref.tp), (ref.pv_h, ref.pv),
        (ref.ag_h, ref.ag), (ref.wk_h, ref.wk), (ref.wv_h, ref.wv), (ref.wq_h, ref.wq), (ref.cot_h.at[0], ref.cot),
        (ref.wo_h, ref.wo), (ref.wd_h, ref.wd), (ref.fg_h, ref.fg), (ref.wg_h, ref.wg), (ref.wu_h, ref.wu),
    )
    copies = [pltpu.make_async_copy(src, dst, ref.lsem.at[i]) for i, (src, dst) in enumerate(pairs)]
    for copy in copies:
        copy.start()
    (loads.inp, loads.ids, loads.pb, loads.tp, loads.pv, loads.ag, loads.wk, loads.wv, loads.wq, loads.cot, loads.wo,
     loads.wd, loads.fg, loads.wg, loads.wu) = copies

    barrier = pltpu.get_barrier_semaphore()
    pl.semaphore_signal(barrier, 1, device_id=sibling, device_id_type=MESH)
    for o in range(1, n_mp):
        pl.semaphore_signal(barrier, 1, device_id=(mod, seq, peer_of(o)), device_id_type=MESH)

    for o in range(1, n_seq):
        pl.semaphore_signal(barrier, 1, device_id=(mod, (seq + o) % n_seq, mp), device_id_type=MESH)
    pl.semaphore_wait(barrier, n_mp + n_seq - 1)

    to_text = message(ref.inp_h.at[0], ref.inc, sibling, mod == 0)

    @pl.when(mod == 0)
    def _():
        to_text.start()

    cot_end = message(ref.cot_h.at[0], ref.cot_e, inner, is_end)
    when(is_end, cot_end.start)

    first = ref.len_s[0, 0]
    long_first = first == LONG
    loads.ids.wait()
    loads.pb.wait()
    mirror = (
        lax.broadcasted_iota(jnp.int32, (128, 128), 0) + lax.broadcasted_iota(jnp.int32, (128, 128), 1) == 127
    ).astype(f32)
    turned_ids = nn(ref.ids[...].astype(f32).astype(bf16), mirror.astype(bf16))
    lines = turned_ids.shape[0]
    turned_ids = jnp.concatenate([turned_ids[i : i + 1, :] for i in reversed(range(lines))], axis=1)
    hot = bucket_hot(turned_ids.astype(jnp.int32))
    ref.hot[...] = hot
    rel = jnp.dot(ref.pb[...], hot, precision=lax.Precision.HIGHEST, preferred_element_type=f32)
    rel = jnp.concatenate([rel, jnp.zeros((heads, WIDE - SPANS), f32)], axis=1)
    blocks = rows // 64
    apart = ((-128, -128), (-128, -192), (-128, -192), (-64, -192))
    along = ((128, 128), (128, 128), (64, 192), (64, 192))

    def window(c):
        return pltpu.roll(rel, (WIDE - (c + 256)) % WIDE, 1)[:, :384]

    lane_row = lax.broadcasted_iota(jnp.int32, (1, rows), 1)
    patch_doc = lane_row // PDOC
    text_doc = (lane_row >= first).astype(jnp.int32)
    query_doc = jnp.where(mod == 0, patch_doc, text_doc)
    for kb in range(blocks):
        ref.win[kb] = window(-64 * kb)
        a0, a1 = (window(c - 64 * kb) for c in apart[kb])
        b0, b1 = (window(c - 64 * kb) for c in along[kb])
        ref.win[blocks + kb] = jnp.where(
            mod == 0, jnp.where(long_first, a0, a1), jnp.where(long_first, b0, b1)
        )
    for kb in range(2 * blocks):
        at = kb % blocks
        in_patch = (mod == 0) if kb < blocks else (mod == 1)
        key_doc = jnp.where(in_patch, at * 64 // PDOC, jnp.where(at * 64 >= first, 1, 0))
        same = query_doc == key_doc

        def one_bias(h, carry, kb=kb, same=same):
            line = jnp.broadcast_to(ref.win[kb, pl.ds(h, 1), :], (64, 384))
            table = pltpu.roll(line, 320, 1, stride=1, stride_axis=0)[:, :rows]
            ref.prob[h, kb * 64 : kb * 64 + 64, :] = jnp.where(same, table, -1000000000.0)
            return carry

        lax.fori_loop(0, heads, one_bias, 0)

    loads.cot.wait()

    def transposed(source, sides, cond=None):
        copy = message(sides.s, sides.r, sibling, cond)

        def body():
            sides.s[...] = source[:, there].T
            copy.start()
            sides.t[...] = source[:, here].T

        when(cond, body)
        return copy

    x_tan, x_na, x_nf, x_branch, x_tan_e, x_nf_e = (
        types.SimpleNamespace(t=ref.xt.at[i], s=ref.xs.at[i], r=ref.xr.at[i]) for i in range(6)
    )
    tan_sent = transposed(ref.cot, x_tan, not_end)

    loads.tp.wait()
    loads.pv.wait()
    loads.inp.wait()

    @pl.when(mod == 1)
    def _():
        count = patch_counts(ref.tp[...], ref.pv[...], rows).T.astype(bf16)
        to_text.wait_recv()
        ref.united[...] = nn(count, ref.inc[...])

    @pl.when(mod == 0)
    def _():
        ref.united[...] = jnp.zeros((rows, dim), f32)

    loads.ag.wait()
    attn_gain = flat(ref.ag)

    def first_norm(at):
        u = ref.united[at, :] + ref.inp[at, :].astype(f32)
        ref.united[at, :] = u
        ref.na[at, :] = (u * rms_scale(u) * attn_gain).astype(bf16)

    row_chunks(0, rows, 32, first_norm)
    loads.wk.wait()
    ref.kv[:, :width] = nn(ref.na[...], ref.wk[...]).astype(bf16)
    loads.wv.wait()
    ref.kv[:, width:] = nn(ref.na[...], ref.wv[...]).astype(bf16)
    kv_sent = message(ref.kv, ref.kvr, sibling)
    kv_sent.start()
    loads.wq.wait()
    ref.q[...] = nn(ref.na[...], ref.wq[...]).astype(bf16)
    ref.kvt[:, :rows] = ref.kv[...].T
    na_sent = transposed(ref.na, x_na)
    kv_sent.wait_recv()
    ref.kvt[:, rows:] = ref.kvr[...].T
    head_of = lax.broadcasted_iota(jnp.int32, (1, width), 1) // HEAD

    def head_mask(h):
        return (head_of == h).astype(f32).astype(bf16)

    def head_rows(h, base=0):
        return pl.ds(pl.multiple_of(base + h * HEAD, HEAD), HEAD)

    def head_fwd(k, h, carry):
        at = part(k)
        qm = ref.q[at, :] * head_mask(h)
        ref.qm[h, at, :] = qm
        s0 = nt(ref.kv[:, :width], qm) * 0.125 + ref.prob[h, :rows, at]
        s1 = nt(ref.kvr[:, :width], qm) * 0.125 + ref.prob[h, rows:, at]
        top = jnp.maximum(jnp.max(s0, axis=0, keepdims=True), jnp.max(s1, axis=0, keepdims=True))
        e0 = jnp.exp(s0 - top)
        e1 = jnp.exp(s1 - top)
        total = jnp.sum(e0, axis=0, keepdims=True) + jnp.sum(e1, axis=0, keepdims=True)
        scale = 1.0 / total
        p0 = e0 * scale
        p1 = e1 * scale
        ref.prob[h, :rows, at] = p0
        ref.prob[h, rows:, at] = p1
        values_t = ref.kvt[head_rows(h, width), :]
        ref.att_t[head_rows(h), at] = nn(values_t[:, :rows], p0.astype(bf16)) + nn(
            values_t[:, rows:], p1.astype(bf16)
        )
        return carry

    def scatter(c, k, product, hold=False):
        ref.part[part(k), :] = product
        ref.stage[c, part(k), :] = product.astype(bf16)
        copies = []
        for o in range(n_mp - 1, 0, -1):
            to = peer_of(o)
            copies.append(message(ref.stage.at[c, share(k, to)], ref.land.at[c, k, o - 1], (mod, seq, to)))
            if not hold:
                copies[-1].start()
        ref.keep[c, kept(k), :] = ref.part[share(k, mp), :]
        return copies

    def summed(c, k, copies):
        for copy in copies:
            copy.wait_recv()
        total = ref.keep[c, kept(k), :]
        for o in range(1, n_mp):
            total += ref.land[c, k, o - 1].astype(f32)
        return total

    def gather(c, k):
        at = ref.whole.at[c, share(k, mp)]
        copies = [message(at, at, (mod, seq, peer_of(o))) for o in range(1, n_mp)]
        for copy in reversed(copies):
            copy.start()
        return copies

    loads.wo.wait()
    attn_sum = []
    for k in parts:
        lax.fori_loop(0, heads, functools.partial(head_fwd, k), 0)
        ref.att[part(k), :] = ref.att_t[:, part(k)].T.astype(bf16)
        attn_sum.append(scatter(0, k, nn(ref.att[part(k), :], ref.wo[...])))
    att_sent = message(ref.att, ref.att_r, sibling)
    att_sent.start()
    loads.wd.wait()
    ref.hg[...] = nt(ref.cot[...], ref.wd[...])
    loads.fg.wait()
    ffn_gain = flat(ref.fg)
    nf_end = []

    def to_inner(k, who):
        at = share(k, who)
        copy = message(ref.whole.at[0, at], ref.nf_e.at[at], inner, is_end)
        when(is_end, copy.start)
        nf_end.append(copy)

    nf_parts = []
    for k in parts:
        middle = ref.united[share(k, mp), :] + summed(0, k, attn_sum[k])
        ref.mid[kept(k), :] = middle
        ref.whole[0, share(k, mp), :] = (middle * rms_scale(middle) * ffn_gain).astype(bf16)
        nf_parts.append(gather(0, k))
        to_inner(k, mp)
    tan_e_sent = message(x_tan_e.s, x_tan_e.r, sibling, is_inner)

    @pl.when(is_inner)
    def _():
        cot_end.wait_recv()
        x_tan_e.s[...] = ref.cot_e[:, there].T
        tan_e_sent.start()
        x_tan_e.t[...] = ref.cot_e[:, here].T
        ref.hg_e[...] = nt(ref.cot_e[...], ref.wd[...])

    loads.wg.wait()
    loads.wu.wait()

    def gelu_rows(at, back_ref=ref.hg, hid=ref.hid, gg=ref.gg, ug=ref.ug):
        g, u, back = ref.gate[at, :], ref.up[at, :], back_ref[at, :]
        squared = g * g
        t = jnp.tanh(ROOT * (g + 0.044715 * squared * g))
        left = 0.5 * (1.0 + t)
        gelu = left * g
        slope = left + 0.5 * g * (1.0 - t * t) * (ROOT * (1.0 + 0.134145 * squared))
        hid[at, :] = (gelu * u).astype(bf16)
        gg[at, :] = (back * u * slope).astype(bf16)
        ug[at, :] = (back * gelu).astype(bf16)

    ffn_in = []
    for k in parts:
        for o, copy in enumerate(nf_parts[k], 1):
            copy.wait_recv()
            to_inner(k, source_of(o))
        at = part(k)
        ref.gate[at, :] = nt(ref.whole[0, at, :], ref.wg[...])
        ref.up[at, :] = nt(ref.whole[0, at, :], ref.wu[...])
        row_chunks(k * part_rows, part_rows, 32, gelu_rows)
        ffn_in.append(scatter(1, k, nn(ref.gg[at, :], ref.wg[...]) + nn(ref.ug[at, :], ref.wu[...])))
    hid_sent = message(ref.hid, ref.hid_r, sibling, not_end)
    gg_sent = message(ref.gg, ref.gg_r, sibling, not_end)
    ug_sent = message(ref.ug, ref.ug_r, sibling, not_end)
    when(not_end, hid_sent.start)
    nf_sent = transposed(ref.whole.at[0], x_nf, not_end)
    when(not_end, gg_sent.start)
    when(not_end, ug_sent.start)

    after = (mod, jnp.minimum(seq + 1, n_seq - 1), mp)
    before = (mod, jnp.maximum(seq - 1, 0), mp)
    weights = []
    ends = (1, 1, 1, 0, 0, 0, 0)
    for e, g, s, a, b, o in zip(ends, ref.wgrad, ref.wsend, ref.wleft, ref.wright, ref.wout, strict=True):
        right, left = {}, {}
        for j in range(n_seq):
            rng = pl.ds(j * block, block)
            if j > e:
                right[j] = message(s.at[rng], a.at[rng], after, (seq >= e) & (seq < j))
            if j < n_seq - 1 - e:
                left[j] = message(s.at[rng], b.at[rng], before, (seq < n_seq - e) & (seq > j))
        weights.append(types.SimpleNamespace(e=e, g=g, s=s, a=a, b=b, o=o, right=right, left=left))
    w_down, w_gate, w_up, w_proj, w_q, w_k, w_v = weights

    def product(w, x, pieces, more=False):
        lo = 0
        for own, other in pieces:
            size = own.shape[1]
            both = nn(x.t[...], own[...]) + nn(x.r[...], other[...])
            if more:
                both += w.g[:, lo : lo + size]
            w.g[:, lo : lo + size] = both
            lo += size

    def hop(group, step, some=slice(None)):
        edge = group[0].e + step
        if edge >= n_seq - 1:
            return

        @pl.when(seq == edge)
        def _():
            for j in list(range(n_seq - 1, edge, -1))[some]:
                rng = slice(j * block, (j + 1) * block)
                for w in group:
                    value = w.g[rng, :]
                    if step > 0:
                        w.right[j].wait_recv()
                        value += w.a[rng, :].astype(f32)
                    w.s[rng, :] = value.astype(bf16)
                    w.right[j].start()

        @pl.when(seq == n_seq - 1 - edge)
        def _():
            for j in list(range(n_seq - 1 - edge))[some]:
                rng = slice(j * block, (j + 1) * block)
                for w in group:
                    value = w.g[rng, :]
                    if step > 0:
                        w.left[j].wait_recv()
                        value += w.b[rng, :].astype(f32)
                    w.s[rng, :] = value.astype(bf16)
                    w.left[j].start()

    def arrive(w):
        for j in range(n_seq):

            @pl.when(seq == j)
            def _(j=j):
                rng = slice(j * block, (j + 1) * block)
                value = w.g[rng, :] if w.e <= j < n_seq - w.e else jnp.zeros(w.o.shape, f32)
                if j > w.e:
                    w.right[j].wait_recv()
                    value += w.a[rng, :].astype(f32)
                if j < n_seq - 1 - w.e:
                    w.left[j].wait_recv()
                    value += w.b[rng, :].astype(f32)
                w.o[...] = value

    gain_sums = []
    branch_parts = []

    def middle_back(k):
        normed_grad = summed(1, k, ffn_in[k])
        middle = ref.mid[kept(k), :]
        scale = rms_scale(middle)
        spread = normed_grad * ffn_gain
        gain_sums.append(jnp.sum(normed_grad * middle * scale, axis=0, keepdims=True))
        middle_grad = (
            ref.cot[share(k, mp), :].astype(f32)
            + scale * spread
            - middle * (scale * scale * scale) * jnp.mean(spread * middle, axis=-1, keepdims=True)
        )
        ref.mgrad[kept(k), :] = middle_grad
        ref.whole[1, share(k, mp), :] = middle_grad.astype(bf16)
        branch_parts.append(gather(1, k))

    hid_e_sent = message(ref.hid_e, ref.hid_er, sibling, is_inner)
    gg_e_sent = message(ref.gg_e, ref.gg_er, sibling, is_inner)
    ug_e_sent = message(ref.ug_e, ref.ug_er, sibling, is_inner)
    nf_e_sent = message(x_nf_e.s, x_nf_e.r, sibling, is_inner)

    @pl.when(not_end)
    def _():
        hid_sent.wait_recv()
        tan_sent.wait_recv()
        product(w_down, x_tan, [(ref.hid, ref.hid_r)])
        nf_sent.wait_recv()
        gg_sent.wait_recv()
        product(w_gate, x_nf, [(ref.gg, ref.gg_r)])
        ug_sent.wait_recv()
        product(w_up, x_nf, [(ref.ug, ref.ug_r)])

    for k in parts:
        middle_back(k)

    @pl.when(is_inner)
    def _():
        for copy in nf_end:
            copy.wait_recv()
        ref.gate[...] = nt(ref.nf_e[...], ref.wg[...])
        ref.up[...] = nt(ref.nf_e[...], ref.wu[...])
        row_chunks(0, rows, 32, lambda at: gelu_rows(at, ref.hg_e, ref.hid_e, ref.gg_e, ref.ug_e))
        hid_e_sent.start()
        x_nf_e.s[...] = ref.nf_e[:, there].T
        nf_e_sent.start()
        gg_e_sent.start()
        ug_e_sent.start()
        x_nf_e.t[...] = ref.nf_e[:, here].T


    def end_products(w, x, pieces, needs):
        @pl.when(is_inner)
        def _():
            for copy in needs:
                copy.wait_recv()
            product(w, x, pieces, more=True)

        hop([w], 0, slice(0, 1))

    ffn_out = [scatter(2, k, nn(ref.hid[part(k), :], ref.wd[...]), hold=True) for k in parts]
    end_products(w_down, x_tan_e, [(ref.hid_e, ref.hid_er)], (hid_e_sent, tan_e_sent))
    end_products(w_gate, x_nf_e, [(ref.gg_e, ref.gg_er)], (gg_e_sent, nf_e_sent))
    end_products(w_up, x_nf_e, [(ref.ug_e, ref.ug_er)], (ug_e_sent,))
    hop([w_down, w_gate, w_up], 0, slice(1, None))

    flip = (
        lax.broadcasted_iota(jnp.int32, (rows, rows), 0) // 64 == lax.broadcasted_iota(jnp.int32, (rows, rows), 1) // 64
    ) & (
        lax.broadcasted_iota(jnp.int32, (rows, rows), 0) % 64
        + lax.broadcasted_iota(jnp.int32, (rows, rows), 1) % 64
        == 63
    )
    ref.turn[...] = flip.astype(f32).astype(bf16)
    ref.dk[...] = jnp.zeros((2 * rows, width), f32)
    ref.dv[...] = jnp.zeros((2 * rows, width), f32)

    def head_bwd(k, h, carry):
        a = part(k)
        gm = ref.ga[a, :] * head_mask(h)
        p0, p1 = ref.prob[h, :rows, a], ref.prob[h, rows:, a]
        d0 = nt(ref.kv[:, width:], gm)
        d1 = nt(ref.kvr[:, width:], gm)
        inner_sum = jnp.sum(p0 * d0, axis=0, keepdims=True) + jnp.sum(p1 * d1, axis=0, keepdims=True)
        g0 = (p0 * (d0 - inner_sum)).astype(bf16)
        g1 = (p1 * (d1 - inner_sum)).astype(bf16)
        keys_t = ref.kvt[head_rows(h), :]
        ref.dq_t[head_rows(h), a] = nn(keys_t[:, :rows], g0) + nn(keys_t[:, rows:], g1)
        qm = ref.qm[h, a, :]
        ref.dk[:rows, :] += nn(g0, qm)
        ref.dk[rows:, :] += nn(g1, qm)
        ref.dv[:rows, :] += nn(p0.astype(bf16), gm)
        ref.dv[rows:, :] += nn(p1.astype(bf16), gm)
        turn = ref.turn[...]
        low, wide = k * part_rows, part_rows + 128
        for side, g in ((0, g0), (1, g1)):
            turned = nn(turn, g)
            for at in range(blocks):
                piece = turned[at * 64 : at * 64 + 64, :]
                piece = jnp.concatenate([piece, jnp.zeros((64, 128), f32)], axis=1)
                piece = pltpu.roll(piece, 1, 1, stride=1, stride_axis=0)
                ref.diag[side * blocks + at, pl.ds(h, 1), low : low + wide] += jnp.sum(piece, axis=0, keepdims=True)
        return carry

    ref.diag[...] = jnp.zeros(ref.diag.shape, f32)
    for k in parts:
        for copy in branch_parts[k]:
            copy.wait_recv()
        ref.ga[part(k), :] = nt(ref.whole[1, part(k), :], ref.wo[...]).astype(bf16)
        if k == PARTS - 1:
            for copies in ffn_out:
                for copy in copies:
                    copy.start()
        lax.fori_loop(0, heads, functools.partial(head_bwd, k), 0)
    branch_sent = transposed(ref.whole.at[1], x_branch)
    ref.kvg_s[:, :width] = (ref.dk[rows:, :] * 0.125).astype(bf16)
    ref.kvg_s[:, width:] = ref.dv[rows:, :].astype(bf16)
    kvg_sent = message(ref.kvg_s, ref.kvg_r, sibling)
    kvg_sent.start()
    ref.dqb[...] = (ref.dq_t[...].T * 0.125).astype(bf16)
    dq_sent = message(ref.dqb, ref.dq_r, sibling)
    dq_sent.start()
    att_sent.wait_recv()
    branch_sent.wait_recv()
    product(w_proj, x_branch, [(ref.att, ref.att_r)])
    hop([w_proj], 0)
    hop([w_down, w_gate], 1)
    na_sent.wait_recv()
    dq_sent.wait_recv()
    product(w_q, x_na, [(ref.dqb, ref.dq_r)])
    hop([w_q], 0)
    kvg_sent.wait_recv()
    ref.dkb[...] = (ref.dk[:rows, :] * 0.125 + ref.kvg_r[:, :width].astype(f32)).astype(bf16)
    ref.dvb[...] = (ref.dv[:rows, :] + ref.kvg_r[:, width:].astype(f32)).astype(bf16)
    dk_sent = message(ref.dkb, ref.dk_r, sibling)
    dv_sent = message(ref.dvb, ref.dv_r, sibling)
    for copy in (dk_sent, dv_sent):
        copy.start()
    attn_in = []
    for k in parts:
        at = part(k)
        rows_in = nt(ref.dqb[at, :], ref.wq[...]) + nt(ref.dkb[at, :], ref.wk[...]) + nt(ref.dvb[at, :], ref.wv[...])
        attn_in.append(scatter(3, k, rows_in))
    for copy in (dk_sent, dv_sent):
        copy.wait_recv()
    product(w_k, x_na, [(ref.dkb, ref.dk_r)])
    product(w_v, x_na, [(ref.dvb, ref.dv_r)])
    hop([w_k, w_v], 0)
    hop([w_up], 1)

    def gain_rows(i, total):
        at = pl.ds(pl.multiple_of(i * 32, 32), 32)
        u = ref.united[at, :]
        return total + jnp.sum(ref.part[at, :] * u * rms_scale(u), axis=0, keepdims=True)

    attn_gain_grad = lax.fori_loop(0, rows // 32, gain_rows, jnp.zeros((1, dim), f32))

    def unwindow(piece, c):
        grown = jnp.concatenate([piece, jnp.zeros((heads, WIDE - 384), f32)], axis=1)
        return pltpu.roll(grown, (c + 256) % WIDE, 1)

    total = jnp.zeros((heads, WIDE), f32)
    for kb in range(blocks):
        total += unwindow(ref.diag[kb], -64 * kb)
        piece = ref.diag[blocks + kb]
        a0, a1 = (unwindow(piece, c - 64 * kb) for c in apart[kb])
        b0, b1 = (unwindow(piece, c - 64 * kb) for c in along[kb])
        total += jnp.where(mod == 0, jnp.where(long_first, a0, a1), jnp.where(long_first, b0, b1))
    bias_grad = lax.dot_general(
        total[:, :SPANS], ref.hot[...], (((1,), (1,)), ((), ())), precision=lax.Precision.HIGHEST, preferred_element_type=f32
    )
    quarter = dim // 4
    for i, line in enumerate((attn_gain_grad, sum(gain_sums))):
        for k in range(4):
            ref.small[4 * i + k : 4 * i + k + 1, :quarter] = line[:, k * quarter : (k + 1) * quarter]
    ref.small[:, quarter:] = jnp.zeros((8, 128), f32)
    ref.small[:heads, quarter : quarter + NB] = bias_grad
    small_mp = [message(ref.small, ref.small_p.at[o - 1], (mod, seq, peer_of(o))) for o in range(1, n_mp)]
    for copy in small_mp:
        copy.start()

    hop([w_proj, w_q], 1)
    for copy in small_mp:
        copy.wait_recv()
    gains = ref.small[:, :quarter]
    for o in range(1, n_mp):
        gains += ref.small_p[o - 1, :, :quarter]
    ref.small2[:, :quarter] = gains
    ref.small2[:, quarter:] = ref.small[:, quarter:]
    small_mod = message(ref.small2, ref.small_m, sibling)
    small_mod.start()

    united_parts = []
    for k in parts:
        normed_grad = summed(3, k, attn_in[k])
        u = ref.united[share(k, mp), :]
        scale = rms_scale(u)
        spread = normed_grad * attn_gain
        united_grad = (
            ref.mgrad[kept(k), :]
            + scale * spread
            - u * (scale * scale * scale) * jnp.mean(spread * u, axis=-1, keepdims=True)
        )
        ref.whole[3, share(k, mp), :] = united_grad.astype(bf16)
        united_parts.append(gather(3, k))
    output_parts = []
    for k in parts:
        ref.whole[2, share(k, mp), :] = (ref.mid[kept(k), :] + summed(2, k, ffn_out[k])).astype(bf16)
        output_parts.append(gather(2, k))
    hop([w_k, w_v], 1)
    small_mod.wait_recv()
    ref.small3[...] = ref.small2[...] + ref.small_m[...]
    small_seq = [
        message(ref.small3, ref.small_q.at[o - 1], (mod, (seq + o) % n_seq, mp)) for o in range(1, n_seq)
    ]
    for copy in small_seq:
        copy.start()
    backs = []
    for k in parts:
        for o in range(n_mp):
            at = share(k, source_of(o) if o else mp)
            if o:
                united_parts[k][o - 1].wait_recv()
            back = message(ref.whole.at[3, at], ref.text_o.at[at], sibling, mod == 1)
            when(mod == 1, back.start)
            backs.append(back)
    for step in range(2, n_seq - 1):
        hop([w_down, w_gate, w_up], step)
        hop([w_proj, w_q], step)
        hop([w_k, w_v], step)
    for copies in output_parts:
        for copy in copies:
            copy.wait_recv()
    ref.out_o[...] = ref.whole[2]
    ref.own_o[...] = ref.whole[3]
    for w in weights:
        arrive(w)

    total = ref.small3[...]
    for i, copy in enumerate(small_seq):
        copy.wait_recv()
        total += ref.small_q[i]
    ref.small_o[...] = total

    @pl.when(mod == 0)
    def _():
        for back in backs:
            back.wait_recv()

    @pl.when(mod == 1)
    def _():
        ref.text_o[...] = jnp.zeros((rows, dim), bf16)

    for cond, copy in sends:
        if cond is None:
            copy.wait_send()
        else:

            @pl.when(cond)
            def _(copy=copy):
                copy.wait_send()

    assert used[0] <= ref.ssem.shape[0]


def finish(n_seq, heads, width, ids, valid, own, text, out, gd, gg, gu, go, gq, gk, gv, small,
           o_out, o_in, o_ag, o_q, o_k, o_v, o_o, o_pb, o_fg, o_gate, o_up, o_down, hold):
    mod, seq = lax.axis_index("mod"), lax.axis_index("seq")
    rows, dim = own.shape
    place = mod * n_seq + seq
    o_out[0] = out[...]

    @pl.when(mod == 0)
    def _():
        count = patch_counts(ids[...], valid[...], rows)
        o_in[0] = own[...].astype(f32) + nn(count.astype(bf16), text[...])

    @pl.when(mod == 1)
    def _():
        o_in[0] = own[...].astype(f32)

    o_q[...] = gq[...]
    o_k[...] = gk[...]
    o_v[...] = gv[...]
    o_o[...] = go[...].T
    o_gate[...] = gg[...].T
    o_up[...] = gu[...].T
    o_down[...] = gd[...].T
    quarter = dim // 4
    part = dim // (2 * n_seq)
    for i, o_gain in enumerate((o_ag, o_fg)):
        line = jnp.concatenate([small[4 * i + k : 4 * i + k + 1, :quarter] for k in range(4)], axis=1)
        line = pltpu.roll(jnp.broadcast_to(line, (8, dim)), dim - place * part, 1)
        o_gain[...] = line[:1, :part]
    few = NB // (2 * n_seq)
    hold[...] = small[:, quarter:].T
    o_pb[...] = hold[pl.ds(place * few, few), :heads]


def per_device(n_seq, n_mp, *args):
    (inputs, text_patches, patch_valid, text_lengths, bucket_table, attn_gain, query_weight, key_weight,
     value_weight, output_weight, position_bias, ffn_gain, gate_weight, up_weight, down_weight, cotangent) = args
    rows, dim = inputs.shape[1:]
    heads = position_bias.shape[1]
    width = heads * HEAD
    ff = down_weight.shape[0]
    own_rows = rows // n_mp
    half = dim // 2
    block = half // n_seq
    text_patches, patch_valid, position_bias = text_patches.T, patch_valid.T, position_bias.T
    gate_weight, up_weight = gate_weight.T, up_weight.T
    ids = jnp.pad(bucket_table, (0, SPANS - bucket_table.shape[0])).reshape(SPANS // 128, 128)
    given = dict(
        len_s=text_lengths, inp_h=inputs, tp_h=text_patches, pv_h=patch_valid, ids_h=ids, pb_h=position_bias,
        ag_h=attn_gain.reshape(dim // 128, 128), fg_h=ffn_gain.reshape(dim // 128, 128), wq_h=query_weight, wk_h=key_weight,
        wv_h=value_weight, wo_h=output_weight, wg_h=gate_weight, wu_h=up_weight, wd_h=down_weight, cot_h=cotangent,
    )
    sizes = sizes_of(heads, ff)
    results = dict(
        wout=[((block, size), f32) for size in sizes], out_o=((rows, dim), bf16), own_o=((rows, dim), bf16),
        text_o=((rows, dim), bf16), small_o=((8, dim // 4 + 128), f32),
    )
    small = ((8, dim // 4 + 128), f32)
    sent = [((half, size), bf16) for size in sizes]
    held = dict(
        inp=((rows, dim), bf16), ids=(ids.shape, jnp.int32), hot=((NB, SPANS), f32), pb=((heads, NB), f32), tp=(text_patches.shape, jnp.int32),
        pv=(patch_valid.shape, jnp.int32), ag=((dim // 128, 128), bf16), fg=((dim // 128, 128), bf16), wq=((dim, width), bf16),
        wk=((dim, width), bf16), wv=((dim, width), bf16), wo=((width, dim), bf16), wg=((ff, dim), bf16),
        wu=((ff, dim), bf16), wd=((ff, dim), bf16), cot=((rows, dim), bf16), inc=((rows, dim), bf16),
        win=((2 * rows // 64, heads, 384), f32), diag=((2 * rows // 64, heads, 384), f32),
        prob=((heads, 2 * rows, rows), f32), xt=((6, half, rows), bf16), xs=((6, half, rows), bf16), xr=((6, half, rows), bf16),
        united=((rows, dim), f32), na=((rows, dim), bf16),
        kv=((rows, 2 * width), bf16), kvr=((rows, 2 * width), bf16), kvt=((2 * width, 2 * rows), bf16),
        q=((rows, width), bf16), qm=((heads, rows, width), bf16), att_t=((width, rows), f32), att=((rows, width), bf16),
        att_r=((rows, width), bf16), part=((rows, dim), f32), stage=((4, rows, dim), bf16),
        land=((4, PARTS, n_mp - 1, own_rows // PARTS, dim), bf16), keep=((4, own_rows, dim), f32), whole=((4, rows, dim), bf16),
        cot_e=((rows, dim), bf16), nf_e=((rows, dim), bf16), hg_e=((rows, ff), f32), hid_e=((rows, ff), bf16),
        hid_er=((rows, ff), bf16), gg_e=((rows, ff), bf16), gg_er=((rows, ff), bf16), ug_e=((rows, ff), bf16),
        ug_er=((rows, ff), bf16), hg=((rows, ff), f32), mid=((own_rows, dim), f32), mgrad=((own_rows, dim), f32), gate=((rows, ff), f32),
        up=((rows, ff), f32), ga=((rows, width), bf16), turn=((rows, rows), bf16), dk=((2 * rows, width), f32),
        dv=((2 * rows, width), f32), dq_t=((width, rows), f32), kvg_s=((rows, 2 * width), bf16),
        kvg_r=((rows, 2 * width), bf16),
    )
    held.update(
        hid=((rows, ff), bf16), hid_r=((rows, ff), bf16), gg=((rows, ff), bf16), gg_r=((rows, ff), bf16),
        ug=((rows, ff), bf16), ug_r=((rows, ff), bf16), dqb=((rows, width), bf16), dq_r=((rows, width), bf16),
        dkb=((rows, width), bf16), dk_r=((rows, width), bf16), dvb=((rows, width), bf16), dv_r=((rows, width), bf16),
        wgrad=[((half, size), f32) for size in sizes], wsend=sent, wleft=sent, wright=sent, small=small, small2=small,
        small3=small, small_m=small, small_q=((n_seq - 1,) + small[0], f32),
        small_p=((n_mp - 1,) + small[0], f32),
    )
    count = 60 + 20 * n_mp + 14 * n_seq
    order = [(name, 0) for name in given]
    out_shape, scratch = [], []
    for specs, into, make in ((results, out_shape, jax.ShapeDtypeStruct), (held, scratch, pltpu.VMEM)):
        for name, spec in specs.items():
            many = spec if isinstance(spec, list) else [spec]
            order.append((name, len(many) if isinstance(spec, list) else 0))
            into.extend(make(*one) for one in many)
    for i, size in enumerate((count, count, len(given) - 1)):
        order.append((("ssem", "rsem", "lsem")[i], 0))
        scratch.append(pltpu.SemaphoreType.DMA((size,)))
    vmem = pl.BlockSpec(memory_space=pltpu.VMEM)
    done = pl.pallas_call(
        functools.partial(mega, n_seq, n_mp, heads, order),
        out_shape=out_shape,
        in_specs=[pl.BlockSpec(memory_space=pltpu.SMEM)] + [pl.BlockSpec(memory_space=pl.ANY)] * (len(given) - 1),
        out_specs=[vmem] * len(out_shape),
        scratch_shapes=scratch,
        compiler_params=pltpu.CompilerParams(
            collective_id=0, has_side_effects=True, vmem_limit_bytes=63 * 2**20
        ),
        name="layer",
    )(*given.values())
    *wout, out, own, text, small_sum = done
    part = dim // (2 * n_seq)
    few = NB // (2 * n_seq)
    shapes = [
        ((1, rows, dim), bf16), ((1, rows, dim), f32), ((1, part), f32), ((block, width), f32), ((block, width), f32),
        ((block, width), f32), ((width, block), f32), ((few, heads), f32), ((1, part), f32), ((ff, block), f32),
        ((ff, block), f32), ((ff, block), f32),
    ]
    outs = pl.pallas_call(
        functools.partial(finish, n_seq, heads, width),
        out_shape=[jax.ShapeDtypeStruct(*spec) for spec in shapes],
        in_specs=[vmem] * 13,
        out_specs=[vmem] * 12,
        scratch_shapes=[pltpu.VMEM((128, 8), f32)],
        compiler_params=pltpu.CompilerParams(vmem_limit_bytes=63 * 2**20),
        name="finish",
    )(
        text_patches, patch_valid, own, text, out, *wout, small_sum
    )
    outs = list(outs)
    for i in (9, 10):
        outs[i] = outs[i].T
    outs[2] = outs[2].reshape(part)
    outs[8] = outs[8].reshape(part)
    return tuple(outs)


def solution(mesh):
    group = ("mod", "seq")
    in_specs = (
        P("mod", "seq", None), P("seq", None), P("seq", None), P("seq", None), P(), P(), P(None, "mp"), P(None, "mp"),
        P(None, "mp"), P("mp", None), P(None, "mp"), P(), P(None, "mp"), P(None, "mp"), P("mp", None),
        P("mod", "seq", None),
    )
    out_specs = (
        P("mod", "seq", None), P("mod", "seq", None), P(group), P(group, "mp"), P(group, "mp"), P(group, "mp"),
        P("mp", group), P(group, "mp"), P(group), P(group, "mp"), P(group, "mp"), P("mp", group),
    )
    body = functools.partial(per_device, mesh.shape["seq"], mesh.shape["mp"])
    return jax.shard_map(body, mesh=mesh, in_specs=in_specs, out_specs=out_specs, check_vma=False)
```

```python
import functools
import types

import jax
import jax.numpy as jnp
from jax import lax
from jax.experimental import pallas as pl
from jax.experimental.pallas import tpu as pltpu
from jax.sharding import PartitionSpec as P

MESH = pl.DeviceIdType.MESH
EPS = 1e-06
PARTS = 2
ROOT = 0.7978845608028654
HEAD = 64
NB = 32
PDOC = 128
LONG = 192
SPANS = 640
WIDE = 896
f32 = jnp.float32
bf16 = jnp.bfloat16


def nn(a, b):
    return jnp.dot(a, b, preferred_element_type=f32)


def nt(a, b):
    return lax.dot_general(a, b, (((1,), (1,)), ((), ())), preferred_element_type=f32)


def rms_scale(x):
    return lax.rsqrt(jnp.mean(x * x, axis=-1, keepdims=True) + EPS)


def row_chunks(first, total, step, body):
    def one(i, carry):
        body(pl.ds(pl.multiple_of(first + i * step, step), step))
        return carry

    lax.fori_loop(0, total // step, one, 0)


def bucket_hot(ids_row):
    return (lax.broadcasted_iota(jnp.int32, (NB, SPANS), 0) == ids_row).astype(f32)


def patch_counts(ids, valid, rows):
    places = lax.broadcasted_iota(jnp.int32, (rows, rows), 0)
    count = jnp.zeros((rows, rows), f32)
    for j in range(ids.shape[0]):
        count += jnp.where(ids[j : j + 1, :] == places, valid[j : j + 1, :].astype(f32), 0.0)
    return count


def flat(ref):
    value = ref[...].astype(f32)
    return jnp.concatenate([value[i : i + 1, :] for i in range(value.shape[0])], axis=1)


def sizes_of(heads, ff):
    width = heads * HEAD
    return (ff, ff, ff, width, width, width, width)


def mega(n_seq, n_mp, heads, order, *refs):
    ref, refs = types.SimpleNamespace(), list(refs)
    for name, many in order:
        setattr(ref, name, [refs.pop(0) for _ in range(many)] if many else refs.pop(0))
    mod, seq, mp = lax.axis_index("mod"), lax.axis_index("seq"), lax.axis_index("mp")
    rows, dim = ref.united.shape
    width = heads * HEAD
    ff = ref.wg.shape[0]
    half = dim // 2
    block = half // n_seq
    part_rows = rows // PARTS
    own_rows = part_rows // n_mp
    parts = range(PARTS)

    def part(k):
        return slice(k * part_rows, (k + 1) * part_rows)

    def share(k, who):
        return pl.ds(pl.multiple_of(k * part_rows + who * own_rows, own_rows), own_rows)

    def kept(k):
        return slice(k * own_rows, (k + 1) * own_rows)

    here = pl.ds(pl.multiple_of(mod * half, half), half)
    there = pl.ds(pl.multiple_of((1 - mod) * half, half), half)
    sibling = (1 - mod, seq, mp)
    used = [0]
    sends = []
    is_end = (seq == 0) | (seq == n_seq - 1)
    not_end = (seq > 0) & (seq < n_seq - 1)
    is_inner = (seq == 1) | (seq == n_seq - 2)
    inner = (mod, seq + 1 - 2 * (seq // (n_seq - 1)), mp)

    def when(cond, body):
        if cond is None:
            body()
        else:
            pl.when(cond)(body)

    def peer_of(o):
        if n_mp == 4:
            return (mp + 1 - 2 * (mp % 2), (mp + 2) % 4, 3 - mp)[o - 1]
        return (mp + o) % n_mp

    def source_of(o):
        if n_mp == 4:
            return peer_of(o)
        return (mp + n_mp - o) % n_mp

    def message(src, dst, device, cond=None):
        index = used[0]
        used[0] += 1
        copy = pltpu.make_async_remote_copy(
            src_ref=src,
            dst_ref=dst,
            send_sem=ref.ssem.at[index],
            recv_sem=ref.rsem.at[index],
            device_id=device,
            device_id_type=MESH,
        )
        sends.append((cond, copy))
        return copy

    loads = types.SimpleNamespace()
    pairs = (
        (ref.inp_h.at[0], ref.inp), (ref.pb_h, ref.pb), (ref.tp_h, ref.tp), (ref.pv_h, ref.pv),
        (ref.ag_h, ref.ag), (ref.wk_h, ref.wk), (ref.wv_h, ref.wv), (ref.wq_h, ref.wq), (ref.cot_h.at[0], ref.cot),
        (ref.wo_h, ref.wo), (ref.wd_h, ref.wd), (ref.fg_h, ref.fg), (ref.wg_h, ref.wg), (ref.wu_h, ref.wu),
    )
    copies = [pltpu.make_async_copy(src, dst, ref.lsem.at[i]) for i, (src, dst) in enumerate(pairs)]
    for copy in copies:
        copy.start()
    (loads.inp, loads.pb, loads.tp, loads.pv, loads.ag, loads.wk, loads.wv, loads.wq, loads.cot, loads.wo,
     loads.wd, loads.fg, loads.wg, loads.wu) = copies

    barrier = pltpu.get_barrier_semaphore()
    pl.semaphore_signal(barrier, 1, device_id=sibling, device_id_type=MESH)
    for o in range(1, n_mp):
        pl.semaphore_signal(barrier, 1, device_id=(mod, seq, peer_of(o)), device_id_type=MESH)

    for o in range(1, n_seq):
        pl.semaphore_signal(barrier, 1, device_id=(mod, (seq + o) % n_seq, mp), device_id_type=MESH)
    pl.semaphore_wait(barrier, n_mp + n_seq - 1)

    to_text = message(ref.inp_h.at[0], ref.inc, sibling, mod == 0)

    @pl.when(mod == 0)
    def _():
        to_text.start()

    cot_end = message(ref.cot_h.at[0], ref.cot_e, inner, is_end)
    when(is_end, cot_end.start)

    first = ref.len_s[0, 0]
    long_first = first == LONG
    loads.pb.wait()
    mirror = (
        lax.broadcasted_iota(jnp.int32, (128, 128), 0) + lax.broadcasted_iota(jnp.int32, (128, 128), 1) == 127
    ).astype(f32)
    places = lax.broadcasted_iota(jnp.int32, (8, 128), 0) * 128 + lax.broadcasted_iota(jnp.int32, (8, 128), 1)
    span = ref.ids_s.shape[0]
    stride = 9 if span % 9 == 0 else 1

    def set_ids(i, ids):
        for k in range(stride):
            ids = jnp.where(places == i * stride + k, ref.ids_s[i * stride + k], ids)
        return ids

    ids = lax.fori_loop(0, span // stride, set_ids, jnp.zeros((8, 128), jnp.int32))
    turned_ids = nn(ids.astype(f32).astype(bf16), mirror.astype(bf16))
    lines = SPANS // 128
    turned_ids = jnp.concatenate([turned_ids[i : i + 1, :] for i in reversed(range(lines))], axis=1)
    hot = bucket_hot(turned_ids.astype(jnp.int32))
    ref.hot[...] = hot
    rel = jnp.dot(ref.pb[...], hot, precision=lax.Precision.HIGHEST, preferred_element_type=f32)
    rel = jnp.concatenate([rel, jnp.zeros((heads, WIDE - SPANS), f32)], axis=1)
    blocks = rows // 64
    apart = ((-128, -128), (-128, -192), (-128, -192), (-64, -192))
    along = ((128, 128), (128, 128), (64, 192), (64, 192))

    def window(c):
        return pltpu.roll(rel, (WIDE - (c + 256)) % WIDE, 1)[:, :384]

    lane_row = lax.broadcasted_iota(jnp.int32, (1, rows), 1)
    patch_doc = lane_row // PDOC
    text_doc = (lane_row >= first).astype(jnp.int32)
    query_doc = jnp.where(mod == 0, patch_doc, text_doc)
    for kb in range(blocks):
        ref.win[kb] = window(-64 * kb)
        a0, a1 = (window(c - 64 * kb) for c in apart[kb])
        b0, b1 = (window(c - 64 * kb) for c in along[kb])
        ref.win[blocks + kb] = jnp.where(
            mod == 0, jnp.where(long_first, a0, a1), jnp.where(long_first, b0, b1)
        )
    for kb in range(2 * blocks):
        at = kb % blocks
        in_patch = (mod == 0) if kb < blocks else (mod == 1)
        key_doc = jnp.where(in_patch, at * 64 // PDOC, jnp.where(at * 64 >= first, 1, 0))
        same = query_doc == key_doc

        def one_bias(h, carry, kb=kb, same=same):
            line = jnp.broadcast_to(ref.win[kb, pl.ds(h, 1), :], (64, 384))
            table = pltpu.roll(line, 320, 1, stride=1, stride_axis=0)[:, :rows]
            ref.prob[h, kb * 64 : kb * 64 + 64, :] = jnp.where(same, table, -1000000000.0)
            return carry

        lax.fori_loop(0, heads, one_bias, 0)

    loads.cot.wait()

    def transposed(source, sides, cond=None):
        copy = message(sides.s, sides.r, sibling, cond)

        def body():
            sides.s[...] = source[:, there].T
            copy.start()
            sides.t[...] = source[:, here].T

        when(cond, body)
        return copy

    x_tan, x_na, x_nf, x_branch, x_tan_e, x_nf_e = (
        types.SimpleNamespace(t=ref.xt.at[i], s=ref.xs.at[i], r=ref.xr.at[i]) for i in range(6)
    )
    tan_sent = transposed(ref.cot, x_tan, not_end)

    loads.tp.wait()
    loads.pv.wait()
    loads.inp.wait()

    @pl.when(mod == 1)
    def _():
        count = patch_counts(ref.tp[...], ref.pv[...], rows).T.astype(bf16)
        to_text.wait_recv()
        ref.united[...] = nn(count, ref.inc[...])

    @pl.when(mod == 0)
    def _():
        ref.united[...] = jnp.zeros((rows, dim), f32)

    loads.ag.wait()
    attn_gain = flat(ref.ag)

    def first_norm(at):
        u = ref.united[at, :] + ref.inp[at, :].astype(f32)
        ref.united[at, :] = u
        ref.na[at, :] = (u * rms_scale(u) * attn_gain).astype(bf16)

    row_chunks(0, rows, 32, first_norm)
    loads.wk.wait()
    ref.kv[:, :width] = nn(ref.na[...], ref.wk[...]).astype(bf16)
    loads.wv.wait()
    ref.kv[:, width:] = nn(ref.na[...], ref.wv[...]).astype(bf16)
    kv_sent = message(ref.kv, ref.kvr, sibling)
    kv_sent.start()
    loads.wq.wait()
    ref.q[...] = nn(ref.na[...], ref.wq[...]).astype(bf16)
    ref.kvt[:, :rows] = ref.kv[...].T
    na_sent = transposed(ref.na, x_na)
    kv_sent.wait_recv()
    ref.kvt[:, rows:] = ref.kvr[...].T
    head_of = lax.broadcasted_iota(jnp.int32, (1, width), 1) // HEAD

    def head_mask(h):
        return (head_of == h).astype(f32).astype(bf16)

    def head_rows(h, base=0):
        return pl.ds(pl.multiple_of(base + h * HEAD, HEAD), HEAD)

    def head_fwd(k, h, carry):
        at = part(k)
        qm = ref.q[at, :] * head_mask(h)
        ref.qm[h, at, :] = qm
        s0 = nt(ref.kv[:, :width], qm) * 0.125 + ref.prob[h, :rows, at]
        s1 = nt(ref.kvr[:, :width], qm) * 0.125 + ref.prob[h, rows:, at]
        top = jnp.maximum(jnp.max(s0, axis=0, keepdims=True), jnp.max(s1, axis=0, keepdims=True))
        e0 = jnp.exp(s0 - top)
        e1 = jnp.exp(s1 - top)
        total = jnp.sum(e0, axis=0, keepdims=True) + jnp.sum(e1, axis=0, keepdims=True)
        scale = 1.0 / total
        p0 = e0 * scale
        p1 = e1 * scale
        ref.prob[h, :rows, at] = p0
        ref.prob[h, rows:, at] = p1
        values_t = ref.kvt[head_rows(h, width), :]
        ref.att_t[head_rows(h), at] = nn(values_t[:, :rows], p0.astype(bf16)) + nn(
            values_t[:, rows:], p1.astype(bf16)
        )
        return carry

    def scatter(c, k, product, hold=False):
        ref.part[part(k), :] = product
        ref.stage[c, part(k), :] = product.astype(bf16)
        copies = []
        for o in range(n_mp - 1, 0, -1):
            to = peer_of(o)
            copies.append(message(ref.stage.at[c, share(k, to)], ref.land.at[c, k, o - 1], (mod, seq, to)))
            if not hold:
                copies[-1].start()
        ref.keep[c, kept(k), :] = ref.part[share(k, mp), :]
        return copies

    def summed(c, k, copies):
        for copy in copies:
            copy.wait_recv()
        total = ref.keep[c, kept(k), :]
        for o in range(1, n_mp):
            total += ref.land[c, k, o - 1].astype(f32)
        return total

    def gather(c, k):
        at = ref.whole.at[c, share(k, mp)]
        copies = [message(at, at, (mod, seq, peer_of(o))) for o in range(1, n_mp)]
        for copy in reversed(copies):
            copy.start()
        return copies

    loads.wo.wait()
    attn_sum = []
    for k in parts:
        lax.fori_loop(0, heads, functools.partial(head_fwd, k), 0)
        ref.att[part(k), :] = ref.att_t[:, part(k)].T.astype(bf16)
        attn_sum.append(scatter(0, k, nn(ref.att[part(k), :], ref.wo[...])))
    att_sent = message(ref.att, ref.att_r, sibling)
    att_sent.start()
    loads.wd.wait()
    ref.hg[...] = nt(ref.cot[...], ref.wd[...])
    loads.fg.wait()
    ffn_gain = flat(ref.fg)
    nf_end = []

    def to_inner(k, who):
        at = share(k, who)
        copy = message(ref.whole.at[0, at], ref.nf_e.at[at], inner, is_end)
        when(is_end, copy.start)
        nf_end.append(copy)

    nf_parts = []
    for k in parts:
        middle = ref.united[share(k, mp), :] + summed(0, k, attn_sum[k])
        ref.mid[kept(k), :] = middle
        ref.whole[0, share(k, mp), :] = (middle * rms_scale(middle) * ffn_gain).astype(bf16)
        nf_parts.append(gather(0, k))
        to_inner(k, mp)
    tan_e_sent = message(x_tan_e.s, x_tan_e.r, sibling, is_inner)

    @pl.when(is_inner)
    def _():
        cot_end.wait_recv()
        x_tan_e.s[...] = ref.cot_e[:, there].T
        tan_e_sent.start()
        x_tan_e.t[...] = ref.cot_e[:, here].T
        ref.hg_e[...] = nt(ref.cot_e[...], ref.wd[...])

    loads.wg.wait()
    loads.wu.wait()

    def gelu_rows(at, back_ref=ref.hg, hid=ref.hid, gg=ref.gg, ug=ref.ug):
        g, u, back = ref.gate[at, :], ref.up[at, :], back_ref[at, :]
        squared = g * g
        t = jnp.tanh(ROOT * (g + 0.044715 * squared * g))
        left = 0.5 * (1.0 + t)
        gelu = left * g
        slope = left + 0.5 * g * (1.0 - t * t) * (ROOT * (1.0 + 0.134145 * squared))
        hid[at, :] = (gelu * u).astype(bf16)
        gg[at, :] = (back * u * slope).astype(bf16)
        ug[at, :] = (back * gelu).astype(bf16)

    ffn_in = []
    for k in parts:
        for o, copy in enumerate(nf_parts[k], 1):
            copy.wait_recv()
            to_inner(k, source_of(o))
        at = part(k)
        ref.gate[at, :] = nt(ref.whole[0, at, :], ref.wg[...])
        ref.up[at, :] = nt(ref.whole[0, at, :], ref.wu[...])
        row_chunks(k * part_rows, part_rows, 32, gelu_rows)
        ffn_in.append(scatter(1, k, nn(ref.gg[at, :], ref.wg[...]) + nn(ref.ug[at, :], ref.wu[...])))
    hid_sent = message(ref.hid, ref.hid_r, sibling, not_end)
    gg_sent = message(ref.gg, ref.gg_r, sibling, not_end)
    ug_sent = message(ref.ug, ref.ug_r, sibling, not_end)
    when(not_end, hid_sent.start)
    nf_sent = transposed(ref.whole.at[0], x_nf, not_end)
    when(not_end, gg_sent.start)
    when(not_end, ug_sent.start)

    after = (mod, jnp.minimum(seq + 1, n_seq - 1), mp)
    before = (mod, jnp.maximum(seq - 1, 0), mp)
    weights = []
    ends = (1, 1, 1, 0, 0, 0, 0)
    for e, g, s, a, b, o in zip(ends, ref.wgrad, ref.wsend, ref.wleft, ref.wright, ref.wout, strict=True):
        right, left = {}, {}
        for j in range(n_seq):
            rng = pl.ds(j * block, block)
            if j > e:
                right[j] = message(s.at[rng], a.at[rng], after, (seq >= e) & (seq < j))
            if j < n_seq - 1 - e:
                left[j] = message(s.at[rng], b.at[rng], before, (seq < n_seq - e) & (seq > j))
        weights.append(types.SimpleNamespace(e=e, g=g, s=s, a=a, b=b, o=o, right=right, left=left))
    w_down, w_gate, w_up, w_proj, w_q, w_k, w_v = weights

    def product(w, x, pieces, more=False):
        lo = 0
        for own, other in pieces:
            size = own.shape[1]
            both = nn(x.t[...], own[...]) + nn(x.r[...], other[...])
            if more:
                both += w.g[:, lo : lo + size]
            w.g[:, lo : lo + size] = both
            lo += size

    def hop(group, step, some=slice(None)):
        edge = group[0].e + step
        if edge >= n_seq - 1:
            return

        @pl.when(seq == edge)
        def _():
            for j in list(range(n_seq - 1, edge, -1))[some]:
                rng = slice(j * block, (j + 1) * block)
                for w in group:
                    value = w.g[rng, :]
                    if step > 0:
                        w.right[j].wait_recv()
                        value += w.a[rng, :].astype(f32)
                    w.s[rng, :] = value.astype(bf16)
                    w.right[j].start()

        @pl.when(seq == n_seq - 1 - edge)
        def _():
            for j in list(range(n_seq - 1 - edge))[some]:
                rng = slice(j * block, (j + 1) * block)
                for w in group:
                    value = w.g[rng, :]
                    if step > 0:
                        w.left[j].wait_recv()
                        value += w.b[rng, :].astype(f32)
                    w.s[rng, :] = value.astype(bf16)
                    w.left[j].start()

    def arrive(w):
        for j in range(n_seq):

            @pl.when(seq == j)
            def _(j=j):
                rng = slice(j * block, (j + 1) * block)
                value = w.g[rng, :] if w.e <= j < n_seq - w.e else jnp.zeros(w.o.shape, f32)
                if j > w.e:
                    w.right[j].wait_recv()
                    value += w.a[rng, :].astype(f32)
                if j < n_seq - 1 - w.e:
                    w.left[j].wait_recv()
                    value += w.b[rng, :].astype(f32)
                w.o[...] = value

    gain_sums = []
    branch_parts = []

    def middle_back(k):
        normed_grad = summed(1, k, ffn_in[k])
        middle = ref.mid[kept(k), :]
        scale = rms_scale(middle)
        spread = normed_grad * ffn_gain
        gain_sums.append(jnp.sum(normed_grad * middle * scale, axis=0, keepdims=True))
        middle_grad = (
            ref.cot[share(k, mp), :].astype(f32)
            + scale * spread
            - middle * (scale * scale * scale) * jnp.mean(spread * middle, axis=-1, keepdims=True)
        )
        ref.mgrad[kept(k), :] = middle_grad
        ref.whole[1, share(k, mp), :] = middle_grad.astype(bf16)
        branch_parts.append(gather(1, k))

    hid_e_sent = message(ref.hid_e, ref.hid_er, sibling, is_inner)
    gg_e_sent = message(ref.gg_e, ref.gg_er, sibling, is_inner)
    ug_e_sent = message(ref.ug_e, ref.ug_er, sibling, is_inner)
    nf_e_sent = message(x_nf_e.s, x_nf_e.r, sibling, is_inner)

    @pl.when(not_end)
    def _():
        hid_sent.wait_recv()
        tan_sent.wait_recv()
        product(w_down, x_tan, [(ref.hid, ref.hid_r)])
        nf_sent.wait_recv()
        gg_sent.wait_recv()
        product(w_gate, x_nf, [(ref.gg, ref.gg_r)])
        ug_sent.wait_recv()
        product(w_up, x_nf, [(ref.ug, ref.ug_r)])

    middle_back(0)
    @pl.when(is_inner)
    def _():
        for copy in nf_end:
            copy.wait_recv()
        ref.gate[...] = nt(ref.nf_e[...], ref.wg[...])
        ref.up[...] = nt(ref.nf_e[...], ref.wu[...])
        row_chunks(0, rows, 32, lambda at: gelu_rows(at, ref.hg_e, ref.hid_e, ref.gg_e, ref.ug_e))
        hid_e_sent.start()
        x_nf_e.s[...] = ref.nf_e[:, there].T
        nf_e_sent.start()
        gg_e_sent.start()
        ug_e_sent.start()
        x_nf_e.t[...] = ref.nf_e[:, here].T


    for k in parts[1:]:
        middle_back(k)

    def end_products(w, x, pieces, needs):
        @pl.when(is_inner)
        def _():
            for copy in needs:
                copy.wait_recv()
            product(w, x, pieces, more=True)

        hop([w], 0, slice(0, 1))

    end_products(w_down, x_tan_e, [(ref.hid_e, ref.hid_er)], (hid_e_sent, tan_e_sent))
    end_products(w_gate, x_nf_e, [(ref.gg_e, ref.gg_er)], (gg_e_sent, nf_e_sent))
    end_products(w_up, x_nf_e, [(ref.ug_e, ref.ug_er)], (ug_e_sent,))
    hop([w_down, w_gate, w_up], 0, slice(1, None))
    ffn_out = [scatter(2, k, nn(ref.hid[part(k), :], ref.wd[...]), hold=True) for k in parts]

    flip = (
        lax.broadcasted_iota(jnp.int32, (rows, rows), 0) // 64 == lax.broadcasted_iota(jnp.int32, (rows, rows), 1) // 64
    ) & (
        lax.broadcasted_iota(jnp.int32, (rows, rows), 0) % 64
        + lax.broadcasted_iota(jnp.int32, (rows, rows), 1) % 64
        == 63
    )
    ref.turn[...] = flip.astype(f32).astype(bf16)
    ref.dk[...] = jnp.zeros((2 * rows, width), f32)
    ref.dv[...] = jnp.zeros((2 * rows, width), f32)

    def head_bwd(k, h, carry):
        a = part(k)
        gm = ref.ga[a, :] * head_mask(h)
        p0, p1 = ref.prob[h, :rows, a], ref.prob[h, rows:, a]
        d0 = nt(ref.kv[:, width:], gm)
        d1 = nt(ref.kvr[:, width:], gm)
        inner_sum = jnp.sum(p0 * d0, axis=0, keepdims=True) + jnp.sum(p1 * d1, axis=0, keepdims=True)
        g0 = (p0 * (d0 - inner_sum)).astype(bf16)
        g1 = (p1 * (d1 - inner_sum)).astype(bf16)
        keys_t = ref.kvt[head_rows(h), :]
        ref.dq_t[head_rows(h), a] = nn(keys_t[:, :rows], g0) + nn(keys_t[:, rows:], g1)
        qm = ref.qm[h, a, :]
        ref.dk[:rows, :] += nn(g0, qm)
        ref.dk[rows:, :] += nn(g1, qm)
        ref.dv[:rows, :] += nn(p0.astype(bf16), gm)
        ref.dv[rows:, :] += nn(p1.astype(bf16), gm)
        turn = ref.turn[...]
        low, wide = k * part_rows, part_rows + 128
        for side, g in ((0, g0), (1, g1)):
            turned = nn(turn, g)
            for at in range(blocks):
                piece = turned[at * 64 : at * 64 + 64, :]
                piece = jnp.concatenate([piece, jnp.zeros((64, 128), f32)], axis=1)
                piece = pltpu.roll(piece, 1, 1, stride=1, stride_axis=0)
                ref.diag[side * blocks + at, pl.ds(h, 1), low : low + wide] += jnp.sum(piece, axis=0, keepdims=True)
        return carry

    ref.diag[...] = jnp.zeros(ref.diag.shape, f32)
    for k in parts:
        for copy in branch_parts[k]:
            copy.wait_recv()
        ref.ga[part(k), :] = nt(ref.whole[1, part(k), :], ref.wo[...]).astype(bf16)
        if k == PARTS - 1:
            for copies in ffn_out:
                for copy in copies:
                    copy.start()
        lax.fori_loop(0, heads, functools.partial(head_bwd, k), 0)
    branch_sent = transposed(ref.whole.at[1], x_branch)
    ref.kvg_s[:, :width] = (ref.dk[rows:, :] * 0.125).astype(bf16)
    ref.kvg_s[:, width:] = ref.dv[rows:, :].astype(bf16)
    kvg_sent = message(ref.kvg_s, ref.kvg_r, sibling)
    kvg_sent.start()
    ref.dqb[...] = (ref.dq_t[...].T * 0.125).astype(bf16)
    dq_sent = message(ref.dqb, ref.dq_r, sibling)
    dq_sent.start()
    att_sent.wait_recv()
    branch_sent.wait_recv()
    product(w_proj, x_branch, [(ref.att, ref.att_r)])
    hop([w_proj], 0)
    hop([w_down, w_gate], 1)
    na_sent.wait_recv()
    dq_sent.wait_recv()
    product(w_q, x_na, [(ref.dqb, ref.dq_r)])
    hop([w_q], 0)
    kvg_sent.wait_recv()
    ref.dkb[...] = (ref.dk[:rows, :] * 0.125 + ref.kvg_r[:, :width].astype(f32)).astype(bf16)
    ref.dvb[...] = (ref.dv[:rows, :] + ref.kvg_r[:, width:].astype(f32)).astype(bf16)
    dk_sent = message(ref.dkb, ref.dk_r, sibling)
    dv_sent = message(ref.dvb, ref.dv_r, sibling)
    for copy in (dk_sent, dv_sent):
        copy.start()
    attn_in = []
    for k in parts:
        at = part(k)
        rows_in = nt(ref.dqb[at, :], ref.wq[...]) + nt(ref.dkb[at, :], ref.wk[...]) + nt(ref.dvb[at, :], ref.wv[...])
        attn_in.append(scatter(3, k, rows_in))
    for copy in (dk_sent, dv_sent):
        copy.wait_recv()
    product(w_k, x_na, [(ref.dkb, ref.dk_r)])
    product(w_v, x_na, [(ref.dvb, ref.dv_r)])
    hop([w_k, w_v], 0)
    hop([w_up], 1)

    def gain_rows(i, total):
        at = pl.ds(pl.multiple_of(i * 32, 32), 32)
        u = ref.united[at, :]
        return total + jnp.sum(ref.part[at, :] * u * rms_scale(u), axis=0, keepdims=True)

    attn_gain_grad = lax.fori_loop(0, rows // 32, gain_rows, jnp.zeros((1, dim), f32))

    def unwindow(piece, c):
        grown = jnp.concatenate([piece, jnp.zeros((heads, WIDE - 384), f32)], axis=1)
        return pltpu.roll(grown, (c + 256) % WIDE, 1)

    total = jnp.zeros((heads, WIDE), f32)
    for kb in range(blocks):
        total += unwindow(ref.diag[kb], -64 * kb)
        piece = ref.diag[blocks + kb]
        a0, a1 = (unwindow(piece, c - 64 * kb) for c in apart[kb])
        b0, b1 = (unwindow(piece, c - 64 * kb) for c in along[kb])
        total += jnp.where(mod == 0, jnp.where(long_first, a0, a1), jnp.where(long_first, b0, b1))
    bias_grad = lax.dot_general(
        total[:, :SPANS], ref.hot[...], (((1,), (1,)), ((), ())), precision=lax.Precision.HIGHEST, preferred_element_type=f32
    )
    quarter = dim // 4
    for i, line in enumerate((attn_gain_grad, sum(gain_sums))):
        for k in range(4):
            ref.small[4 * i + k : 4 * i + k + 1, :quarter] = line[:, k * quarter : (k + 1) * quarter]
    ref.small[:, quarter:] = jnp.zeros((8, 128), f32)
    ref.small[:heads, quarter : quarter + NB] = bias_grad
    small_mp = [message(ref.small, ref.small_p.at[o - 1], (mod, seq, peer_of(o))) for o in range(1, n_mp)]
    for copy in small_mp:
        copy.start()

    hop([w_proj, w_q], 1)
    for copy in small_mp:
        copy.wait_recv()
    gains = ref.small[:, :quarter]
    for o in range(1, n_mp):
        gains += ref.small_p[o - 1, :, :quarter]
    ref.small2[:, :quarter] = gains
    ref.small2[:, quarter:] = ref.small[:, quarter:]
    small_mod = message(ref.small2, ref.small_m, sibling)
    small_mod.start()

    united_parts = []
    for k in parts:
        normed_grad = summed(3, k, attn_in[k])
        u = ref.united[share(k, mp), :]
        scale = rms_scale(u)
        spread = normed_grad * attn_gain
        united_grad = (
            ref.mgrad[kept(k), :]
            + scale * spread
            - u * (scale * scale * scale) * jnp.mean(spread * u, axis=-1, keepdims=True)
        )
        ref.whole[3, share(k, mp), :] = united_grad.astype(bf16)
        united_parts.append(gather(3, k))
    output_parts = []
    for k in parts:
        ref.whole[2, share(k, mp), :] = (ref.mid[kept(k), :] + summed(2, k, ffn_out[k])).astype(bf16)
        output_parts.append(gather(2, k))
    hop([w_k, w_v], 1)
    small_mod.wait_recv()
    ref.small3[...] = ref.small2[...] + ref.small_m[...]
    small_seq = [
        message(ref.small3, ref.small_q.at[o - 1], (mod, (seq + o) % n_seq, mp)) for o in range(1, n_seq)
    ]
    for copy in small_seq:
        copy.start()
    backs = []
    for k in parts:
        for o in range(n_mp):
            at = share(k, source_of(o) if o else mp)
            if o:
                united_parts[k][o - 1].wait_recv()
            back = message(ref.whole.at[3, at], ref.text_o.at[at], sibling, mod == 1)
            when(mod == 1, back.start)
            backs.append(back)
    for step in range(2, n_seq - 1):
        hop([w_down, w_gate, w_up], step)
        hop([w_proj, w_q], step)
        hop([w_k, w_v], step)
    for copies in output_parts:
        for copy in copies:
            copy.wait_recv()
    ref.out_o[...] = ref.whole[2]
    ref.own_o[...] = ref.whole[3]
    for w in weights:
        arrive(w)

    total = ref.small3[...]
    for i, copy in enumerate(small_seq):
        copy.wait_recv()
        total += ref.small_q[i]
    ref.small_o[...] = total

    @pl.when(mod == 0)
    def _():
        for back in backs:
            back.wait_recv()

    @pl.when(mod == 1)
    def _():
        ref.text_o[...] = jnp.zeros((rows, dim), bf16)

    for cond, copy in sends:
        if cond is None:
            copy.wait_send()
        else:

            @pl.when(cond)
            def _(copy=copy):
                copy.wait_send()

    assert used[0] <= ref.ssem.shape[0]


def finish(n_seq, heads, width, ids, valid, own, text, out, gd, gg, gu, go, gq, gk, gv, small,
           o_out, o_in, o_ag, o_q, o_k, o_v, o_o, o_pb, o_fg, o_gate, o_up, o_down, hold):
    mod, seq = lax.axis_index("mod"), lax.axis_index("seq")
    rows, dim = own.shape
    place = mod * n_seq + seq
    o_out[0] = out[...]

    @pl.when(mod == 0)
    def _():
        count = patch_counts(ids[...], valid[...], rows)
        o_in[0] = own[...].astype(f32) + nn(count.astype(bf16), text[...])

    @pl.when(mod == 1)
    def _():
        o_in[0] = own[...].astype(f32)

    o_q[...] = gq[...]
    o_k[...] = gk[...]
    o_v[...] = gv[...]
    o_o[...] = go[...].T
    o_gate[...] = gg[...].T
    o_up[...] = gu[...].T
    o_down[...] = gd[...].T
    quarter = dim // 4
    part = dim // (2 * n_seq)
    for i, o_gain in enumerate((o_ag, o_fg)):
        line = jnp.concatenate([small[4 * i + k : 4 * i + k + 1, :quarter] for k in range(4)], axis=1)
        line = pltpu.roll(jnp.broadcast_to(line, (8, dim)), dim - place * part, 1)
        o_gain[...] = line[:1, :part]
    few = NB // (2 * n_seq)
    hold[...] = small[:, quarter:].T
    o_pb[...] = hold[pl.ds(place * few, few), :heads]


def per_device(n_seq, n_mp, *args):
    (inputs, text_patches, patch_valid, text_lengths, bucket_table, attn_gain, query_weight, key_weight,
     value_weight, output_weight, position_bias, ffn_gain, gate_weight, up_weight, down_weight, cotangent) = args
    rows, dim = inputs.shape[1:]
    heads = position_bias.shape[1]
    width = heads * HEAD
    ff = down_weight.shape[0]
    own_rows = rows // n_mp
    half = dim // 2
    block = half // n_seq
    text_patches, patch_valid, position_bias = text_patches.T, patch_valid.T, position_bias.T
    gate_weight, up_weight = gate_weight.T, up_weight.T
    given = dict(
        len_s=text_lengths, ids_s=bucket_table, inp_h=inputs, tp_h=text_patches, pv_h=patch_valid, pb_h=position_bias,
        ag_h=attn_gain.reshape(dim // 128, 128), fg_h=ffn_gain.reshape(dim // 128, 128), wq_h=query_weight, wk_h=key_weight,
        wv_h=value_weight, wo_h=output_weight, wg_h=gate_weight, wu_h=up_weight, wd_h=down_weight, cot_h=cotangent,
    )
    sizes = sizes_of(heads, ff)
    results = dict(
        wout=[((block, size), f32) for size in sizes], out_o=((rows, dim), bf16), own_o=((rows, dim), bf16),
        text_o=((rows, dim), bf16), small_o=((8, dim // 4 + 128), f32),
    )
    small = ((8, dim // 4 + 128), f32)
    sent = [((half, size), bf16) for size in sizes]
    held = dict(
        inp=((rows, dim), bf16), hot=((NB, SPANS), f32), pb=((heads, NB), f32), tp=(text_patches.shape, jnp.int32),
        pv=(patch_valid.shape, jnp.int32), ag=((dim // 128, 128), bf16), fg=((dim // 128, 128), bf16), wq=((dim, width), bf16),
        wk=((dim, width), bf16), wv=((dim, width), bf16), wo=((width, dim), bf16), wg=((ff, dim), bf16),
        wu=((ff, dim), bf16), wd=((ff, dim), bf16), cot=((rows, dim), bf16), inc=((rows, dim), bf16),
        win=((2 * rows // 64, heads, 384), f32), diag=((2 * rows // 64, heads, 384), f32),
        prob=((heads, 2 * rows, rows), f32), xt=((6, half, rows), bf16), xs=((6, half, rows), bf16), xr=((6, half, rows), bf16),
        united=((rows, dim), f32), na=((rows, dim), bf16),
        kv=((rows, 2 * width), bf16), kvr=((rows, 2 * width), bf16), kvt=((2 * width, 2 * rows), bf16),
        q=((rows, width), bf16), qm=((heads, rows, width), bf16), att_t=((width, rows), f32), att=((rows, width), bf16),
        att_r=((rows, width), bf16), part=((rows, dim), f32), stage=((4, rows, dim), bf16),
        land=((4, PARTS, n_mp - 1, own_rows // PARTS, dim), bf16), keep=((4, own_rows, dim), f32), whole=((4, rows, dim), bf16),
        cot_e=((rows, dim), bf16), nf_e=((rows, dim), bf16), hg_e=((rows, ff), f32), hid_e=((rows, ff), bf16),
        hid_er=((rows, ff), bf16), gg_e=((rows, ff), bf16), gg_er=((rows, ff), bf16), ug_e=((rows, ff), bf16),
        ug_er=((rows, ff), bf16), hg=((rows, ff), f32), mid=((own_rows, dim), f32), mgrad=((own_rows, dim), f32), gate=((rows, ff), f32),
        up=((rows, ff), f32), ga=((rows, width), bf16), turn=((rows, rows), bf16), dk=((2 * rows, width), f32),
        dv=((2 * rows, width), f32), dq_t=((width, rows), f32), kvg_s=((rows, 2 * width), bf16),
        kvg_r=((rows, 2 * width), bf16),
    )
    held.update(
        hid=((rows, ff), bf16), hid_r=((rows, ff), bf16), gg=((rows, ff), bf16), gg_r=((rows, ff), bf16),
        ug=((rows, ff), bf16), ug_r=((rows, ff), bf16), dqb=((rows, width), bf16), dq_r=((rows, width), bf16),
        dkb=((rows, width), bf16), dk_r=((rows, width), bf16), dvb=((rows, width), bf16), dv_r=((rows, width), bf16),
        wgrad=[((half, size), f32) for size in sizes], wsend=sent, wleft=sent, wright=sent, small=small, small2=small,
        small3=small, small_m=small, small_q=((n_seq - 1,) + small[0], f32),
        small_p=((n_mp - 1,) + small[0], f32),
    )
    count = 60 + 20 * n_mp + 14 * n_seq
    order = [(name, 0) for name in given]
    out_shape, scratch = [], []
    for specs, into, make in ((results, out_shape, pltpu.VMEM), (held, scratch, pltpu.VMEM)):
        for name, spec in specs.items():
            many = spec if isinstance(spec, list) else [spec]
            order.append((name, len(many) if isinstance(spec, list) else 0))
            into.extend(make(*one) for one in many)
    for i, size in enumerate((count, count, len(given) - 2)):
        order.append((("ssem", "rsem", "lsem")[i], 0))
        scratch.append(pltpu.SemaphoreType.DMA((size,)))
    vmem = pl.BlockSpec(memory_space=pltpu.VMEM)
    done = pl.pallas_call(
        functools.partial(mega, n_seq, n_mp, heads, order),
        out_shape=out_shape,
        in_specs=[pl.BlockSpec(memory_space=pltpu.SMEM)] * 2 + [pl.BlockSpec(memory_space=pl.ANY)] * (len(given) - 2),
        scratch_shapes=scratch,
        compiler_params=pltpu.CompilerParams(
            collective_id=0, has_side_effects=True, vmem_limit_bytes=58 * 2**20
        ),
        name="layer",
    )(*given.values())
    done = [pltpu.with_memory_space_constraint(one, pltpu.VMEM) for one in done]
    *wout, out, own, text, small_sum = done
    part = dim // (2 * n_seq)
    few = NB // (2 * n_seq)
    shapes = [
        ((1, rows, dim), bf16), ((1, rows, dim), f32), ((1, part), f32), ((block, width), f32), ((block, width), f32),
        ((block, width), f32), ((width, block), f32), ((few, heads), f32), ((1, part), f32), ((ff, block), f32),
        ((ff, block), f32), ((ff, block), f32),
    ]
    outs = pl.pallas_call(
        functools.partial(finish, n_seq, heads, width),
        out_shape=[jax.ShapeDtypeStruct(*spec) for spec in shapes],
        in_specs=[vmem] * 13,
        out_specs=[vmem] * 12,
        scratch_shapes=[pltpu.VMEM((128, 8), f32)],
        compiler_params=pltpu.CompilerParams(vmem_limit_bytes=16 * 2**20),
        name="finish",
    )(
        text_patches, patch_valid, own, text, out, *wout, small_sum
    )
    outs = list(outs)
    for i in (9, 10):
        outs[i] = outs[i].T
    outs[2] = outs[2].reshape(part)
    outs[8] = outs[8].reshape(part)
    return tuple(outs)


def solution(mesh):
    group = ("mod", "seq")
    in_specs = (
        P("mod", "seq", None), P("seq", None), P("seq", None), P("seq", None), P(), P(), P(None, "mp"), P(None, "mp"),
        P(None, "mp"), P("mp", None), P(None, "mp"), P(), P(None, "mp"), P(None, "mp"), P("mp", None),
        P("mod", "seq", None),
    )
    out_specs = (
        P("mod", "seq", None), P("mod", "seq", None), P(group), P(group, "mp"), P(group, "mp"), P(group, "mp"),
        P("mp", group), P(group, "mp"), P(group), P(group, "mp"), P(group, "mp"), P("mp", group),
    )
    body = functools.partial(per_device, mesh.shape["seq"], mesh.shape["mp"])
    return jax.shard_map(body, mesh=mesh, in_specs=in_specs, out_specs=out_specs, check_vma=False)
```

```python
import functools
import types

import jax
import jax.numpy as jnp
from jax import lax
from jax.experimental import pallas as pl
from jax.experimental.pallas import tpu as pltpu
from jax.sharding import PartitionSpec as P

MESH = pl.DeviceIdType.MESH
EPS = 1e-06
PARTS = 2
ROOT = 0.7978845608028654
HEAD = 64
NB = 32
PDOC = 128
LONG = 192
SPANS = 640
WIDE = 896
f32 = jnp.float32
bf16 = jnp.bfloat16


def nn(a, b):
    return jnp.dot(a, b, preferred_element_type=f32)


def nt(a, b):
    return lax.dot_general(a, b, (((1,), (1,)), ((), ())), preferred_element_type=f32)


def rms_scale(x):
    return lax.rsqrt(jnp.mean(x * x, axis=-1, keepdims=True) + EPS)


def row_chunks(first, total, step, body):
    def one(i, carry):
        body(pl.ds(pl.multiple_of(first + i * step, step), step))
        return carry

    lax.fori_loop(0, total // step, one, 0)


def bucket_hot(ids_row):
    return (lax.broadcasted_iota(jnp.int32, (NB, SPANS), 0) == ids_row).astype(f32)


def patch_counts(ids, valid, rows):
    places = lax.broadcasted_iota(jnp.int32, (rows, rows), 0)
    count = jnp.zeros((rows, rows), f32)
    for j in range(ids.shape[0]):
        count += jnp.where(ids[j : j + 1, :] == places, valid[j : j + 1, :].astype(f32), 0.0)
    return count


def flat(ref):
    value = ref[...].astype(f32)
    return jnp.concatenate([value[i : i + 1, :] for i in range(value.shape[0])], axis=1)


def sizes_of(heads, ff):
    width = heads * HEAD
    return (ff, ff, ff, width, width, width, width)


def mega(n_seq, n_mp, heads, order, *refs):
    ref, refs = types.SimpleNamespace(), list(refs)
    for name, many in order:
        setattr(ref, name, [refs.pop(0) for _ in range(many)] if many else refs.pop(0))
    mod, seq, mp = lax.axis_index("mod"), lax.axis_index("seq"), lax.axis_index("mp")
    rows, dim = ref.united.shape
    width = heads * HEAD
    ff = ref.wg.shape[0]
    half = dim // 2
    block = half // n_seq
    part_rows = rows // PARTS
    own_rows = part_rows // n_mp
    parts = range(PARTS)

    def part(k):
        return slice(k * part_rows, (k + 1) * part_rows)

    def share(k, who):
        return pl.ds(pl.multiple_of(k * part_rows + who * own_rows, own_rows), own_rows)

    def kept(k):
        return slice(k * own_rows, (k + 1) * own_rows)

    here = pl.ds(pl.multiple_of(mod * half, half), half)
    there = pl.ds(pl.multiple_of((1 - mod) * half, half), half)
    sibling = (1 - mod, seq, mp)
    used = [0]
    sends = []
    is_end = (seq == 0) | (seq == n_seq - 1)
    not_end = (seq > 0) & (seq < n_seq - 1)
    is_inner = (seq == 1) | (seq == n_seq - 2)
    inner = (mod, seq + 1 - 2 * (seq // (n_seq - 1)), mp)

    def when(cond, body):
        if cond is None:
            body()
        else:
            pl.when(cond)(body)

    def peer_of(o):
        if n_mp == 4:
            return (mp + 1 - 2 * (mp % 2), (mp + 2) % 4, 3 - mp)[o - 1]
        return (mp + o) % n_mp

    def source_of(o):
        if n_mp == 4:
            return peer_of(o)
        return (mp + n_mp - o) % n_mp

    def message(src, dst, device, cond=None):
        index = used[0]
        used[0] += 1
        copy = pltpu.make_async_remote_copy(
            src_ref=src,
            dst_ref=dst,
            send_sem=ref.ssem.at[index],
            recv_sem=ref.rsem.at[index],
            device_id=device,
            device_id_type=MESH,
        )
        sends.append((cond, copy))
        return copy

    loads = types.SimpleNamespace()
    pairs = (
        (ref.inp_h.at[0], ref.inp), (ref.pb_h, ref.pb), (ref.tp_h, ref.tp), (ref.pv_h, ref.pv),
        (ref.ag_h, ref.ag), (ref.wk_h, ref.wk), (ref.wv_h, ref.wv), (ref.wq_h, ref.wq), (ref.cot_h.at[0], ref.cot),
        (ref.wo_h, ref.wo), (ref.wd_h, ref.wd), (ref.fg_h, ref.fg), (ref.wg_h, ref.wg), (ref.wu_h, ref.wu),
    )
    copies = [pltpu.make_async_copy(src, dst, ref.lsem.at[i]) for i, (src, dst) in enumerate(pairs)]
    for copy in copies:
        copy.start()
    (loads.inp, loads.pb, loads.tp, loads.pv, loads.ag, loads.wk, loads.wv, loads.wq, loads.cot, loads.wo,
     loads.wd, loads.fg, loads.wg, loads.wu) = copies

    barrier = pltpu.get_barrier_semaphore()
    pl.semaphore_signal(barrier, 1, device_id=sibling, device_id_type=MESH)
    for o in range(1, n_mp):
        pl.semaphore_signal(barrier, 1, device_id=(mod, seq, peer_of(o)), device_id_type=MESH)

    for o in range(1, n_seq):
        pl.semaphore_signal(barrier, 1, device_id=(mod, (seq + o) % n_seq, mp), device_id_type=MESH)
    pl.semaphore_wait(barrier, n_mp + n_seq - 1)

    to_text = message(ref.inp_h.at[0], ref.inc, sibling, mod == 0)

    @pl.when(mod == 0)
    def _():
        to_text.start()

    cot_end = message(ref.cot_h.at[0], ref.cot_e, inner, is_end)
    when(is_end, cot_end.start)

    first = ref.len_s[0, 0]
    long_first = first == LONG
    loads.pb.wait()
    mirror = (
        lax.broadcasted_iota(jnp.int32, (128, 128), 0) + lax.broadcasted_iota(jnp.int32, (128, 128), 1) == 127
    ).astype(f32)
    places = lax.broadcasted_iota(jnp.int32, (8, 128), 0) * 128 + lax.broadcasted_iota(jnp.int32, (8, 128), 1)
    span = ref.ids_s.shape[0]
    stride = 9 if span % 9 == 0 else 1

    def set_ids(i, ids):
        for k in range(stride):
            ids = jnp.where(places == i * stride + k, ref.ids_s[i * stride + k], ids)
        return ids

    ids = lax.fori_loop(0, span // stride, set_ids, jnp.zeros((8, 128), jnp.int32))
    turned_ids = nn(ids.astype(f32).astype(bf16), mirror.astype(bf16))
    lines = SPANS // 128
    turned_ids = jnp.concatenate([turned_ids[i : i + 1, :] for i in reversed(range(lines))], axis=1)
    hot = bucket_hot(turned_ids.astype(jnp.int32))
    ref.hot[...] = hot
    rel = jnp.dot(ref.pb[...], hot, precision=lax.Precision.HIGHEST, preferred_element_type=f32)
    rel = jnp.concatenate([rel, jnp.zeros((heads, WIDE - SPANS), f32)], axis=1)
    blocks = rows // 64
    apart = ((-128, -128), (-128, -192), (-128, -192), (-64, -192))
    along = ((128, 128), (128, 128), (64, 192), (64, 192))

    def window(c):
        return pltpu.roll(rel, (WIDE - (c + 256)) % WIDE, 1)[:, :384]

    lane_row = lax.broadcasted_iota(jnp.int32, (1, rows), 1)
    patch_doc = lane_row // PDOC
    text_doc = (lane_row >= first).astype(jnp.int32)
    query_doc = jnp.where(mod == 0, patch_doc, text_doc)
    for kb in range(blocks):
        ref.win[kb] = window(-64 * kb)
        a0, a1 = (window(c - 64 * kb) for c in apart[kb])
        b0, b1 = (window(c - 64 * kb) for c in along[kb])
        ref.win[blocks + kb] = jnp.where(
            mod == 0, jnp.where(long_first, a0, a1), jnp.where(long_first, b0, b1)
        )
    for kb in range(2 * blocks):
        at = kb % blocks
        in_patch = (mod == 0) if kb < blocks else (mod == 1)
        key_doc = jnp.where(in_patch, at * 64 // PDOC, jnp.where(at * 64 >= first, 1, 0))
        same = query_doc == key_doc

        def one_bias(h, carry, kb=kb, same=same):
            line = jnp.broadcast_to(ref.win[kb, pl.ds(h, 1), :], (64, 384))
            table = pltpu.roll(line, 320, 1, stride=1, stride_axis=0)[:, :rows]
            ref.prob[h, kb * 64 : kb * 64 + 64, :] = jnp.where(same, table, -1000000000.0)
            return carry

        lax.fori_loop(0, heads, one_bias, 0)

    loads.cot.wait()

    def transposed(source, sides, cond=None):
        copy = message(sides.s, sides.r, sibling, cond)

        def body():
            sides.s[...] = source[:, there].T
            copy.start()
            sides.t[...] = source[:, here].T

        when(cond, body)
        return copy

    x_tan, x_na, x_nf, x_branch, x_tan_e, x_nf_e = (
        types.SimpleNamespace(t=ref.xt.at[i], s=ref.xs.at[i], r=ref.xr.at[i]) for i in range(6)
    )
    tan_sent = transposed(ref.cot, x_tan, not_end)

    loads.tp.wait()
    loads.pv.wait()
    loads.inp.wait()

    @pl.when(mod == 1)
    def _():
        count = patch_counts(ref.tp[...], ref.pv[...], rows).T.astype(bf16)
        to_text.wait_recv()
        ref.united[...] = nn(count, ref.inc[...])

    @pl.when(mod == 0)
    def _():
        ref.united[...] = jnp.zeros((rows, dim), f32)

    loads.ag.wait()
    attn_gain = flat(ref.ag)

    def first_norm(at):
        u = ref.united[at, :] + ref.inp[at, :].astype(f32)
        ref.united[at, :] = u
        ref.na[at, :] = (u * rms_scale(u) * attn_gain).astype(bf16)

    row_chunks(0, rows, 32, first_norm)
    loads.wk.wait()
    ref.kv[:, :width] = nn(ref.na[...], ref.wk[...]).astype(bf16)
    loads.wv.wait()
    ref.kv[:, width:] = nn(ref.na[...], ref.wv[...]).astype(bf16)
    kv_sent = message(ref.kv, ref.kvr, sibling)
    kv_sent.start()
    loads.wq.wait()
    ref.q[...] = nn(ref.na[...], ref.wq[...]).astype(bf16)
    ref.kvt[:, :rows] = ref.kv[...].T
    na_sent = transposed(ref.na, x_na)
    kv_sent.wait_recv()
    ref.kvt[:, rows:] = ref.kvr[...].T
    head_of = lax.broadcasted_iota(jnp.int32, (1, width), 1) // HEAD

    def head_mask(h):
        return (head_of == h).astype(f32).astype(bf16)

    def head_rows(h, base=0):
        return pl.ds(pl.multiple_of(base + h * HEAD, HEAD), HEAD)

    def head_fwd(k, h, carry):
        at = part(k)
        qm = ref.q[at, :] * head_mask(h)
        ref.qm[h, at, :] = qm
        s0 = nt(ref.kv[:, :width], qm) * 0.125 + ref.prob[h, :rows, at]
        s1 = nt(ref.kvr[:, :width], qm) * 0.125 + ref.prob[h, rows:, at]
        top = jnp.maximum(jnp.max(s0, axis=0, keepdims=True), jnp.max(s1, axis=0, keepdims=True))
        e0 = jnp.exp(s0 - top)
        e1 = jnp.exp(s1 - top)
        total = jnp.sum(e0, axis=0, keepdims=True) + jnp.sum(e1, axis=0, keepdims=True)
        scale = 1.0 / total
        p0 = e0 * scale
        p1 = e1 * scale
        ref.prob[h, :rows, at] = p0
        ref.prob[h, rows:, at] = p1
        values_t = ref.kvt[head_rows(h, width), :]
        ref.att_t[head_rows(h), at] = nn(values_t[:, :rows], p0.astype(bf16)) + nn(
            values_t[:, rows:], p1.astype(bf16)
        )
        return carry

    def scatter(c, k, product, hold=False):
        ref.part[part(k), :] = product
        ref.stage[c, part(k), :] = product.astype(bf16)
        copies = []
        for o in range(n_mp - 1, 0, -1):
            to = peer_of(o)
            copies.append(message(ref.stage.at[c, share(k, to)], ref.land.at[c, k, o - 1], (mod, seq, to)))
            if not hold:
                copies[-1].start()
        ref.keep[c, kept(k), :] = ref.part[share(k, mp), :]
        return copies

    def summed(c, k, copies):
        for copy in copies:
            copy.wait_recv()
        total = ref.keep[c, kept(k), :]
        for o in range(1, n_mp):
            total += ref.land[c, k, o - 1].astype(f32)
        return total

    def gather(c, k):
        at = ref.whole.at[c, share(k, mp)]
        copies = [message(at, at, (mod, seq, peer_of(o))) for o in range(1, n_mp)]
        for copy in reversed(copies):
            copy.start()
        return copies

    loads.wo.wait()
    attn_sum = []
    for k in parts:
        lax.fori_loop(0, heads, functools.partial(head_fwd, k), 0)
        ref.att[part(k), :] = ref.att_t[:, part(k)].T.astype(bf16)
        attn_sum.append(scatter(0, k, nn(ref.att[part(k), :], ref.wo[...])))
    att_sent = message(ref.att, ref.att_r, sibling)
    att_sent.start()
    loads.wd.wait()
    ref.hg[...] = nt(ref.cot[...], ref.wd[...])
    loads.fg.wait()
    ffn_gain = flat(ref.fg)
    nf_end = []

    def to_inner(k, who):
        at = share(k, who)
        copy = message(ref.whole.at[0, at], ref.nf_e.at[at], inner, is_end)
        when(is_end, copy.start)
        nf_end.append(copy)

    nf_parts = []
    for k in parts:
        middle = ref.united[share(k, mp), :] + summed(0, k, attn_sum[k])
        ref.mid[kept(k), :] = middle
        ref.whole[0, share(k, mp), :] = (middle * rms_scale(middle) * ffn_gain).astype(bf16)
        nf_parts.append(gather(0, k))
        to_inner(k, mp)
    tan_e_sent = message(x_tan_e.s, x_tan_e.r, sibling, is_inner)

    @pl.when(is_inner)
    def _():
        cot_end.wait_recv()
        x_tan_e.s[...] = ref.cot_e[:, there].T
        tan_e_sent.start()
        x_tan_e.t[...] = ref.cot_e[:, here].T
        ref.hg_e[...] = nt(ref.cot_e[...], ref.wd[...])

    loads.wg.wait()
    loads.wu.wait()

    def gelu_rows(at, back_ref=ref.hg, hid=ref.hid, gg=ref.gg, ug=ref.ug):
        g, u, back = ref.gate[at, :], ref.up[at, :], back_ref[at, :]
        squared = g * g
        t = jnp.tanh(ROOT * (g + 0.044715 * squared * g))
        left = 0.5 * (1.0 + t)
        gelu = left * g
        slope = left + 0.5 * g * (1.0 - t * t) * (ROOT * (1.0 + 0.134145 * squared))
        hid[at, :] = (gelu * u).astype(bf16)
        gg[at, :] = (back * u * slope).astype(bf16)
        ug[at, :] = (back * gelu).astype(bf16)

    ffn_in = []
    for k in parts:
        for o, copy in enumerate(nf_parts[k], 1):
            copy.wait_recv()
            to_inner(k, source_of(o))
        at = part(k)
        ref.gate[at, :] = nt(ref.whole[0, at, :], ref.wg[...])
        ref.up[at, :] = nt(ref.whole[0, at, :], ref.wu[...])
        row_chunks(k * part_rows, part_rows, 32, gelu_rows)
        ffn_in.append(scatter(1, k, nn(ref.gg[at, :], ref.wg[...]) + nn(ref.ug[at, :], ref.wu[...])))
    hid_sent = message(ref.hid, ref.hid_r, sibling, not_end)
    gg_sent = message(ref.gg, ref.gg_r, sibling, not_end)
    ug_sent = message(ref.ug, ref.ug_r, sibling, not_end)
    when(not_end, hid_sent.start)
    nf_sent = transposed(ref.whole.at[0], x_nf, not_end)
    when(not_end, gg_sent.start)
    when(not_end, ug_sent.start)

    after = (mod, jnp.minimum(seq + 1, n_seq - 1), mp)
    before = (mod, jnp.maximum(seq - 1, 0), mp)
    weights = []
    ends = (1, 1, 1, 0, 0, 0, 0)
    for e, g, s, a, b, o in zip(ends, ref.wgrad, ref.wsend, ref.wleft, ref.wright, ref.wout, strict=True):
        right, left = {}, {}
        for j in range(n_seq):
            rng = pl.ds(j * block, block)
            if j > e:
                right[j] = message(s.at[rng], a.at[rng], after, (seq >= e) & (seq < j))
            if j < n_seq - 1 - e:
                left[j] = message(s.at[rng], b.at[rng], before, (seq < n_seq - e) & (seq > j))
        weights.append(types.SimpleNamespace(e=e, g=g, s=s, a=a, b=b, o=o, right=right, left=left))
    w_down, w_gate, w_up, w_proj, w_q, w_k, w_v = weights

    def product(w, x, pieces, more=False):
        lo = 0
        for own, other in pieces:
            size = own.shape[1]
            both = nn(x.t[...], own[...]) + nn(x.r[...], other[...])
            if more:
                both += w.g[:, lo : lo + size]
            w.g[:, lo : lo + size] = both
            lo += size

    def hop(group, step, some=slice(None)):
        edge = group[0].e + step
        if edge >= n_seq - 1:
            return

        @pl.when(seq == edge)
        def _():
            for j in list(range(n_seq - 1, edge, -1))[some]:
                rng = slice(j * block, (j + 1) * block)
                for w in group:
                    value = w.g[rng, :]
                    if step > 0:
                        w.right[j].wait_recv()
                        value += w.a[rng, :].astype(f32)
                    w.s[rng, :] = value.astype(bf16)
                    w.right[j].start()

        @pl.when(seq == n_seq - 1 - edge)
        def _():
            for j in list(range(n_seq - 1 - edge))[some]:
                rng = slice(j * block, (j + 1) * block)
                for w in group:
                    value = w.g[rng, :]
                    if step > 0:
                        w.left[j].wait_recv()
                        value += w.b[rng, :].astype(f32)
                    w.s[rng, :] = value.astype(bf16)
                    w.left[j].start()

    def arrive(w):
        for j in range(n_seq):

            @pl.when(seq == j)
            def _(j=j):
                rng = slice(j * block, (j + 1) * block)
                value = w.g[rng, :] if w.e <= j < n_seq - w.e else jnp.zeros(w.o.shape, f32)
                if j > w.e:
                    w.right[j].wait_recv()
                    value += w.a[rng, :].astype(f32)
                if j < n_seq - 1 - w.e:
                    w.left[j].wait_recv()
                    value += w.b[rng, :].astype(f32)
                w.o[...] = value

    gain_sums = []
    branch_parts = []

    def middle_back(k):
        normed_grad = summed(1, k, ffn_in[k])
        middle = ref.mid[kept(k), :]
        scale = rms_scale(middle)
        spread = normed_grad * ffn_gain
        gain_sums.append(jnp.sum(normed_grad * middle * scale, axis=0, keepdims=True))
        middle_grad = (
            ref.cot[share(k, mp), :].astype(f32)
            + scale * spread
            - middle * (scale * scale * scale) * jnp.mean(spread * middle, axis=-1, keepdims=True)
        )
        ref.mgrad[kept(k), :] = middle_grad
        ref.whole[1, share(k, mp), :] = middle_grad.astype(bf16)
        branch_parts.append(gather(1, k))

    hid_e_sent = message(ref.hid_e, ref.hid_er, sibling, is_inner)
    gg_e_sent = message(ref.gg_e, ref.gg_er, sibling, is_inner)
    ug_e_sent = message(ref.ug_e, ref.ug_er, sibling, is_inner)
    nf_e_sent = message(x_nf_e.s, x_nf_e.r, sibling, is_inner)

    @pl.when(not_end)
    def _():
        hid_sent.wait_recv()
        tan_sent.wait_recv()
        product(w_down, x_tan, [(ref.hid, ref.hid_r)])
        nf_sent.wait_recv()
        gg_sent.wait_recv()
        product(w_gate, x_nf, [(ref.gg, ref.gg_r)])
        ug_sent.wait_recv()
        product(w_up, x_nf, [(ref.ug, ref.ug_r)])

    middle_back(0)
    @pl.when(is_inner)
    def _():
        for copy in nf_end:
            copy.wait_recv()
        ref.gate[...] = nt(ref.nf_e[...], ref.wg[...])
        ref.up[...] = nt(ref.nf_e[...], ref.wu[...])
        row_chunks(0, rows, 32, lambda at: gelu_rows(at, ref.hg_e, ref.hid_e, ref.gg_e, ref.ug_e))
        hid_e_sent.start()
        x_nf_e.s[...] = ref.nf_e[:, there].T
        nf_e_sent.start()
        gg_e_sent.start()
        ug_e_sent.start()
        x_nf_e.t[...] = ref.nf_e[:, here].T


    for k in parts[1:]:
        middle_back(k)

    def end_products(w, x, pieces, needs):
        @pl.when(is_inner)
        def _():
            for copy in needs:
                copy.wait_recv()
            product(w, x, pieces, more=True)

        hop([w], 0, slice(0, 1))

    end_products(w_down, x_tan_e, [(ref.hid_e, ref.hid_er)], (hid_e_sent, tan_e_sent))
    end_products(w_gate, x_nf_e, [(ref.gg_e, ref.gg_er)], (gg_e_sent, nf_e_sent))
    end_products(w_up, x_nf_e, [(ref.ug_e, ref.ug_er)], (ug_e_sent,))
    hop([w_down, w_gate, w_up], 0, slice(1, None))
    ffn_out = [scatter(2, k, nn(ref.hid[part(k), :], ref.wd[...]), hold=True) for k in parts]

    flip = (
        lax.broadcasted_iota(jnp.int32, (rows, rows), 0) // 64 == lax.broadcasted_iota(jnp.int32, (rows, rows), 1) // 64
    ) & (
        lax.broadcasted_iota(jnp.int32, (rows, rows), 0) % 64
        + lax.broadcasted_iota(jnp.int32, (rows, rows), 1) % 64
        == 63
    )
    ref.turn[...] = flip.astype(f32).astype(bf16)
    ref.dk[...] = jnp.zeros((2 * rows, width), f32)
    ref.dv[...] = jnp.zeros((2 * rows, width), f32)

    def head_bwd(k, h, carry):
        a = part(k)
        gm = ref.ga[a, :] * head_mask(h)
        p0, p1 = ref.prob[h, :rows, a], ref.prob[h, rows:, a]
        d0 = nt(ref.kv[:, width:], gm)
        d1 = nt(ref.kvr[:, width:], gm)
        inner_sum = jnp.sum(p0 * d0, axis=0, keepdims=True) + jnp.sum(p1 * d1, axis=0, keepdims=True)
        g0 = (p0 * (d0 - inner_sum)).astype(bf16)
        g1 = (p1 * (d1 - inner_sum)).astype(bf16)
        keys_t = ref.kvt[head_rows(h), :]
        ref.dq_t[head_rows(h), a] = nn(keys_t[:, :rows], g0) + nn(keys_t[:, rows:], g1)
        qm = ref.qm[h, a, :]
        ref.dk[:rows, :] += nn(g0, qm)
        ref.dk[rows:, :] += nn(g1, qm)
        ref.dv[:rows, :] += nn(p0.astype(bf16), gm)
        ref.dv[rows:, :] += nn(p1.astype(bf16), gm)
        turn = ref.turn[...]
        low, wide = k * part_rows, part_rows + 128
        for side, g in ((0, g0), (1, g1)):
            turned = nn(turn, g)
            for at in range(blocks):
                piece = turned[at * 64 : at * 64 + 64, :]
                piece = jnp.concatenate([piece, jnp.zeros((64, 128), f32)], axis=1)
                piece = pltpu.roll(piece, 1, 1, stride=1, stride_axis=0)
                ref.diag[side * blocks + at, pl.ds(h, 1), low : low + wide] += jnp.sum(piece, axis=0, keepdims=True)
        return carry

    ref.diag[...] = jnp.zeros(ref.diag.shape, f32)
    for k in parts:
        for copy in branch_parts[k]:
            copy.wait_recv()
        ref.ga[part(k), :] = nt(ref.whole[1, part(k), :], ref.wo[...]).astype(bf16)
        if k == PARTS - 1:
            for copies in ffn_out:
                for copy in copies:
                    copy.start()
        lax.fori_loop(0, heads, functools.partial(head_bwd, k), 0)
    ref.kvg_s[:, :width] = (ref.dk[rows:, :] * 0.125).astype(bf16)
    ref.kvg_s[:, width:] = ref.dv[rows:, :].astype(bf16)
    kvg_sent = message(ref.kvg_s, ref.kvg_r, sibling)
    kvg_sent.start()
    branch_sent = transposed(ref.whole.at[1], x_branch)
    ref.dqb[...] = (ref.dq_t[...].T * 0.125).astype(bf16)
    dq_sent = message(ref.dqb, ref.dq_r, sibling)
    dq_sent.start()
    att_sent.wait_recv()
    branch_sent.wait_recv()
    product(w_proj, x_branch, [(ref.att, ref.att_r)])
    hop([w_proj], 0)
    hop([w_down, w_gate], 1)
    na_sent.wait_recv()
    dq_sent.wait_recv()
    product(w_q, x_na, [(ref.dqb, ref.dq_r)])
    hop([w_q], 0)
    kvg_sent.wait_recv()
    ref.dkb[...] = (ref.dk[:rows, :] * 0.125 + ref.kvg_r[:, :width].astype(f32)).astype(bf16)
    ref.dvb[...] = (ref.dv[:rows, :] + ref.kvg_r[:, width:].astype(f32)).astype(bf16)
    dk_sent = message(ref.dkb, ref.dk_r, sibling)
    dv_sent = message(ref.dvb, ref.dv_r, sibling)
    for copy in (dk_sent, dv_sent):
        copy.start()
    attn_in = []
    for k in parts:
        at = part(k)
        rows_in = nt(ref.dqb[at, :], ref.wq[...]) + nt(ref.dkb[at, :], ref.wk[...]) + nt(ref.dvb[at, :], ref.wv[...])
        attn_in.append(scatter(3, k, rows_in))
    for copy in (dk_sent, dv_sent):
        copy.wait_recv()
    product(w_k, x_na, [(ref.dkb, ref.dk_r)])
    product(w_v, x_na, [(ref.dvb, ref.dv_r)])
    hop([w_k, w_v], 0)
    hop([w_up], 1)

    def gain_rows(i, total):
        at = pl.ds(pl.multiple_of(i * 32, 32), 32)
        u = ref.united[at, :]
        return total + jnp.sum(ref.part[at, :] * u * rms_scale(u), axis=0, keepdims=True)

    attn_gain_grad = lax.fori_loop(0, rows // 32, gain_rows, jnp.zeros((1, dim), f32))

    def unwindow(piece, c):
        grown = jnp.concatenate([piece, jnp.zeros((heads, WIDE - 384), f32)], axis=1)
        return pltpu.roll(grown, (c + 256) % WIDE, 1)

    total = jnp.zeros((heads, WIDE), f32)
    for kb in range(blocks):
        total += unwindow(ref.diag[kb], -64 * kb)
        piece = ref.diag[blocks + kb]
        a0, a1 = (unwindow(piece, c - 64 * kb) for c in apart[kb])
        b0, b1 = (unwindow(piece, c - 64 * kb) for c in along[kb])
        total += jnp.where(mod == 0, jnp.where(long_first, a0, a1), jnp.where(long_first, b0, b1))
    bias_grad = lax.dot_general(
        total[:, :SPANS], ref.hot[...], (((1,), (1,)), ((), ())), precision=lax.Precision.HIGHEST, preferred_element_type=f32
    )
    quarter = dim // 4
    for i, line in enumerate((attn_gain_grad, sum(gain_sums))):
        for k in range(4):
            ref.small[4 * i + k : 4 * i + k + 1, :quarter] = line[:, k * quarter : (k + 1) * quarter]
    ref.small[:, quarter:] = jnp.zeros((8, 128), f32)
    ref.small[:heads, quarter : quarter + NB] = bias_grad
    small_mp = [message(ref.small, ref.small_p.at[o - 1], (mod, seq, peer_of(o))) for o in range(1, n_mp)]
    for copy in small_mp:
        copy.start()

    hop([w_proj, w_q], 1)
    for copy in small_mp:
        copy.wait_recv()
    gains = ref.small[:, :quarter]
    for o in range(1, n_mp):
        gains += ref.small_p[o - 1, :, :quarter]
    ref.small2[:, :quarter] = gains
    ref.small2[:, quarter:] = ref.small[:, quarter:]
    small_mod = message(ref.small2, ref.small_m, sibling)
    small_mod.start()

    united_parts = []
    for k in parts:
        normed_grad = summed(3, k, attn_in[k])
        u = ref.united[share(k, mp), :]
        scale = rms_scale(u)
        spread = normed_grad * attn_gain
        united_grad = (
            ref.mgrad[kept(k), :]
            + scale * spread
            - u * (scale * scale * scale) * jnp.mean(spread * u, axis=-1, keepdims=True)
        )
        ref.whole[3, share(k, mp), :] = united_grad.astype(bf16)
        united_parts.append(gather(3, k))
    output_parts = []
    for k in parts:
        ref.whole[2, share(k, mp), :] = (ref.mid[kept(k), :] + summed(2, k, ffn_out[k])).astype(bf16)
        output_parts.append(gather(2, k))
    hop([w_k, w_v], 1)
    small_mod.wait_recv()
    ref.small3[...] = ref.small2[...] + ref.small_m[...]
    small_seq = [
        message(ref.small3, ref.small_q.at[o - 1], (mod, (seq + o) % n_seq, mp)) for o in range(1, n_seq)
    ]
    for copy in small_seq:
        copy.start()
    backs = []
    for k in parts:
        for o in range(n_mp):
            at = share(k, source_of(o) if o else mp)
            if o:
                united_parts[k][o - 1].wait_recv()
            back = message(ref.whole.at[3, at], ref.text_o.at[at], sibling, mod == 1)
            when(mod == 1, back.start)
            backs.append(back)
    for step in range(2, n_seq - 1):
        hop([w_down, w_gate, w_up], step)
        hop([w_proj, w_q], step)
        hop([w_k, w_v], step)
    for copies in output_parts:
        for copy in copies:
            copy.wait_recv()
    ref.out_o[...] = ref.whole[2]
    ref.own_o[...] = ref.whole[3]
    for w in weights:
        arrive(w)

    total = ref.small3[...]
    for i, copy in enumerate(small_seq):
        copy.wait_recv()
        total += ref.small_q[i]
    ref.small_o[...] = total

    @pl.when(mod == 0)
    def _():
        for back in backs:
            back.wait_recv()

    @pl.when(mod == 1)
    def _():
        ref.text_o[...] = jnp.zeros((rows, dim), bf16)

    for cond, copy in sends:
        if cond is None:
            copy.wait_send()
        else:

            @pl.when(cond)
            def _(copy=copy):
                copy.wait_send()

    assert used[0] <= ref.ssem.shape[0]


def finish(n_seq, heads, width, ids, valid, own, text, out, gd, gg, gu, go, gq, gk, gv, small,
           o_out, o_in, o_ag, o_q, o_k, o_v, o_o, o_pb, o_fg, o_gate, o_up, o_down, hold):
    mod, seq = lax.axis_index("mod"), lax.axis_index("seq")
    rows, dim = own.shape
    place = mod * n_seq + seq
    o_out[0] = out[...]

    @pl.when(mod == 0)
    def _():
        count = patch_counts(ids[...], valid[...], rows)
        o_in[0] = own[...].astype(f32) + nn(count.astype(bf16), text[...])

    @pl.when(mod == 1)
    def _():
        o_in[0] = own[...].astype(f32)

    o_q[...] = gq[...]
    o_k[...] = gk[...]
    o_v[...] = gv[...]
    o_o[...] = go[...].T
    o_gate[...] = gg[...].T
    o_up[...] = gu[...].T
    o_down[...] = gd[...].T
    quarter = dim // 4
    part = dim // (2 * n_seq)
    for i, o_gain in enumerate((o_ag, o_fg)):
        line = jnp.concatenate([small[4 * i + k : 4 * i + k + 1, :quarter] for k in range(4)], axis=1)
        line = pltpu.roll(jnp.broadcast_to(line, (8, dim)), dim - place * part, 1)
        o_gain[...] = line[:1, :part]
    few = NB // (2 * n_seq)
    hold[...] = small[:, quarter:].T
    o_pb[...] = hold[pl.ds(place * few, few), :heads]


def per_device(n_seq, n_mp, *args):
    (inputs, text_patches, patch_valid, text_lengths, bucket_table, attn_gain, query_weight, key_weight,
     value_weight, output_weight, position_bias, ffn_gain, gate_weight, up_weight, down_weight, cotangent) = args
    rows, dim = inputs.shape[1:]
    heads = position_bias.shape[1]
    width = heads * HEAD
    ff = down_weight.shape[0]
    own_rows = rows // n_mp
    half = dim // 2
    block = half // n_seq
    text_patches, patch_valid, position_bias = text_patches.T, patch_valid.T, position_bias.T
    gate_weight, up_weight = gate_weight.T, up_weight.T
    given = dict(
        len_s=text_lengths, ids_s=bucket_table, inp_h=inputs, tp_h=text_patches, pv_h=patch_valid, pb_h=position_bias,
        ag_h=attn_gain.reshape(dim // 128, 128), fg_h=ffn_gain.reshape(dim // 128, 128), wq_h=query_weight, wk_h=key_weight,
        wv_h=value_weight, wo_h=output_weight, wg_h=gate_weight, wu_h=up_weight, wd_h=down_weight, cot_h=cotangent,
    )
    sizes = sizes_of(heads, ff)
    results = dict(
        wout=[((block, size), f32) for size in sizes], out_o=((rows, dim), bf16), own_o=((rows, dim), bf16),
        text_o=((rows, dim), bf16), small_o=((8, dim // 4 + 128), f32),
    )
    small = ((8, dim // 4 + 128), f32)
    sent = [((half, size), bf16) for size in sizes]
    held = dict(
        inp=((rows, dim), bf16), hot=((NB, SPANS), f32), pb=((heads, NB), f32), tp=(text_patches.shape, jnp.int32),
        pv=(patch_valid.shape, jnp.int32), ag=((dim // 128, 128), bf16), fg=((dim // 128, 128), bf16), wq=((dim, width), bf16),
        wk=((dim, width), bf16), wv=((dim, width), bf16), wo=((width, dim), bf16), wg=((ff, dim), bf16),
        wu=((ff, dim), bf16), wd=((ff, dim), bf16), cot=((rows, dim), bf16), inc=((rows, dim), bf16),
        win=((2 * rows // 64, heads, 384), f32), diag=((2 * rows // 64, heads, 384), f32),
        prob=((heads, 2 * rows, rows), f32), xt=((6, half, rows), bf16), xs=((6, half, rows), bf16), xr=((6, half, rows), bf16),
        united=((rows, dim), f32), na=((rows, dim), bf16),
        kv=((rows, 2 * width), bf16), kvr=((rows, 2 * width), bf16), kvt=((2 * width, 2 * rows), bf16),
        q=((rows, width), bf16), qm=((heads, rows, width), bf16), att_t=((width, rows), f32), att=((rows, width), bf16),
        att_r=((rows, width), bf16), part=((rows, dim), f32), stage=((4, rows, dim), bf16),
        land=((4, PARTS, n_mp - 1, own_rows // PARTS, dim), bf16), keep=((4, own_rows, dim), f32), whole=((4, rows, dim), bf16),
        cot_e=((rows, dim), bf16), nf_e=((rows, dim), bf16), hg_e=((rows, ff), f32), hid_e=((rows, ff), bf16),
        hid_er=((rows, ff), bf16), gg_e=((rows, ff), bf16), gg_er=((rows, ff), bf16), ug_e=((rows, ff), bf16),
        ug_er=((rows, ff), bf16), hg=((rows, ff), f32), mid=((own_rows, dim), f32), mgrad=((own_rows, dim), f32), gate=((rows, ff), f32),
        up=((rows, ff), f32), ga=((rows, width), bf16), turn=((rows, rows), bf16), dk=((2 * rows, width), f32),
        dv=((2 * rows, width), f32), dq_t=((width, rows), f32), kvg_s=((rows, 2 * width), bf16),
        kvg_r=((rows, 2 * width), bf16),
    )
    held.update(
        hid=((rows, ff), bf16), hid_r=((rows, ff), bf16), gg=((rows, ff), bf16), gg_r=((rows, ff), bf16),
        ug=((rows, ff), bf16), ug_r=((rows, ff), bf16), dqb=((rows, width), bf16), dq_r=((rows, width), bf16),
        dkb=((rows, width), bf16), dk_r=((rows, width), bf16), dvb=((rows, width), bf16), dv_r=((rows, width), bf16),
        wgrad=[((half, size), f32) for size in sizes], wsend=sent, wleft=sent, wright=sent, small=small, small2=small,
        small3=small, small_m=small, small_q=((n_seq - 1,) + small[0], f32),
        small_p=((n_mp - 1,) + small[0], f32),
    )
    count = 60 + 20 * n_mp + 14 * n_seq
    order = [(name, 0) for name in given]
    out_shape, scratch = [], []
    for specs, into, make in ((results, out_shape, pltpu.VMEM), (held, scratch, pltpu.VMEM)):
        for name, spec in specs.items():
            many = spec if isinstance(spec, list) else [spec]
            order.append((name, len(many) if isinstance(spec, list) else 0))
            into.extend(make(*one) for one in many)
    for i, size in enumerate((count, count, len(given) - 2)):
        order.append((("ssem", "rsem", "lsem")[i], 0))
        scratch.append(pltpu.SemaphoreType.DMA((size,)))
    vmem = pl.BlockSpec(memory_space=pltpu.VMEM)
    done = pl.pallas_call(
        functools.partial(mega, n_seq, n_mp, heads, order),
        out_shape=out_shape,
        in_specs=[pl.BlockSpec(memory_space=pltpu.SMEM)] * 2 + [pl.BlockSpec(memory_space=pl.ANY)] * (len(given) - 2),
        scratch_shapes=scratch,
        compiler_params=pltpu.CompilerParams(
            collective_id=0, has_side_effects=True, vmem_limit_bytes=58 * 2**20
        ),
        name="layer",
    )(*given.values())
    done = [pltpu.with_memory_space_constraint(one, pltpu.VMEM) for one in done]
    *wout, out, own, text, small_sum = done
    part = dim // (2 * n_seq)
    few = NB // (2 * n_seq)
    shapes = [
        ((1, rows, dim), bf16), ((1, rows, dim), f32), ((1, part), f32), ((block, width), f32), ((block, width), f32),
        ((block, width), f32), ((width, block), f32), ((few, heads), f32), ((1, part), f32), ((ff, block), f32),
        ((ff, block), f32), ((ff, block), f32),
    ]
    outs = pl.pallas_call(
        functools.partial(finish, n_seq, heads, width),
        out_shape=[jax.ShapeDtypeStruct(*spec) for spec in shapes],
        in_specs=[vmem] * 13,
        out_specs=[vmem] * 12,
        scratch_shapes=[pltpu.VMEM((128, 8), f32)],
        compiler_params=pltpu.CompilerParams(vmem_limit_bytes=16 * 2**20),
        name="finish",
    )(
        text_patches, patch_valid, own, text, out, *wout, small_sum
    )
    outs = list(outs)
    for i in (9, 10):
        outs[i] = outs[i].T
    outs[2] = outs[2].reshape(part)
    outs[8] = outs[8].reshape(part)
    return tuple(outs)


def solution(mesh):
    group = ("mod", "seq")
    in_specs = (
        P("mod", "seq", None), P("seq", None), P("seq", None), P("seq", None), P(), P(), P(None, "mp"), P(None, "mp"),
        P(None, "mp"), P("mp", None), P(None, "mp"), P(), P(None, "mp"), P(None, "mp"), P("mp", None),
        P("mod", "seq", None),
    )
    out_specs = (
        P("mod", "seq", None), P("mod", "seq", None), P(group), P(group, "mp"), P(group, "mp"), P(group, "mp"),
        P("mp", group), P(group, "mp"), P(group), P(group, "mp"), P(group, "mp"), P("mp", group),
    )
    body = functools.partial(per_device, mesh.shape["seq"], mesh.shape["mp"])
    return jax.shard_map(body, mesh=mesh, in_specs=in_specs, out_specs=out_specs, check_vma=False)
```

```python
import functools
import types

import jax
import jax.numpy as jnp
from jax import lax
from jax.experimental import pallas as pl
from jax.experimental.pallas import tpu as pltpu
from jax.sharding import PartitionSpec as P

MESH = pl.DeviceIdType.MESH
EPS = 1e-06
PARTS = 2
ROOT = 0.7978845608028654
HEAD = 64
NB = 32
PDOC = 128
LONG = 192
SPANS = 640
WIDE = 896
f32 = jnp.float32
bf16 = jnp.bfloat16


def nn(a, b):
    return jnp.dot(a, b, preferred_element_type=f32)


def nt(a, b):
    return lax.dot_general(a, b, (((1,), (1,)), ((), ())), preferred_element_type=f32)


def rms_scale(x):
    return lax.rsqrt(jnp.mean(x * x, axis=-1, keepdims=True) + EPS)


def row_chunks(first, total, step, body):
    def one(i, carry):
        body(pl.ds(pl.multiple_of(first + i * step, step), step))
        return carry

    lax.fori_loop(0, total // step, one, 0)


def bucket_hot(ids_row):
    return (lax.broadcasted_iota(jnp.int32, (NB, SPANS), 0) == ids_row).astype(f32)


def patch_counts(ids, valid, rows):
    places = lax.broadcasted_iota(jnp.int32, (rows, rows), 0)
    count = jnp.zeros((rows, rows), f32)
    for j in range(ids.shape[0]):
        count += jnp.where(ids[j : j + 1, :] == places, valid[j : j + 1, :].astype(f32), 0.0)
    return count


def flat(ref):
    value = ref[...].astype(f32)
    return jnp.concatenate([value[i : i + 1, :] for i in range(value.shape[0])], axis=1)


def sizes_of(heads, ff):
    width = heads * HEAD
    return (ff, ff, ff, width, width, width, width)


def mega(n_seq, n_mp, heads, order, *refs):
    ref, refs = types.SimpleNamespace(), list(refs)
    for name, many in order:
        setattr(ref, name, [refs.pop(0) for _ in range(many)] if many else refs.pop(0))
    mod, seq, mp = lax.axis_index("mod"), lax.axis_index("seq"), lax.axis_index("mp")
    rows, dim = ref.united.shape
    width = heads * HEAD
    ff = ref.wg.shape[0]
    half = dim // 2
    block = half // n_seq
    part_rows = rows // PARTS
    own_rows = part_rows // n_mp
    parts = range(PARTS)

    def part(k):
        return slice(k * part_rows, (k + 1) * part_rows)

    def share(k, who):
        return pl.ds(pl.multiple_of(k * part_rows + who * own_rows, own_rows), own_rows)

    def kept(k):
        return slice(k * own_rows, (k + 1) * own_rows)

    here = pl.ds(pl.multiple_of(mod * half, half), half)
    there = pl.ds(pl.multiple_of((1 - mod) * half, half), half)
    sibling = (1 - mod, seq, mp)
    used = [0]
    sends = []
    is_end = (seq == 0) | (seq == n_seq - 1)
    not_end = (seq > 0) & (seq < n_seq - 1)
    is_inner = (seq == 1) | (seq == n_seq - 2)
    inner = (mod, seq + 1 - 2 * (seq // (n_seq - 1)), mp)

    def when(cond, body):
        if cond is None:
            body()
        else:
            pl.when(cond)(body)

    def peer_of(o):
        if n_mp == 4:
            return (mp + 1 - 2 * (mp % 2), (mp + 2) % 4, 3 - mp)[o - 1]
        return (mp + o) % n_mp

    def source_of(o):
        if n_mp == 4:
            return peer_of(o)
        return (mp + n_mp - o) % n_mp

    def message(src, dst, device, cond=None):
        index = used[0]
        used[0] += 1
        copy = pltpu.make_async_remote_copy(
            src_ref=src,
            dst_ref=dst,
            send_sem=ref.ssem.at[index],
            recv_sem=ref.rsem.at[index],
            device_id=device,
            device_id_type=MESH,
        )
        sends.append((cond, copy))
        return copy

    loads = types.SimpleNamespace()
    pairs = (
        (ref.inp_h.at[0], ref.inp), (ref.pb_h, ref.pb), (ref.tp_h, ref.tp), (ref.pv_h, ref.pv),
        (ref.ag_h, ref.ag), (ref.wk_h, ref.wk), (ref.wv_h, ref.wv), (ref.wq_h, ref.wq), (ref.cot_h.at[0], ref.cot),
        (ref.wo_h, ref.wo), (ref.wd_h, ref.wd), (ref.fg_h, ref.fg), (ref.wg_h, ref.wg), (ref.wu_h, ref.wu),
    )
    copies = [pltpu.make_async_copy(src, dst, ref.lsem.at[i]) for i, (src, dst) in enumerate(pairs)]
    for copy in copies:
        copy.start()
    (loads.inp, loads.pb, loads.tp, loads.pv, loads.ag, loads.wk, loads.wv, loads.wq, loads.cot, loads.wo,
     loads.wd, loads.fg, loads.wg, loads.wu) = copies

    barrier = pltpu.get_barrier_semaphore()
    pl.semaphore_signal(barrier, 1, device_id=sibling, device_id_type=MESH)
    for o in range(1, n_mp):
        pl.semaphore_signal(barrier, 1, device_id=(mod, seq, peer_of(o)), device_id_type=MESH)

    for o in range(1, n_seq):
        pl.semaphore_signal(barrier, 1, device_id=(mod, (seq + o) % n_seq, mp), device_id_type=MESH)
    pl.semaphore_wait(barrier, n_mp + n_seq - 1)

    to_text = message(ref.inp_h.at[0], ref.inc, sibling, mod == 0)

    @pl.when(mod == 0)
    def _():
        to_text.start()

    cot_end = message(ref.cot_h.at[0], ref.cot_e, inner, is_end)
    when(is_end, cot_end.start)

    first = ref.len_s[0, 0]
    long_first = first == LONG
    loads.pb.wait()
    mirror = (
        lax.broadcasted_iota(jnp.int32, (128, 128), 0) + lax.broadcasted_iota(jnp.int32, (128, 128), 1) == 127
    ).astype(f32)
    places = lax.broadcasted_iota(jnp.int32, (8, 128), 0) * 128 + lax.broadcasted_iota(jnp.int32, (8, 128), 1)
    span = ref.ids_s.shape[0]
    stride = 9 if span % 9 == 0 else 1

    def set_ids(i, ids):
        for k in range(stride):
            ids = jnp.where(places == i * stride + k, ref.ids_s[i * stride + k], ids)
        return ids

    ids = lax.fori_loop(0, span // stride, set_ids, jnp.zeros((8, 128), jnp.int32))
    turned_ids = nn(ids.astype(f32).astype(bf16), mirror.astype(bf16))
    lines = SPANS // 128
    turned_ids = jnp.concatenate([turned_ids[i : i + 1, :] for i in reversed(range(lines))], axis=1)
    hot = bucket_hot(turned_ids.astype(jnp.int32))
    ref.hot[...] = hot
    rel = jnp.dot(ref.pb[...], hot, precision=lax.Precision.HIGHEST, preferred_element_type=f32)
    rel = jnp.concatenate([rel, jnp.zeros((heads, WIDE - SPANS), f32)], axis=1)
    blocks = rows // 64
    apart = ((-128, -128), (-128, -192), (-128, -192), (-64, -192))
    along = ((128, 128), (128, 128), (64, 192), (64, 192))

    def window(c):
        return pltpu.roll(rel, (WIDE - (c + 256)) % WIDE, 1)[:, :384]

    lane_row = lax.broadcasted_iota(jnp.int32, (1, rows), 1)
    patch_doc = lane_row // PDOC
    text_doc = (lane_row >= first).astype(jnp.int32)
    query_doc = jnp.where(mod == 0, patch_doc, text_doc)
    for kb in range(blocks):
        ref.win[kb] = window(-64 * kb)
        a0, a1 = (window(c - 64 * kb) for c in apart[kb])
        b0, b1 = (window(c - 64 * kb) for c in along[kb])
        ref.win[blocks + kb] = jnp.where(
            mod == 0, jnp.where(long_first, a0, a1), jnp.where(long_first, b0, b1)
        )
    for kb in range(2 * blocks):
        at = kb % blocks
        in_patch = (mod == 0) if kb < blocks else (mod == 1)
        key_doc = jnp.where(in_patch, at * 64 // PDOC, jnp.where(at * 64 >= first, 1, 0))
        same = query_doc == key_doc

        def one_bias(h, carry, kb=kb, same=same):
            line = jnp.broadcast_to(ref.win[kb, pl.ds(h, 1), :], (64, 384))
            table = pltpu.roll(line, 320, 1, stride=1, stride_axis=0)[:, :rows]
            ref.prob[h, kb * 64 : kb * 64 + 64, :] = jnp.where(same, table, -1000000000.0)
            return carry

        lax.fori_loop(0, heads, one_bias, 0)

    loads.cot.wait()

    def transposed(source, sides, cond=None):
        copy = message(sides.s, sides.r, sibling, cond)

        def body():
            sides.s[...] = source[:, there].T
            copy.start()
            sides.t[...] = source[:, here].T

        when(cond, body)
        return copy

    x_tan, x_na, x_nf, x_branch, x_tan_e, x_nf_e = (
        types.SimpleNamespace(t=ref.xt.at[i], s=ref.xs.at[i], r=ref.xr.at[i]) for i in range(6)
    )
    tan_sent = transposed(ref.cot, x_tan, not_end)

    loads.tp.wait()
    loads.pv.wait()
    loads.inp.wait()

    @pl.when(mod == 1)
    def _():
        count = patch_counts(ref.tp[...], ref.pv[...], rows).T.astype(bf16)
        to_text.wait_recv()
        ref.united[...] = nn(count, ref.inc[...])

    @pl.when(mod == 0)
    def _():
        ref.united[...] = jnp.zeros((rows, dim), f32)

    loads.ag.wait()
    attn_gain = flat(ref.ag)

    def first_norm(at):
        u = ref.united[at, :] + ref.inp[at, :].astype(f32)
        ref.united[at, :] = u
        ref.na[at, :] = (u * rms_scale(u) * attn_gain).astype(bf16)

    row_chunks(0, rows, 32, first_norm)
    loads.wk.wait()
    ref.kv[:, :width] = nn(ref.na[...], ref.wk[...]).astype(bf16)
    loads.wv.wait()
    ref.kv[:, width:] = nn(ref.na[...], ref.wv[...]).astype(bf16)
    kv_sent = message(ref.kv, ref.kvr, sibling)
    kv_sent.start()
    loads.wq.wait()
    ref.q[...] = nn(ref.na[...], ref.wq[...]).astype(bf16)
    ref.kvt[:, :rows] = ref.kv[...].T
    na_sent = transposed(ref.na, x_na)
    kv_sent.wait_recv()
    ref.kvt[:, rows:] = ref.kvr[...].T
    head_of = lax.broadcasted_iota(jnp.int32, (1, width), 1) // HEAD

    def head_mask(h):
        return (head_of == h).astype(f32).astype(bf16)

    def head_rows(h, base=0):
        return pl.ds(pl.multiple_of(base + h * HEAD, HEAD), HEAD)

    def head_fwd(k, h, carry):
        at = part(k)
        qm = ref.q[at, :] * head_mask(h)
        ref.qm[h, at, :] = qm
        s0 = nt(ref.kv[:, :width], qm) * 0.125 + ref.prob[h, :rows, at]
        s1 = nt(ref.kvr[:, :width], qm) * 0.125 + ref.prob[h, rows:, at]
        top = jnp.maximum(jnp.max(s0, axis=0, keepdims=True), jnp.max(s1, axis=0, keepdims=True))
        e0 = jnp.exp(s0 - top)
        e1 = jnp.exp(s1 - top)
        total = jnp.sum(e0, axis=0, keepdims=True) + jnp.sum(e1, axis=0, keepdims=True)
        scale = 1.0 / total
        p0 = e0 * scale
        p1 = e1 * scale
        ref.prob[h, :rows, at] = p0
        ref.prob[h, rows:, at] = p1
        values_t = ref.kvt[head_rows(h, width), :]
        ref.att_t[head_rows(h), at] = nn(values_t[:, :rows], p0.astype(bf16)) + nn(
            values_t[:, rows:], p1.astype(bf16)
        )
        return carry

    def scatter(c, k, product, hold=False):
        ref.part[part(k), :] = product
        ref.stage[c, part(k), :] = product.astype(bf16)
        copies = []
        for o in range(n_mp - 1, 0, -1):
            to = peer_of(o)
            copies.append(message(ref.stage.at[c, share(k, to)], ref.land.at[c, k, o - 1], (mod, seq, to)))
            if not hold:
                copies[-1].start()
        ref.keep[c, kept(k), :] = ref.part[share(k, mp), :]
        return copies

    def summed(c, k, copies):
        for copy in copies:
            copy.wait_recv()
        total = ref.keep[c, kept(k), :]
        for o in range(1, n_mp):
            total += ref.land[c, k, o - 1].astype(f32)
        return total

    def gather(c, k):
        at = ref.whole.at[c, share(k, mp)]
        copies = [message(at, at, (mod, seq, peer_of(o))) for o in range(1, n_mp)]
        for copy in reversed(copies):
            copy.start()
        return copies

    loads.wo.wait()
    attn_sum = []
    for k in parts:
        lax.fori_loop(0, heads, functools.partial(head_fwd, k), 0)
        ref.att[part(k), :] = ref.att_t[:, part(k)].T.astype(bf16)
        attn_sum.append(scatter(0, k, nn(ref.att[part(k), :], ref.wo[...])))
    att_sent = message(ref.att, ref.att_r, sibling)
    att_sent.start()
    loads.wd.wait()
    ref.hg[...] = nt(ref.cot[...], ref.wd[...])
    loads.fg.wait()
    ffn_gain = flat(ref.fg)
    nf_end = []

    def to_inner(k, who):
        at = share(k, who)
        copy = message(ref.whole.at[0, at], ref.nf_e.at[at], inner, is_end)
        when(is_end, copy.start)
        nf_end.append(copy)

    nf_parts = []
    for k in parts:
        middle = ref.united[share(k, mp), :] + summed(0, k, attn_sum[k])
        ref.mid[kept(k), :] = middle
        ref.whole[0, share(k, mp), :] = (middle * rms_scale(middle) * ffn_gain).astype(bf16)
        nf_parts.append(gather(0, k))
        to_inner(k, mp)
    tan_e_sent = message(x_tan_e.s, x_tan_e.r, sibling, is_inner)

    @pl.when(is_inner)
    def _():
        cot_end.wait_recv()
        x_tan_e.s[...] = ref.cot_e[:, there].T
        tan_e_sent.start()
        x_tan_e.t[...] = ref.cot_e[:, here].T
        ref.hg_e[...] = nt(ref.cot_e[...], ref.wd[...])

    loads.wg.wait()
    loads.wu.wait()

    def gelu_rows(at, back_ref=ref.hg, hid=ref.hid, gg=ref.gg, ug=ref.ug):
        g, u, back = ref.gate[at, :], ref.up[at, :], back_ref[at, :]
        squared = g * g
        t = jnp.tanh(ROOT * (g + 0.044715 * squared * g))
        left = 0.5 * (1.0 + t)
        gelu = left * g
        slope = left + 0.5 * g * (1.0 - t * t) * (ROOT * (1.0 + 0.134145 * squared))
        hid[at, :] = (gelu * u).astype(bf16)
        gg[at, :] = (back * u * slope).astype(bf16)
        ug[at, :] = (back * gelu).astype(bf16)

    ffn_in = []
    for k in parts:
        for o, copy in enumerate(nf_parts[k], 1):
            copy.wait_recv()
            to_inner(k, source_of(o))
        at = part(k)
        ref.gate[at, :] = nt(ref.whole[0, at, :], ref.wg[...])
        ref.up[at, :] = nt(ref.whole[0, at, :], ref.wu[...])
        row_chunks(k * part_rows, part_rows, 16, gelu_rows)
        ffn_in.append(scatter(1, k, nn(ref.gg[at, :], ref.wg[...]) + nn(ref.ug[at, :], ref.wu[...])))
    hid_sent = message(ref.hid, ref.hid_r, sibling, not_end)
    gg_sent = message(ref.gg, ref.gg_r, sibling, not_end)
    ug_sent = message(ref.ug, ref.ug_r, sibling, not_end)
    when(not_end, hid_sent.start)
    nf_sent = transposed(ref.whole.at[0], x_nf, not_end)
    when(not_end, gg_sent.start)
    when(not_end, ug_sent.start)

    after = (mod, jnp.minimum(seq + 1, n_seq - 1), mp)
    before = (mod, jnp.maximum(seq - 1, 0), mp)
    weights = []
    ends = (1, 1, 1, 0, 0, 0, 0)
    for e, g, s, a, b, o in zip(ends, ref.wgrad, ref.wsend, ref.wleft, ref.wright, ref.wout, strict=True):
        right, left = {}, {}
        for j in range(n_seq):
            rng = pl.ds(j * block, block)
            if j > e:
                right[j] = message(s.at[rng], a.at[rng], after, (seq >= e) & (seq < j))
            if j < n_seq - 1 - e:
                left[j] = message(s.at[rng], b.at[rng], before, (seq < n_seq - e) & (seq > j))
        weights.append(types.SimpleNamespace(e=e, g=g, s=s, a=a, b=b, o=o, right=right, left=left))
    w_down, w_gate, w_up, w_proj, w_q, w_k, w_v = weights

    def product(w, x, pieces, more=False):
        lo = 0
        for own, other in pieces:
            size = own.shape[1]
            both = nn(x.t[...], own[...]) + nn(x.r[...], other[...])
            if more:
                both += w.g[:, lo : lo + size]
            w.g[:, lo : lo + size] = both
            lo += size

    def hop(group, step, some=slice(None)):
        edge = group[0].e + step
        if edge >= n_seq - 1:
            return

        @pl.when(seq == edge)
        def _():
            for j in list(range(n_seq - 1, edge, -1))[some]:
                rng = slice(j * block, (j + 1) * block)
                for w in group:
                    value = w.g[rng, :]
                    if step > 0:
                        w.right[j].wait_recv()
                        value += w.a[rng, :].astype(f32)
                    w.s[rng, :] = value.astype(bf16)
                    w.right[j].start()

        @pl.when(seq == n_seq - 1 - edge)
        def _():
            for j in list(range(n_seq - 1 - edge))[some]:
                rng = slice(j * block, (j + 1) * block)
                for w in group:
                    value = w.g[rng, :]
                    if step > 0:
                        w.left[j].wait_recv()
                        value += w.b[rng, :].astype(f32)
                    w.s[rng, :] = value.astype(bf16)
                    w.left[j].start()

    def arrive(w):
        for j in range(n_seq):

            @pl.when(seq == j)
            def _(j=j):
                rng = slice(j * block, (j + 1) * block)
                value = w.g[rng, :] if w.e <= j < n_seq - w.e else jnp.zeros(w.o.shape, f32)
                if j > w.e:
                    w.right[j].wait_recv()
                    value += w.a[rng, :].astype(f32)
                if j < n_seq - 1 - w.e:
                    w.left[j].wait_recv()
                    value += w.b[rng, :].astype(f32)
                w.o[...] = value

    gain_sums = []
    branch_parts = []

    def middle_back(k):
        normed_grad = summed(1, k, ffn_in[k])
        middle = ref.mid[kept(k), :]
        scale = rms_scale(middle)
        spread = normed_grad * ffn_gain
        gain_sums.append(jnp.sum(normed_grad * middle * scale, axis=0, keepdims=True))
        middle_grad = (
            ref.cot[share(k, mp), :].astype(f32)
            + scale * spread
            - middle * (scale * scale * scale) * jnp.mean(spread * middle, axis=-1, keepdims=True)
        )
        ref.mgrad[kept(k), :] = middle_grad
        ref.whole[1, share(k, mp), :] = middle_grad.astype(bf16)
        branch_parts.append(gather(1, k))

    hid_e_sent = message(ref.hid_e, ref.hid_er, sibling, is_inner)
    gg_e_sent = message(ref.gg_e, ref.gg_er, sibling, is_inner)
    ug_e_sent = message(ref.ug_e, ref.ug_er, sibling, is_inner)
    nf_e_sent = message(x_nf_e.s, x_nf_e.r, sibling, is_inner)

    @pl.when(not_end)
    def _():
        hid_sent.wait_recv()
        tan_sent.wait_recv()
        product(w_down, x_tan, [(ref.hid, ref.hid_r)])
        nf_sent.wait_recv()
        gg_sent.wait_recv()
        product(w_gate, x_nf, [(ref.gg, ref.gg_r)])
        ug_sent.wait_recv()
        product(w_up, x_nf, [(ref.ug, ref.ug_r)])

    middle_back(0)
    @pl.when(is_inner)
    def _():
        for copy in nf_end:
            copy.wait_recv()
        ref.gate[...] = nt(ref.nf_e[...], ref.wg[...])
        ref.up[...] = nt(ref.nf_e[...], ref.wu[...])
        row_chunks(0, rows, 16, lambda at: gelu_rows(at, ref.hg_e, ref.hid_e, ref.gg_e, ref.ug_e))
        hid_e_sent.start()
        x_nf_e.s[...] = ref.nf_e[:, there].T
        nf_e_sent.start()
        gg_e_sent.start()
        ug_e_sent.start()
        x_nf_e.t[...] = ref.nf_e[:, here].T


    for k in parts[1:]:
        middle_back(k)

    def end_products(w, x, pieces, needs):
        @pl.when(is_inner)
        def _():
            for copy in needs:
                copy.wait_recv()
            product(w, x, pieces, more=True)

        hop([w], 0, slice(0, 1))

    end_products(w_down, x_tan_e, [(ref.hid_e, ref.hid_er)], (hid_e_sent, tan_e_sent))
    end_products(w_gate, x_nf_e, [(ref.gg_e, ref.gg_er)], (gg_e_sent, nf_e_sent))
    end_products(w_up, x_nf_e, [(ref.ug_e, ref.ug_er)], (ug_e_sent,))
    hop([w_down, w_gate, w_up], 0, slice(1, None))
    ffn_out = [scatter(2, k, nn(ref.hid[part(k), :], ref.wd[...]), hold=True) for k in parts]

    flip = (
        lax.broadcasted_iota(jnp.int32, (rows, rows), 0) // 64 == lax.broadcasted_iota(jnp.int32, (rows, rows), 1) // 64
    ) & (
        lax.broadcasted_iota(jnp.int32, (rows, rows), 0) % 64
        + lax.broadcasted_iota(jnp.int32, (rows, rows), 1) % 64
        == 63
    )
    ref.turn[...] = flip.astype(f32).astype(bf16)
    ref.dk[...] = jnp.zeros((2 * rows, width), f32)
    ref.dv[...] = jnp.zeros((2 * rows, width), f32)

    def head_bwd(k, h, carry):
        a = part(k)
        gm = ref.ga[a, :] * head_mask(h)
        p0, p1 = ref.prob[h, :rows, a], ref.prob[h, rows:, a]
        d0 = nt(ref.kv[:, width:], gm)
        d1 = nt(ref.kvr[:, width:], gm)
        inner_sum = jnp.sum(p0 * d0, axis=0, keepdims=True) + jnp.sum(p1 * d1, axis=0, keepdims=True)
        g0 = (p0 * (d0 - inner_sum)).astype(bf16)
        g1 = (p1 * (d1 - inner_sum)).astype(bf16)
        keys_t = ref.kvt[head_rows(h), :]
        ref.dq_t[head_rows(h), a] = nn(keys_t[:, :rows], g0) + nn(keys_t[:, rows:], g1)
        qm = ref.qm[h, a, :]
        ref.dk[:rows, :] += nn(g0, qm)
        ref.dk[rows:, :] += nn(g1, qm)
        ref.dv[:rows, :] += nn(p0.astype(bf16), gm)
        ref.dv[rows:, :] += nn(p1.astype(bf16), gm)
        turn = ref.turn[...]
        low, wide = k * part_rows, part_rows + 128
        for side, g in ((0, g0), (1, g1)):
            turned = nn(turn, g)
            for at in range(blocks):
                piece = turned[at * 64 : at * 64 + 64, :]
                piece = jnp.concatenate([piece, jnp.zeros((64, 128), f32)], axis=1)
                piece = pltpu.roll(piece, 1, 1, stride=1, stride_axis=0)
                ref.diag[side * blocks + at, pl.ds(h, 1), low : low + wide] += jnp.sum(piece, axis=0, keepdims=True)
        return carry

    ref.diag[...] = jnp.zeros(ref.diag.shape, f32)
    for k in parts:
        for copy in branch_parts[k]:
            copy.wait_recv()
        ref.ga[part(k), :] = nt(ref.whole[1, part(k), :], ref.wo[...]).astype(bf16)
        if k == PARTS - 1:
            for copies in ffn_out:
                for copy in copies:
                    copy.start()
        lax.fori_loop(0, heads, functools.partial(head_bwd, k), 0)
    ref.kvg_s[:, :width] = (ref.dk[rows:, :] * 0.125).astype(bf16)
    ref.kvg_s[:, width:] = ref.dv[rows:, :].astype(bf16)
    kvg_sent = message(ref.kvg_s, ref.kvg_r, sibling)
    kvg_sent.start()
    branch_sent = transposed(ref.whole.at[1], x_branch)
    ref.dqb[...] = (ref.dq_t[...].T * 0.125).astype(bf16)
    dq_sent = message(ref.dqb, ref.dq_r, sibling)
    dq_sent.start()
    att_sent.wait_recv()
    branch_sent.wait_recv()
    product(w_proj, x_branch, [(ref.att, ref.att_r)])
    hop([w_proj], 0)
    hop([w_down, w_gate], 1)
    na_sent.wait_recv()
    dq_sent.wait_recv()
    product(w_q, x_na, [(ref.dqb, ref.dq_r)])
    hop([w_q], 0)
    kvg_sent.wait_recv()
    ref.dkb[...] = (ref.dk[:rows, :] * 0.125 + ref.kvg_r[:, :width].astype(f32)).astype(bf16)
    ref.dvb[...] = (ref.dv[:rows, :] + ref.kvg_r[:, width:].astype(f32)).astype(bf16)
    dk_sent = message(ref.dkb, ref.dk_r, sibling)
    dv_sent = message(ref.dvb, ref.dv_r, sibling)
    for copy in (dk_sent, dv_sent):
        copy.start()
    attn_in = []
    for k in parts:
        at = part(k)
        rows_in = nt(ref.dqb[at, :], ref.wq[...]) + nt(ref.dkb[at, :], ref.wk[...]) + nt(ref.dvb[at, :], ref.wv[...])
        attn_in.append(scatter(3, k, rows_in))
    for copy in (dk_sent, dv_sent):
        copy.wait_recv()
    product(w_k, x_na, [(ref.dkb, ref.dk_r)])
    product(w_v, x_na, [(ref.dvb, ref.dv_r)])
    hop([w_k, w_v], 0)
    hop([w_up], 1)

    def gain_rows(i, total):
        at = pl.ds(pl.multiple_of(i * 32, 32), 32)
        u = ref.united[at, :]
        return total + jnp.sum(ref.part[at, :] * u * rms_scale(u), axis=0, keepdims=True)

    attn_gain_grad = lax.fori_loop(0, rows // 32, gain_rows, jnp.zeros((1, dim), f32))

    def unwindow(piece, c):
        grown = jnp.concatenate([piece, jnp.zeros((heads, WIDE - 384), f32)], axis=1)
        return pltpu.roll(grown, (c + 256) % WIDE, 1)

    total = jnp.zeros((heads, WIDE), f32)
    for kb in range(blocks):
        total += unwindow(ref.diag[kb], -64 * kb)
        piece = ref.diag[blocks + kb]
        a0, a1 = (unwindow(piece, c - 64 * kb) for c in apart[kb])
        b0, b1 = (unwindow(piece, c - 64 * kb) for c in along[kb])
        total += jnp.where(mod == 0, jnp.where(long_first, a0, a1), jnp.where(long_first, b0, b1))
    bias_grad = lax.dot_general(
        total[:, :SPANS], ref.hot[...], (((1,), (1,)), ((), ())), precision=lax.Precision.HIGHEST, preferred_element_type=f32
    )
    quarter = dim // 4
    for i, line in enumerate((attn_gain_grad, sum(gain_sums))):
        for k in range(4):
            ref.small[4 * i + k : 4 * i + k + 1, :quarter] = line[:, k * quarter : (k + 1) * quarter]
    ref.small[:, quarter:] = jnp.zeros((8, 128), f32)
    ref.small[:heads, quarter : quarter + NB] = bias_grad
    small_mp = [message(ref.small, ref.small_p.at[o - 1], (mod, seq, peer_of(o))) for o in range(1, n_mp)]
    for copy in small_mp:
        copy.start()

    hop([w_proj, w_q], 1)
    for copy in small_mp:
        copy.wait_recv()
    gains = ref.small[:, :quarter]
    for o in range(1, n_mp):
        gains += ref.small_p[o - 1, :, :quarter]
    ref.small2[:, :quarter] = gains
    ref.small2[:, quarter:] = ref.small[:, quarter:]
    small_mod = message(ref.small2, ref.small_m, sibling)
    small_mod.start()

    united_parts = []
    for k in parts:
        normed_grad = summed(3, k, attn_in[k])
        u = ref.united[share(k, mp), :]
        scale = rms_scale(u)
        spread = normed_grad * attn_gain
        united_grad = (
            ref.mgrad[kept(k), :]
            + scale * spread
            - u * (scale * scale * scale) * jnp.mean(spread * u, axis=-1, keepdims=True)
        )
        ref.whole[3, share(k, mp), :] = united_grad.astype(bf16)
        united_parts.append(gather(3, k))
    output_parts = []
    for k in parts:
        ref.whole[2, share(k, mp), :] = (ref.mid[kept(k), :] + summed(2, k, ffn_out[k])).astype(bf16)
        output_parts.append(gather(2, k))
    hop([w_k, w_v], 1)
    small_mod.wait_recv()
    ref.small3[...] = ref.small2[...] + ref.small_m[...]
    small_seq = [
        message(ref.small3, ref.small_q.at[o - 1], (mod, (seq + o) % n_seq, mp)) for o in range(1, n_seq)
    ]
    for copy in small_seq:
        copy.start()
    backs = []
    for k in parts:
        for o in range(n_mp):
            at = share(k, source_of(o) if o else mp)
            if o:
                united_parts[k][o - 1].wait_recv()
            back = message(ref.whole.at[3, at], ref.text_o.at[at], sibling, mod == 1)
            when(mod == 1, back.start)
            backs.append(back)
    for step in range(2, n_seq - 1):
        hop([w_down, w_gate, w_up], step)
        hop([w_proj, w_q], step)
        hop([w_k, w_v], step)
    for copies in output_parts:
        for copy in copies:
            copy.wait_recv()
    ref.out_o[...] = ref.whole[2]
    ref.own_o[...] = ref.whole[3]
    for w in weights:
        arrive(w)

    total = ref.small3[...]
    for i, copy in enumerate(small_seq):
        copy.wait_recv()
        total += ref.small_q[i]
    ref.small_o[...] = total

    @pl.when(mod == 0)
    def _():
        for back in backs:
            back.wait_recv()

    @pl.when(mod == 1)
    def _():
        ref.text_o[...] = jnp.zeros((rows, dim), bf16)

    for cond, copy in sends:
        if cond is None:
            copy.wait_send()
        else:

            @pl.when(cond)
            def _(copy=copy):
                copy.wait_send()

    assert used[0] <= ref.ssem.shape[0]


def finish(n_seq, heads, width, ids, valid, own, text, out, gd, gg, gu, go, gq, gk, gv, small,
           o_out, o_in, o_ag, o_q, o_k, o_v, o_o, o_pb, o_fg, o_gate, o_up, o_down, hold):
    mod, seq = lax.axis_index("mod"), lax.axis_index("seq")
    rows, dim = own.shape
    place = mod * n_seq + seq
    o_out[0] = out[...]

    @pl.when(mod == 0)
    def _():
        count = patch_counts(ids[...], valid[...], rows)
        o_in[0] = own[...].astype(f32) + nn(count.astype(bf16), text[...])

    @pl.when(mod == 1)
    def _():
        o_in[0] = own[...].astype(f32)

    o_q[...] = gq[...]
    o_k[...] = gk[...]
    o_v[...] = gv[...]
    o_o[...] = go[...].T
    o_gate[...] = gg[...].T
    o_up[...] = gu[...].T
    o_down[...] = gd[...].T
    quarter = dim // 4
    part = dim // (2 * n_seq)
    for i, o_gain in enumerate((o_ag, o_fg)):
        line = jnp.concatenate([small[4 * i + k : 4 * i + k + 1, :quarter] for k in range(4)], axis=1)
        line = pltpu.roll(jnp.broadcast_to(line, (8, dim)), dim - place * part, 1)
        o_gain[...] = line[:1, :part]
    few = NB // (2 * n_seq)
    hold[...] = small[:, quarter:].T
    o_pb[...] = hold[pl.ds(place * few, few), :heads]


def per_device(n_seq, n_mp, *args):
    (inputs, text_patches, patch_valid, text_lengths, bucket_table, attn_gain, query_weight, key_weight,
     value_weight, output_weight, position_bias, ffn_gain, gate_weight, up_weight, down_weight, cotangent) = args
    rows, dim = inputs.shape[1:]
    heads = position_bias.shape[1]
    width = heads * HEAD
    ff = down_weight.shape[0]
    own_rows = rows // n_mp
    half = dim // 2
    block = half // n_seq
    text_patches, patch_valid, position_bias = text_patches.T, patch_valid.T, position_bias.T
    gate_weight, up_weight = gate_weight.T, up_weight.T
    given = dict(
        len_s=text_lengths, ids_s=bucket_table, inp_h=inputs, tp_h=text_patches, pv_h=patch_valid, pb_h=position_bias,
        ag_h=attn_gain.reshape(dim // 128, 128), fg_h=ffn_gain.reshape(dim // 128, 128), wq_h=query_weight, wk_h=key_weight,
        wv_h=value_weight, wo_h=output_weight, wg_h=gate_weight, wu_h=up_weight, wd_h=down_weight, cot_h=cotangent,
    )
    sizes = sizes_of(heads, ff)
    results = dict(
        wout=[((block, size), f32) for size in sizes], out_o=((rows, dim), bf16), own_o=((rows, dim), bf16),
        text_o=((rows, dim), bf16), small_o=((8, dim // 4 + 128), f32),
    )
    small = ((8, dim // 4 + 128), f32)
    sent = [((half, size), bf16) for size in sizes]
    held = dict(
        inp=((rows, dim), bf16), hot=((NB, SPANS), f32), pb=((heads, NB), f32), tp=(text_patches.shape, jnp.int32),
        pv=(patch_valid.shape, jnp.int32), ag=((dim // 128, 128), bf16), fg=((dim // 128, 128), bf16), wq=((dim, width), bf16),
        wk=((dim, width), bf16), wv=((dim, width), bf16), wo=((width, dim), bf16), wg=((ff, dim), bf16),
        wu=((ff, dim), bf16), wd=((ff, dim), bf16), cot=((rows, dim), bf16), inc=((rows, dim), bf16),
        win=((2 * rows // 64, heads, 384), f32), diag=((2 * rows // 64, heads, 384), f32),
        prob=((heads, 2 * rows, rows), f32), xt=((6, half, rows), bf16), xs=((6, half, rows), bf16), xr=((6, half, rows), bf16),
        united=((rows, dim), f32), na=((rows, dim), bf16),
        kv=((rows, 2 * width), bf16), kvr=((rows, 2 * width), bf16), kvt=((2 * width, 2 * rows), bf16),
        q=((rows, width), bf16), qm=((heads, rows, width), bf16), att_t=((width, rows), f32), att=((rows, width), bf16),
        att_r=((rows, width), bf16), part=((rows, dim), f32), stage=((4, rows, dim), bf16),
        land=((4, PARTS, n_mp - 1, own_rows // PARTS, dim), bf16), keep=((4, own_rows, dim), f32), whole=((4, rows, dim), bf16),
        cot_e=((rows, dim), bf16), nf_e=((rows, dim), bf16), hg_e=((rows, ff), f32), hid_e=((rows, ff), bf16),
        hid_er=((rows, ff), bf16), gg_e=((rows, ff), bf16), gg_er=((rows, ff), bf16), ug_e=((rows, ff), bf16),
        ug_er=((rows, ff), bf16), hg=((rows, ff), f32), mid=((own_rows, dim), f32), mgrad=((own_rows, dim), f32), gate=((rows, ff), f32),
        up=((rows, ff), f32), ga=((rows, width), bf16), turn=((rows, rows), bf16), dk=((2 * rows, width), f32),
        dv=((2 * rows, width), f32), dq_t=((width, rows), f32), kvg_s=((rows, 2 * width), bf16),
        kvg_r=((rows, 2 * width), bf16),
    )
    held.update(
        hid=((rows, ff), bf16), hid_r=((rows, ff), bf16), gg=((rows, ff), bf16), gg_r=((rows, ff), bf16),
        ug=((rows, ff), bf16), ug_r=((rows, ff), bf16), dqb=((rows, width), bf16), dq_r=((rows, width), bf16),
        dkb=((rows, width), bf16), dk_r=((rows, width), bf16), dvb=((rows, width), bf16), dv_r=((rows, width), bf16),
        wgrad=[((half, size), f32) for size in sizes], wsend=sent, wleft=sent, wright=sent, small=small, small2=small,
        small3=small, small_m=small, small_q=((n_seq - 1,) + small[0], f32),
        small_p=((n_mp - 1,) + small[0], f32),
    )
    count = 60 + 20 * n_mp + 14 * n_seq
    order = [(name, 0) for name in given]
    out_shape, scratch = [], []
    for specs, into, make in ((results, out_shape, pltpu.VMEM), (held, scratch, pltpu.VMEM)):
        for name, spec in specs.items():
            many = spec if isinstance(spec, list) else [spec]
            order.append((name, len(many) if isinstance(spec, list) else 0))
            into.extend(make(*one) for one in many)
    for i, size in enumerate((count, count, len(given) - 2)):
        order.append((("ssem", "rsem", "lsem")[i], 0))
        scratch.append(pltpu.SemaphoreType.DMA((size,)))
    vmem = pl.BlockSpec(memory_space=pltpu.VMEM)
    done = pl.pallas_call(
        functools.partial(mega, n_seq, n_mp, heads, order),
        out_shape=out_shape,
        in_specs=[pl.BlockSpec(memory_space=pltpu.SMEM)] * 2 + [pl.BlockSpec(memory_space=pl.ANY)] * (len(given) - 2),
        scratch_shapes=scratch,
        compiler_params=pltpu.CompilerParams(
            collective_id=0, has_side_effects=True, vmem_limit_bytes=58 * 2**20
        ),
        name="layer",
    )(*given.values())
    done = [pltpu.with_memory_space_constraint(one, pltpu.VMEM) for one in done]
    *wout, out, own, text, small_sum = done
    part = dim // (2 * n_seq)
    few = NB // (2 * n_seq)
    shapes = [
        ((1, rows, dim), bf16), ((1, rows, dim), f32), ((1, part), f32), ((block, width), f32), ((block, width), f32),
        ((block, width), f32), ((width, block), f32), ((few, heads), f32), ((1, part), f32), ((ff, block), f32),
        ((ff, block), f32), ((ff, block), f32),
    ]
    outs = pl.pallas_call(
        functools.partial(finish, n_seq, heads, width),
        out_shape=[jax.ShapeDtypeStruct(*spec) for spec in shapes],
        in_specs=[vmem] * 13,
        out_specs=[vmem] * 12,
        scratch_shapes=[pltpu.VMEM((128, 8), f32)],
        compiler_params=pltpu.CompilerParams(vmem_limit_bytes=16 * 2**20),
        name="finish",
    )(
        text_patches, patch_valid, own, text, out, *wout, small_sum
    )
    outs = list(outs)
    for i in (9, 10):
        outs[i] = outs[i].T
    outs[2] = outs[2].reshape(part)
    outs[8] = outs[8].reshape(part)
    return tuple(outs)


def solution(mesh):
    group = ("mod", "seq")
    in_specs = (
        P("mod", "seq", None), P("seq", None), P("seq", None), P("seq", None), P(), P(), P(None, "mp"), P(None, "mp"),
        P(None, "mp"), P("mp", None), P(None, "mp"), P(), P(None, "mp"), P(None, "mp"), P("mp", None),
        P("mod", "seq", None),
    )
    out_specs = (
        P("mod", "seq", None), P("mod", "seq", None), P(group), P(group, "mp"), P(group, "mp"), P(group, "mp"),
        P("mp", group), P(group, "mp"), P(group), P(group, "mp"), P(group, "mp"), P("mp", group),
    )
    body = functools.partial(per_device, mesh.shape["seq"], mesh.shape["mp"])
    return jax.shard_map(body, mesh=mesh, in_specs=in_specs, out_specs=out_specs, check_vma=False)
```
